32 devices in a mesh: resp: 8 (over z, x), head: 4 (over y, core).
Axes of the slice: x: 2, y: 2, z: 4, core: 2. Of those that a mesh axis runs over, the one named last changes fastest.
Arguments:
- queries: bfloat16 [2048, 8192], P('resp', 'head'), may hold values from -240 to 240
- d_out: bfloat16 [2048, 8192], P('resp', 'head'), may hold values from -24 to 24
- prefix_keys: bfloat16 [128, 1024], P('resp', 'head'), may hold values from -17 to 17
- prefix_values: bfloat16 [128, 1024], P('resp', 'head'), may hold values from -6 to 6
- k_weight: bfloat16 [8192, 1024], P(None, 'head'), may hold values from -0.0625 to 0.0625
- v_weight: bfloat16 [8192, 1024], P(None, 'head'), may hold values from -0.0625 to 0.0625
- lengths: int32 [8], P('resp'), may hold values from 1 to 256, as said below
Outputs:
- prefix_dk: bfloat16 [128, 1024], P('resp', 'head')
- prefix_dv: bfloat16 [128, 1024], P('resp', 'head')
- input_grad: bfloat16 [128, 8192], P('resp', 'head')
The draws below stay inside these ranges and needn't reach their ends.
Inputs may be any that keep to these rules, and one draw needn't show every extreme that they name: `lengths`: every response has at least one live token and one response has exactly 256.
All inputs are finite; a program needn't handle non-finite values.
Results may differ from the reference program's by a relative error of at most 0.015.
Values may be sent and summed in bfloat16 or wider, within the bound.
No kernel may reach another device: no remote copies, remote signals or barrier semaphores. Data moves between devices by JAX's collectives and lax.ppermute only.
A program may use at most 128 MiB of HBM per device.

```python
import jax
import jax.numpy as jnp
from jax import lax

D = 8192
HEADS = 64
KV = 8
HD = 128
LEN = 256
RESPONSES = 8
ROWS = 2048
PREFIX = 128


def shared_keys(key, spread):
    base = jnp.clip(jax.random.normal(jax.random.fold_in(key, 101), (PREFIX, KV * HD), jnp.float32), -6.0, 6.0)
    logs = jax.random.uniform(jax.random.fold_in(key, 102), (PREFIX, 1), jnp.float32, -spread, spread)
    return base * jnp.exp(logs)


def draw_prefix_keys(key, part):
    spread = 0.0
    return shared_keys(key, spread).astype(jnp.bfloat16)


def draw_queries(key, part):
    key = jax.random.fold_in(key, 7)
    entries = jnp.clip(jax.random.normal(key, (ROWS, HEADS * HD), jnp.float32), -6.0, 6.0)
    return entries.astype(jnp.bfloat16)


def draw_lengths(key, part):
    key = jax.random.fold_in(key, 11)
    drawn = jax.random.randint(key, (RESPONSES,), 1, LEN + 1)
    chosen = jax.random.randint(jax.random.fold_in(key, 1), (), 0, RESPONSES)
    return drawn.at[chosen].set(LEN).astype(jnp.int32)


def shard_levels(own_key, shape, shards, least, high):
    loudness = 1.0
    for dim, parts in shards:
        steps = jax.random.uniform(jax.random.fold_in(jax.random.fold_in(own_key, 6), dim), (parts,), jnp.float32, least / len(shards), high / len(shards))
        loudness = loudness * jnp.repeat(jnp.exp(steps), shape[dim] // parts).reshape((-1,) + (1,) * (len(shape) - 1 - dim))
    return loudness


def scatter_about(stream_key, dims, deviation, reach, shards=(), kind=jnp.bfloat16):
    factor_of = shard_levels(stream_key, dims, shards, -0.22, 0.18) if shards else 1.0
    array = jax.random.normal(stream_key, dims, jnp.float32) * deviation * factor_of
    return jnp.minimum(jnp.maximum(array, -reach), reach).astype(kind)


def setup_inputs(seed: int = 0) -> dict:
    streams_of = jax.random.split(jax.random.key(seed), 8)
    return {
        "queries": draw_queries(jax.random.fold_in(streams_of[7], 71), 0),
        "d_out": scatter_about(streams_of[1], (ROWS, HEADS * HD), 4.0, 24.0, ((0, 8), (1, 4))),
        "prefix_keys": draw_prefix_keys(jax.random.fold_in(streams_of[7], 71), 0),
        "prefix_values": scatter_about(streams_of[3], (PREFIX, KV * HD), 1.0, 6.0, ((0, 8), (1, 4))),
        "k_weight": scatter_about(streams_of[4], (D, KV * HD), D ** -0.5, 0.0625, ((1, 4),)),
        "v_weight": scatter_about(streams_of[5], (D, KV * HD), D ** -0.5, 0.0625, ((1, 4),)),
        "lengths": draw_lengths(jax.random.fold_in(streams_of[7], 71), 0),
    }


def reference(queries, d_out, prefix_keys, prefix_values, k_weight, v_weight, lengths):
    group = HEADS // KV
    scale = HD ** -0.5
    keys = prefix_keys.astype(jnp.float32).reshape(PREFIX, KV, HD)
    values = prefix_values.astype(jnp.float32).reshape(PREFIX, KV, HD)
    query_blocks = queries.reshape(RESPONSES, LEN, KV, group, HD)
    grad_blocks = d_out.reshape(RESPONSES, LEN, KV, group, HD)

    def one_response(carry, inputs):
        query, grad, length = inputs
        live = jnp.arange(LEN, dtype=jnp.int32) < length
        grad = jnp.where(live[:, None, None, None], grad, jnp.zeros_like(grad))
        query_f = query.astype(jnp.float32)
        grad_f = grad.astype(jnp.float32)
        scores = jnp.einsum('tkgd,skd->tkgs', query_f, keys) * scale
        top = jnp.max(scores, axis=-1, keepdims=True)
        lse = top + jnp.log(jnp.sum(jnp.exp(scores - top), axis=-1, keepdims=True))
        probs = jnp.exp(scores - lse)
        dprobs = jnp.einsum('tkgd,skd->tkgs', grad_f, values)
        delta = jnp.sum(probs * dprobs, axis=-1, keepdims=True)
        probs_low = lax.optimization_barrier(probs.astype(jnp.bfloat16)).astype(jnp.float32)
        grad_v = jnp.einsum('tkgs,tkgd->skd', probs_low, grad_f)
        dscores = (probs * (dprobs - delta) * scale).astype(jnp.bfloat16)
        dscores = lax.optimization_barrier(dscores).astype(jnp.float32)
        grad_k = jnp.einsum('tkgs,tkgd->skd', dscores, query_f)
        return (carry[0] + grad_k, carry[1] + grad_v), None

    zeros = jnp.zeros((PREFIX, KV, HD), jnp.float32)
    (grad_k, grad_v), _ = lax.scan(one_response, (zeros, zeros), (query_blocks, grad_blocks, lengths))
    dk_low = grad_k.reshape(PREFIX, KV * HD).astype(jnp.bfloat16)
    dv_low = grad_v.reshape(PREFIX, KV * HD).astype(jnp.bfloat16)
    input_grad = jnp.dot(dk_low, k_weight.T, preferred_element_type=jnp.float32)
    input_grad = input_grad + jnp.dot(dv_low, v_weight.T, preferred_element_type=jnp.float32)
    return dk_low, dv_low, input_grad.astype(jnp.bfloat16)
```

```python
import functools

import jax
import jax.numpy as jnp
from jax import lax
from jax.experimental import pallas as pl
from jax.experimental.pallas import tpu as pltpu
from jax.sharding import PartitionSpec as P

HD = 128
LEN = 256
NT = (((1,), (1,)), ((), ()))


def attention_kernel(lengths_ref, q_ref, g_ref, kv_ref, out_ref):
    scale = HD ** (-0.5)
    tokens, both = kv_ref.shape
    width = both // 2
    kv_local = width // HD
    group = q_ref.shape[1] // HD // kv_local
    for part in range(q_ref.shape[0] // LEN):
        rows = pl.ds(part * LEN, LEN)
        live = lax.broadcasted_iota(jnp.int32, (1, LEN), 1) < lengths_ref[part]
        for k in range(kv_local):
            key_cols = pl.ds(k * HD, HD)
            value_cols = pl.ds(width + k * HD, HD)
            keys = kv_ref[:, key_cols]
            values = kv_ref[:, value_cols]
            grad_k = jnp.zeros((tokens, HD), jnp.float32)
            grad_v = jnp.zeros((tokens, HD), jnp.float32)
            for h in range(group):
                cols = pl.ds((k * group + h) * HD, HD)
                q = q_ref[rows, cols]
                g = g_ref[rows, cols]
                scores = lax.dot_general(keys, q, NT, preferred_element_type=jnp.float32)
                dprobs = lax.dot_general(values, g, NT, preferred_element_type=jnp.float32)
                top = jnp.max(scores, axis=0, keepdims=True)
                expo = jnp.exp((scores - top) * scale)
                total = jnp.sum(expo, axis=0, keepdims=True)
                weighted = jnp.sum(expo * dprobs, axis=0, keepdims=True)
                inverse = 1.0 / total
                delta = weighted * inverse
                factor = jnp.where(live, inverse, 0.0)
                probs = expo * factor
                dscores = probs * ((dprobs - delta) * scale)
                grad_v += jnp.dot(
                    probs.astype(jnp.bfloat16), g, preferred_element_type=jnp.float32
                )
                grad_k += jnp.dot(
                    dscores.astype(jnp.bfloat16), q, preferred_element_type=jnp.float32
                )
            if part:
                grad_k += out_ref[:, key_cols]
                grad_v += out_ref[:, value_cols]
            out_ref[:, key_cols] = grad_k
            out_ref[:, value_cols] = grad_v


def projection_kernel(parts_ref, kw_ref, vw_ref, dk_ref, dv_ref, out_ref):
    width = dk_ref.shape[1]
    total = parts_ref[0].astype(jnp.float32)
    for i in range(1, parts_ref.shape[0]):
        total += parts_ref[i].astype(jnp.float32)
    low = total.astype(jnp.bfloat16)
    dk_ref[...] = low[:, :width]
    dv_ref[...] = low[:, width:]
    out = lax.dot_general(low[:, :width], kw_ref[...], NT, preferred_element_type=jnp.float32)
    out += lax.dot_general(low[:, width:], vw_ref[...], NT, preferred_element_type=jnp.float32)
    out_ref[0] = out.astype(out_ref.dtype)


def body(resp, head, queries, d_out, prefix_keys, prefix_values, k_weight, v_weight, lengths):
    own, width = prefix_keys.shape
    features = k_weight.shape[0] // head
    tokens = resp * own

    both = jnp.concatenate([prefix_keys, prefix_values], axis=1)
    both = jnp.broadcast_to(both[None], (resp, own, 2 * width))
    both = lax.all_to_all(both, "resp", 0, 0, tiled=True).reshape(tokens, 2 * width)

    vmem = pl.BlockSpec(memory_space=pltpu.VMEM)
    partial = pl.pallas_call(
        attention_kernel,
        out_shape=jax.ShapeDtypeStruct((tokens, 2 * width), jnp.float32),
        in_specs=[pl.BlockSpec(memory_space=pltpu.SMEM), vmem, vmem, vmem],
        out_specs=vmem,
        compiler_params=pltpu.CompilerParams(vmem_limit_bytes=40 << 20),
        name="attention",
    )(lengths, queries, d_out, both)

    shares = lax.all_to_all(
        partial.astype(jnp.bfloat16).reshape(resp, own, 2 * width), "resp", 0, 0, tiled=True
    )

    steps = 4
    block = features * head // steps
    per = features // block if block < features else 1
    weight = pl.BlockSpec((block, width), lambda i: (i, 0))
    small = pl.BlockSpec((own, width), lambda i: (0, 0))
    dk_low, dv_low, terms = pl.pallas_call(
        projection_kernel,
        grid=(steps,),
        out_shape=[
            jax.ShapeDtypeStruct((own, width), jnp.bfloat16),
            jax.ShapeDtypeStruct((own, width), jnp.bfloat16),
            jax.ShapeDtypeStruct((head, own, features), jnp.bfloat16),
        ],
        in_specs=[
            pl.BlockSpec((resp, own, 2 * width), lambda i: (0, 0, 0)),
            weight,
            weight,
        ],
        out_specs=[
            small,
            small,
            pl.BlockSpec((1, own, block), lambda i: (i // per, 0, i % per)),
        ],
        compiler_params=pltpu.CompilerParams(vmem_limit_bytes=40 << 20),
        name="projection",
    )(shares, k_weight, v_weight)

    terms = lax.all_to_all(terms, "head", 0, 0, tiled=True)
    input_grad = jnp.sum(terms.astype(jnp.float32), axis=0).astype(jnp.bfloat16)
    return dk_low, dv_low, input_grad


def solution(mesh):
    placed = (
        P("resp", "head"),
        P("resp", "head"),
        P("resp", "head"),
        P("resp", "head"),
        P(None, "head"),
        P(None, "head"),
        P("resp"),
    )
    return jax.shard_map(
        functools.partial(body, mesh.shape["resp"], mesh.shape["head"]),
        mesh=mesh,
        in_specs=placed,
        out_specs=(P("resp", "head"), P("resp", "head"), P("resp", "head")),
        check_vma=False,
    )
```

```python
import functools

import jax
import jax.numpy as jnp
from jax import lax
from jax.experimental import pallas as pl
from jax.experimental.pallas import tpu as pltpu
from jax.sharding import PartitionSpec as P

HD = 128
LEN = 256
NT = (((1,), (1,)), ((), ()))
VMEM_LIMIT = 40 << 20


def prefetch_kernel(*refs):
    count = len(refs) // 2
    sems = refs[-1]
    copies = [
        pltpu.make_async_copy(refs[i], refs[count + i], sems.at[i]) for i in range(count)
    ]
    for copy in copies:
        copy.start()
    for copy in copies:
        copy.wait()


def attention_kernel(lengths_ref, q_ref, g_ref, *refs):
    scale = HD ** (-0.5)
    count = len(refs) // 2
    kv_refs, out_refs = refs[:count], refs[count:]
    own, both = kv_refs[0].shape
    tokens = own * count
    width = both // 2
    kv_local = width // HD
    group = q_ref.shape[1] // HD // kv_local
    lives = [
        lax.broadcasted_iota(jnp.int32, (1, LEN), 1) < lengths_ref[part]
        for part in range(q_ref.shape[0] // LEN)
    ]
    for k in range(kv_local):
        key_cols = pl.ds(k * HD, HD)
        value_cols = pl.ds(width + k * HD, HD)
        keys = jnp.concatenate([ref[:, key_cols] for ref in kv_refs], axis=0)
        values = jnp.concatenate([ref[:, value_cols] for ref in kv_refs], axis=0)
        grad_k = jnp.zeros((tokens, HD), jnp.float32)
        grad_v = jnp.zeros((tokens, HD), jnp.float32)
        for part, live in enumerate(lives):
            rows = pl.ds(part * LEN, LEN)
            for h in range(group):
                cols = pl.ds((k * group + h) * HD, HD)
                q = q_ref[rows, cols]
                g = g_ref[rows, cols]
                scores = lax.dot_general(keys, q, NT, preferred_element_type=jnp.float32)
                dprobs = lax.dot_general(values, g, NT, preferred_element_type=jnp.float32)
                top = jnp.max(scores, axis=0, keepdims=True)
                expo = jnp.exp((scores - top) * scale)
                total = jnp.sum(expo, axis=0, keepdims=True)
                weighted = jnp.sum(expo * dprobs, axis=0, keepdims=True)
                inverse = 1.0 / total
                delta = weighted * inverse
                factor = jnp.where(live, inverse, 0.0)
                probs = expo * factor
                dscores = probs * ((dprobs - delta) * scale)
                grad_v += jnp.dot(
                    probs.astype(jnp.bfloat16), g, preferred_element_type=jnp.float32
                )
                grad_k += jnp.dot(
                    dscores.astype(jnp.bfloat16), q, preferred_element_type=jnp.float32
                )
        for i, ref in enumerate(out_refs):
            rows = slice(i * own, (i + 1) * own)
            ref[:, key_cols] = grad_k[rows].astype(ref.dtype)
            ref[:, value_cols] = grad_v[rows].astype(ref.dtype)


def projection_kernel(count, head, *refs):
    parts, (kw_ref, vw_ref, dk_ref, dv_ref), out_refs = (
        refs[:count],
        refs[count : count + 4],
        refs[count + 4 :],
    )
    width = dk_ref.shape[1]
    total = parts[0][...]
    for ref in parts[1:]:
        total += ref[...].astype(jnp.float32)
    low = total.astype(jnp.bfloat16)
    dk_ref[...] = low[:, :width]
    dv_ref[...] = low[:, width:]
    features = out_refs[0].shape[1]
    me = lax.axis_index("head")
    for i, ref in enumerate(out_refs):
        rows = pl.ds(pl.multiple_of(lax.rem(me + i, head) * features, features), features)
        out = lax.dot_general(
            low[:, :width], kw_ref[rows, :], NT, preferred_element_type=jnp.float32
        )
        out += lax.dot_general(
            low[:, width:], vw_ref[rows, :], NT, preferred_element_type=jnp.float32
        )
        ref[...] = out.astype(ref.dtype)


def shift(x, axis, count, by):
    return lax.ppermute(x, axis, [(i, (i + by) % count) for i in range(count)])


def body(resp, head, queries, d_out, prefix_keys, prefix_values, k_weight, v_weight, lengths):
    own, width = prefix_keys.shape
    features = k_weight.shape[0] // head
    vmem = pl.BlockSpec(memory_space=pltpu.VMEM)
    hbm = pl.BlockSpec(memory_space=pltpu.HBM)
    params = pltpu.CompilerParams(vmem_limit_bytes=VMEM_LIMIT)

    both = jnp.concatenate([prefix_keys, prefix_values], axis=1)
    blocks = [both] + [shift(both, "resp", resp, d) for d in range(1, resp)]

    large = (queries, d_out, k_weight, v_weight)
    queries, d_out, k_weight, v_weight = pl.pallas_call(
        prefetch_kernel,
        out_shape=[pltpu.VMEM(x.shape, x.dtype) for x in large],
        in_specs=[hbm] * len(large),
        out_specs=[vmem] * len(large),
        scratch_shapes=[pltpu.SemaphoreType.DMA((len(large),))],
        compiler_params=params,
        cost_estimate=pl.CostEstimate(
            flops=0, transcendentals=0, bytes_accessed=sum(x.size * 2 for x in large)
        ),
        name="prefetch",
    )(*[pltpu.with_memory_space_constraint(x, pltpu.HBM) for x in large])

    partial = pl.pallas_call(
        attention_kernel,
        out_shape=[jax.ShapeDtypeStruct((own, 2 * width), jnp.float32)]
        + [jax.ShapeDtypeStruct((own, 2 * width), jnp.bfloat16)] * (resp - 1),
        in_specs=[pl.BlockSpec(memory_space=pltpu.SMEM)] + [vmem] * (resp + 2),
        out_specs=[vmem] * resp,
        compiler_params=params,
        name="attention",
    )(lengths, queries, d_out, *blocks)

    shares = [partial[0]] + [shift(partial[d], "resp", resp, resp - d) for d in range(1, resp)]

    dk_low, dv_low, *terms = pl.pallas_call(
        functools.partial(projection_kernel, resp, head),
        out_shape=[jax.ShapeDtypeStruct((own, width), jnp.bfloat16)] * 2
        + [jax.ShapeDtypeStruct((own, features), jnp.float32)]
        + [jax.ShapeDtypeStruct((own, features), jnp.bfloat16)] * (head - 1),
        in_specs=[vmem] * (resp + 2),
        out_specs=[vmem] * (head + 2),
        compiler_params=params,
        name="projection",
    )(*shares, k_weight, v_weight)

    total = terms[0]
    for d in range(1, head):
        total += shift(terms[d], "head", head, d).astype(jnp.float32)
    return dk_low, dv_low, total.astype(jnp.bfloat16)


def solution(mesh):
    placed = (
        P("resp", "head"),
        P("resp", "head"),
        P("resp", "head"),
        P("resp", "head"),
        P(None, "head"),
        P(None, "head"),
        P("resp"),
    )
    return jax.shard_map(
        functools.partial(body, mesh.shape["resp"], mesh.shape["head"]),
        mesh=mesh,
        in_specs=placed,
        out_specs=(P("resp", "head"), P("resp", "head"), P("resp", "head")),
        check_vma=False,
    )
```

```python
import functools

import jax
import jax.numpy as jnp
from jax import lax
from jax.experimental import pallas as pl
from jax.experimental.pallas import tpu as pltpu
from jax.sharding import PartitionSpec as P

HD = 128
LEN = 256
NT = (((1,), (1,)), ((), ()))
VMEM_LIMIT = 40 << 20


def join_kernel(k_hbm, v_hbm, out_ref, sems):
    width = k_hbm.shape[1]
    copies = [
        pltpu.make_async_copy(k_hbm, out_ref.at[:, pl.ds(0, width)], sems.at[0]),
        pltpu.make_async_copy(v_hbm, out_ref.at[:, pl.ds(width, width)], sems.at[1]),
    ]
    for copy in copies:
        copy.start()
    for copy in copies:
        copy.wait()


def attention_kernel(
    lengths_ref,
    near_ref,
    far_ref,
    q_hbm,
    g_hbm,
    kw_hbm,
    vw_hbm,
    keep_ref,
    send_ref,
    kw_ref,
    vw_ref,
    q_ref,
    g_ref,
    head_sems,
    weight_sems,
):
    scale = HD ** (-0.5)
    half, both = near_ref.shape
    width = both // 2
    kv_local = width // HD
    heads = q_ref.shape[1] // HD
    group = heads // kv_local
    chunks = head_sems.shape[1]
    per = heads // chunks
    lives = [
        lax.broadcasted_iota(jnp.int32, (1, LEN), 1) < lengths_ref[part]
        for part in range(q_ref.shape[0] // LEN)
    ]
    loads = []
    for c in range(chunks):
        cols = pl.ds(c * per * HD, per * HD)
        pair = [
            pltpu.make_async_copy(q_hbm.at[:, cols], q_ref.at[:, cols], head_sems.at[0, c]),
            pltpu.make_async_copy(g_hbm.at[:, cols], g_ref.at[:, cols], head_sems.at[1, c]),
        ]
        for copy in pair:
            copy.start()
        loads.append(pair)
    weights = [
        pltpu.make_async_copy(kw_hbm, kw_ref, weight_sems.at[0]),
        pltpu.make_async_copy(vw_hbm, vw_ref, weight_sems.at[1]),
    ]
    for copy in weights:
        copy.start()
    for k in range(kv_local):
        key_cols = pl.ds(k * HD, HD)
        value_cols = pl.ds(width + k * HD, HD)
        keys = jnp.concatenate([near_ref[:, key_cols], far_ref[:, key_cols]], axis=0)
        values = jnp.concatenate([near_ref[:, value_cols], far_ref[:, value_cols]], axis=0)
        grad_k = jnp.zeros((2 * half, HD), jnp.float32)
        grad_v = jnp.zeros((2 * half, HD), jnp.float32)
        for h in range(k * group, (k + 1) * group):
            if h % per == 0:
                for copy in loads[h // per]:
                    copy.wait()
            cols = pl.ds(h * HD, HD)
            for part, live in enumerate(lives):
                rows = pl.ds(part * LEN, LEN)
                q = q_ref[rows, cols]
                g = g_ref[rows, cols]
                scores = lax.dot_general(keys, q, NT, preferred_element_type=jnp.float32)
                dprobs = lax.dot_general(values, g, NT, preferred_element_type=jnp.float32)
                top = jnp.max(scores, axis=0, keepdims=True)
                expo = jnp.exp((scores - top) * scale)
                total = jnp.sum(expo, axis=0, keepdims=True)
                weighted = jnp.sum(expo * dprobs, axis=0, keepdims=True)
                inverse = 1.0 / total
                delta = weighted * inverse
                factor = jnp.where(live, inverse, 0.0)
                probs = expo * factor
                dscores = probs * ((dprobs - delta) * scale)
                grad_v += jnp.dot(
                    probs.astype(jnp.bfloat16), g, preferred_element_type=jnp.float32
                )
                grad_k += jnp.dot(
                    dscores.astype(jnp.bfloat16), q, preferred_element_type=jnp.float32
                )
        keep_ref[:, key_cols] = grad_k[:half]
        keep_ref[:, value_cols] = grad_v[:half]
        send_ref[:, key_cols] = grad_k[half:].astype(send_ref.dtype)
        send_ref[:, value_cols] = grad_v[half:].astype(send_ref.dtype)
    for copy in weights:
        copy.wait()


def project(low_k, low_v, kw_ref, vw_ref, out_ref, owners):
    features = out_ref.shape[1] // len(owners)
    for i, owner in enumerate(owners):
        rows = pl.ds(pl.multiple_of(owner * features, features), features)
        out = lax.dot_general(low_k, kw_ref[rows, :], NT, preferred_element_type=jnp.float32)
        out += lax.dot_general(low_v, vw_ref[rows, :], NT, preferred_element_type=jnp.float32)
        out_ref[:, i * features : (i + 1) * features] = out.astype(out_ref.dtype)


def send_projection_kernel(order, keep_ref, got_ref, kw_ref, vw_ref, dk_ref, dv_ref, low_ref, out_ref):
    width = dk_ref.shape[1]
    low = (keep_ref[...] + got_ref[...].astype(jnp.float32)).astype(jnp.bfloat16)
    low_k, low_v = low[:, :width], low[:, width:]
    dk_ref[...] = low_k
    dv_ref[...] = low_v
    low_ref[...] = low
    me = lax.axis_index("head")
    project(low_k, low_v, kw_ref, vw_ref, out_ref, [me ^ i for i in order])


def keep_projection_kernel(order, low_ref, kw_ref, vw_ref, out_ref):
    width = kw_ref.shape[1]
    me = lax.axis_index("head")
    project(low_ref[:, :width], low_ref[:, width:], kw_ref, vw_ref, out_ref, [me ^ i for i in order])


def swap(x, axis, count, bit):
    return lax.ppermute(x, axis, [(i, i ^ bit) for i in range(count)])


def body(resp, head, queries, d_out, prefix_keys, prefix_values, k_weight, v_weight, lengths):
    own, width = prefix_keys.shape
    features = k_weight.shape[0] // head
    vmem = pl.BlockSpec(memory_space=pltpu.VMEM)
    hbm = pl.BlockSpec(memory_space=pltpu.HBM)
    params = pltpu.CompilerParams(vmem_limit_bytes=VMEM_LIMIT)
    resp_bits = [1 << i for i in range(resp.bit_length() - 1)]
    head_bits = [1 << i for i in range(head.bit_length() - 1)]

    near = pl.pallas_call(
        join_kernel,
        out_shape=pltpu.VMEM((own, 2 * width), jnp.bfloat16),
        in_specs=[hbm, hbm],
        out_specs=vmem,
        scratch_shapes=[pltpu.SemaphoreType.DMA((2,))],
        compiler_params=params,
        name="join",
    )(*[pltpu.with_memory_space_constraint(x, pltpu.HBM) for x in (prefix_keys, prefix_values)])
    for bit in resp_bits[::-1]:
        far = swap(near, "resp", resp, bit)
        if bit > 1:
            near = jnp.concatenate([near, far], axis=0)

    half = resp * own // 2
    chunks = 4
    large = [
        pltpu.with_memory_space_constraint(x, pltpu.HBM)
        for x in (queries, d_out, k_weight, v_weight)
    ]
    keep, send, k_weight, v_weight = pl.pallas_call(
        attention_kernel,
        out_shape=[
            jax.ShapeDtypeStruct((half, 2 * width), jnp.float32),
            jax.ShapeDtypeStruct((half, 2 * width), jnp.bfloat16),
            pltpu.VMEM(k_weight.shape, k_weight.dtype),
            pltpu.VMEM(v_weight.shape, v_weight.dtype),
        ],
        in_specs=[pl.BlockSpec(memory_space=pltpu.SMEM), vmem, vmem] + [hbm] * 4,
        out_specs=[vmem] * 4,
        scratch_shapes=[
            pltpu.VMEM(queries.shape, queries.dtype),
            pltpu.VMEM(d_out.shape, d_out.dtype),
            pltpu.SemaphoreType.DMA((2, chunks)),
            pltpu.SemaphoreType.DMA((2,)),
        ],
        compiler_params=params,
        name="attention",
    )(lengths, near, far, *large)

    for bit in resp_bits:
        got = swap(send, "resp", resp, bit)
        if bit < resp // 2:
            half //= 2
            total = keep + got.astype(jnp.float32)
            keep, send = total[:half], total[half:].astype(jnp.bfloat16)

    order = [0]
    for bit in head_bits[::-1]:
        order = order + [i + bit for i in order]
    wide = head // 2 * features
    dk_low, dv_low, low, send = pl.pallas_call(
        functools.partial(send_projection_kernel, order[head // 2 :]),
        out_shape=[jax.ShapeDtypeStruct((own, width), jnp.bfloat16)] * 2
        + [pltpu.VMEM((own, 2 * width), jnp.bfloat16)]
        + [pltpu.VMEM((own, wide), jnp.bfloat16)],
        in_specs=[vmem] * 4,
        out_specs=[vmem] * 4,
        compiler_params=params,
        name="projection_to_send",
    )(keep, got, k_weight, v_weight)
    keep = pl.pallas_call(
        functools.partial(keep_projection_kernel, order[: head // 2]),
        out_shape=jax.ShapeDtypeStruct((own, wide), jnp.float32),
        in_specs=[vmem] * 3,
        out_specs=vmem,
        compiler_params=params,
        cost_estimate=pl.CostEstimate(
            flops=4 * own * width * wide, transcendentals=0, bytes_accessed=4 * width * wide
        ),
        name="projection_to_keep",
    )(low, k_weight, v_weight)
    for bit in head_bits:
        total = keep + swap(send, "head", head, bit).astype(jnp.float32)
        wide //= 2
        keep, send = total[:, :wide], total[:, wide:].astype(jnp.bfloat16)
    return dk_low, dv_low, total.astype(jnp.bfloat16)


def solution(mesh):
    placed = (
        P("resp", "head"),
        P("resp", "head"),
        P("resp", "head"),
        P("resp", "head"),
        P(None, "head"),
        P(None, "head"),
        P("resp"),
    )
    return jax.shard_map(
        functools.partial(body, mesh.shape["resp"], mesh.shape["head"]),
        mesh=mesh,
        in_specs=placed,
        out_specs=(P("resp", "head"), P("resp", "head"), P("resp", "head")),
        check_vma=False,
    )
```

```python
import functools

import jax
import jax.numpy as jnp
from jax import lax
from jax.experimental import pallas as pl
from jax.experimental.pallas import tpu as pltpu
from jax.sharding import PartitionSpec as P

HD = 128
LEN = 256
NT = (((1,), (1,)), ((), ()))
VMEM_LIMIT = 40 << 20
LOG2E = 1.4426950408889634


def join_kernel(k_hbm, v_hbm, out_ref, sems):
    width = k_hbm.shape[1]
    copies = []
    for i in range(out_ref.shape[0]):
        copies += [
            pltpu.make_async_copy(k_hbm, out_ref.at[i, :, pl.ds(0, width)], sems.at[0, i]),
            pltpu.make_async_copy(v_hbm, out_ref.at[i, :, pl.ds(width, width)], sems.at[1, i]),
        ]
    for copy in copies:
        copy.start()
    for copy in copies:
        copy.wait()


def load_kernel(q_hbm, g_hbm, q_ref, g_ref, sems):
    copies = [
        pltpu.make_async_copy(q_hbm, q_ref, sems.at[0]),
        pltpu.make_async_copy(g_hbm, g_ref, sems.at[1]),
    ]
    for copy in copies:
        copy.start()
    for copy in copies:
        copy.wait()


def attention_kernel(
    lengths_ref,
    kv_ref,
    q_ref,
    g_ref,
    kw_hbm,
    vw_hbm,
    out_ref,
    kw_ref,
    vw_ref,
    probs_ref,
    dscores_ref,
    sems,
):
    weights = [
        pltpu.make_async_copy(kw_hbm, kw_ref, sems.at[0]),
        pltpu.make_async_copy(vw_hbm, vw_ref, sems.at[1]),
    ]
    for copy in weights:
        copy.start()
    scale = HD ** (-0.5)
    width = kv_ref.shape[1] // 2
    kv_local = width // HD
    parts = q_ref.shape[0] // LEN
    group = q_ref.shape[1] // HD // kv_local
    lives = [
        lax.broadcasted_iota(jnp.int32, (1, LEN), 1) < lengths_ref[part] for part in range(parts)
    ]
    units = [(k, h, part) for k in range(kv_local) for h in range(group) for part in range(parts)]

    def place(unit):
        k, h, part = unit
        return pl.ds(part * LEN, LEN), pl.ds((k * group + h) * HD, HD)

    def products(unit):
        k = unit[0]
        where = place(unit)
        keys = kv_ref[:, k * HD : (k + 1) * HD]
        values = kv_ref[:, width + k * HD : width + (k + 1) * HD]
        return (
            lax.dot_general(keys, q_ref[where], NT, preferred_element_type=jnp.float32),
            lax.dot_general(values, g_ref[where], NT, preferred_element_type=jnp.float32),
        )

    following = products(units[0])
    for i, unit in enumerate(units):
        k, h, part = unit
        scores, dprobs = following
        if i + 1 < len(units):
            following = products(units[i + 1])
        top = jnp.max(scores, axis=0, keepdims=True)
        expo = jnp.exp2((scores - top) * (scale * LOG2E))
        total = jnp.sum(expo, axis=0, keepdims=True)
        weighted = jnp.sum(expo * dprobs, axis=0, keepdims=True)
        inverse = 1.0 / total
        delta = weighted * inverse
        factor = jnp.where(lives[part], inverse, 0.0)
        probs = expo * factor
        at = (h * parts + part) * LEN
        probs_ref[k, :, at : at + LEN] = probs.astype(jnp.bfloat16)
        dscores_ref[k, :, at : at + LEN] = (probs * (dprobs - delta)).astype(jnp.bfloat16)
        if (h, part) == (group - 1, parts - 1):
            mine = [place(u) for u in units if u[0] == k]
            q_all = jnp.concatenate([q_ref[where] for where in mine], axis=0)
            g_all = jnp.concatenate([g_ref[where] for where in mine], axis=0)
            grad_k = jnp.dot(dscores_ref[k], q_all, preferred_element_type=jnp.float32) * scale
            grad_v = jnp.dot(probs_ref[k], g_all, preferred_element_type=jnp.float32)
            out_ref[:, k * HD : (k + 1) * HD] = grad_k.astype(out_ref.dtype)
            out_ref[:, width + k * HD : width + (k + 1) * HD] = grad_v.astype(out_ref.dtype)
    for copy in weights:
        copy.wait()


def project(low_k, low_v, kw_ref, vw_ref, out_ref, owners):
    features = out_ref.shape[1] // len(owners)
    for i, owner in enumerate(owners):
        rows = pl.ds(pl.multiple_of(owner * features, features), features)
        out = lax.dot_general(low_k, kw_ref[rows, :], NT, preferred_element_type=jnp.float32)
        out += lax.dot_general(low_v, vw_ref[rows, :], NT, preferred_element_type=jnp.float32)
        out_ref[:, i * features : (i + 1) * features] = out.astype(out_ref.dtype)


def send_projection_kernel(order, parts_ref, kw_ref, vw_ref, dk_ref, dv_ref, low_ref, out_ref):
    width = dk_ref.shape[1]
    total = parts_ref[0].astype(jnp.float32)
    for i in range(1, parts_ref.shape[0]):
        total += parts_ref[i].astype(jnp.float32)
    low = total.astype(jnp.bfloat16)
    low_k, low_v = low[:, :width], low[:, width:]
    dk_ref[...] = low_k
    dv_ref[...] = low_v
    low_ref[...] = low
    me = lax.axis_index("head")
    project(low_k, low_v, kw_ref, vw_ref, out_ref, [me ^ i for i in order])


def keep_projection_kernel(order, low_ref, kw_ref, vw_ref, out_ref):
    width = kw_ref.shape[1]
    me = lax.axis_index("head")
    project(low_ref[:, :width], low_ref[:, width:], kw_ref, vw_ref, out_ref, [me ^ i for i in order])


def swap(x, axis, count, bit):
    return lax.ppermute(x, axis, [(i, i ^ bit) for i in range(count)])


def body(resp, head, queries, d_out, prefix_keys, prefix_values, k_weight, v_weight, lengths):
    own, width = prefix_keys.shape
    features = k_weight.shape[0] // head
    vmem = pl.BlockSpec(memory_space=pltpu.VMEM)
    hbm = pl.BlockSpec(memory_space=pltpu.HBM)
    params = pltpu.CompilerParams(vmem_limit_bytes=VMEM_LIMIT)
    head_bits = [1 << i for i in range(head.bit_length() - 1)]

    def in_hbm(*xs):
        return [pltpu.with_memory_space_constraint(x, pltpu.HBM) for x in xs]

    both = pl.pallas_call(
        join_kernel,
        out_shape=pltpu.VMEM((resp, own, 2 * width), jnp.bfloat16),
        in_specs=[hbm] * 2,
        out_specs=vmem,
        scratch_shapes=[pltpu.SemaphoreType.DMA((2, resp))],
        compiler_params=params,
        name="join",
    )(*in_hbm(prefix_keys, prefix_values))
    both = lax.all_to_all(both, "resp", 0, 0, tiled=True).reshape(resp * own, 2 * width)

    queries, d_out = pl.pallas_call(
        load_kernel,
        out_shape=[pltpu.VMEM(x.shape, x.dtype) for x in (queries, d_out)],
        in_specs=[hbm] * 2,
        out_specs=[vmem] * 2,
        scratch_shapes=[pltpu.SemaphoreType.DMA((2,))],
        compiler_params=params,
        cost_estimate=pl.CostEstimate(
            flops=0, transcendentals=0, bytes_accessed=4 * queries.size * 2
        ),
        name="load",
    )(*in_hbm(queries, d_out))

    tokens = resp * own
    kv_local = width // HD
    depth = queries.size // kv_local // HD
    partial, k_weight, v_weight = pl.pallas_call(
        attention_kernel,
        out_shape=[
            pltpu.VMEM((tokens, 2 * width), jnp.bfloat16),
            pltpu.VMEM(k_weight.shape, k_weight.dtype),
            pltpu.VMEM(v_weight.shape, v_weight.dtype),
        ],
        in_specs=[pl.BlockSpec(memory_space=pltpu.SMEM)] + [vmem] * 3 + [hbm] * 2,
        out_specs=[vmem] * 3,
        scratch_shapes=[
            pltpu.VMEM((kv_local, tokens, depth), jnp.bfloat16),
            pltpu.VMEM((kv_local, tokens, depth), jnp.bfloat16),
            pltpu.SemaphoreType.DMA((2,)),
        ],
        compiler_params=params,
        name="attention",
    )(lengths, both, queries, d_out, *in_hbm(k_weight, v_weight))

    shares = lax.all_to_all(
        partial.reshape(resp, own, 2 * width), "resp", 0, 0, tiled=True
    )

    order = [0]
    for bit in head_bits[::-1]:
        order = order + [i + bit for i in order]
    wide = head // 2 * features
    dk_low, dv_low, low, send = pl.pallas_call(
        functools.partial(send_projection_kernel, order[head // 2 :]),
        out_shape=[jax.ShapeDtypeStruct((own, width), jnp.bfloat16)] * 2
        + [pltpu.VMEM((own, 2 * width), jnp.bfloat16)]
        + [pltpu.VMEM((own, wide), jnp.bfloat16)],
        in_specs=[vmem] * 3,
        out_specs=[vmem] * 4,
        compiler_params=params,
        name="projection_to_send",
    )(shares, k_weight, v_weight)
    keep = pl.pallas_call(
        functools.partial(keep_projection_kernel, order[: head // 2]),
        out_shape=jax.ShapeDtypeStruct((own, wide), jnp.float32),
        in_specs=[vmem] * 3,
        out_specs=vmem,
        compiler_params=params,
        cost_estimate=pl.CostEstimate(
            flops=4 * own * width * wide, transcendentals=0, bytes_accessed=4 * width * wide
        ),
        name="projection_to_keep",
    )(low, k_weight, v_weight)
    for bit in head_bits:
        total = keep + swap(send, "head", head, bit).astype(jnp.float32)
        wide //= 2
        keep, send = total[:, :wide], total[:, wide:].astype(jnp.bfloat16)
    return dk_low, dv_low, total.astype(jnp.bfloat16)


def solution(mesh):
    placed = (
        P("resp", "head"),
        P("resp", "head"),
        P("resp", "head"),
        P("resp", "head"),
        P(None, "head"),
        P(None, "head"),
        P("resp"),
    )
    return jax.shard_map(
        functools.partial(body, mesh.shape["resp"], mesh.shape["head"]),
        mesh=mesh,
        in_specs=placed,
        out_specs=(P("resp", "head"), P("resp", "head"), P("resp", "head")),
        check_vma=False,
    )
```

```python
import functools

import jax
import jax.numpy as jnp
from jax import lax
from jax.experimental import pallas as pl
from jax.experimental.pallas import tpu as pltpu
from jax.sharding import PartitionSpec as P

HD = 128
LEN = 256
NT = (((1,), (1,)), ((), ()))
VMEM_LIMIT = 40 << 20
LOG2E = 1.4426950408889634


def join_kernel(k_hbm, v_hbm, out_ref, both_ref, sems):
    width = k_hbm.shape[1]
    copies = [
        pltpu.make_async_copy(k_hbm, both_ref.at[:, pl.ds(0, width)], sems.at[0]),
        pltpu.make_async_copy(v_hbm, both_ref.at[:, pl.ds(width, width)], sems.at[1]),
    ]
    for copy in copies:
        copy.start()
    for copy in copies:
        copy.wait()
    both = both_ref[...]
    for i in range(out_ref.shape[0]):
        out_ref[i] = both


def load_kernel(q_hbm, g_hbm, q_ref, g_ref, sems):
    copies = [
        pltpu.make_async_copy(q_hbm, q_ref, sems.at[0]),
        pltpu.make_async_copy(g_hbm, g_ref, sems.at[1]),
    ]
    for copy in copies:
        copy.start()
    for copy in copies:
        copy.wait()


def attention_kernel(
    lengths_ref,
    kv_ref,
    q_ref,
    g_ref,
    kw_hbm,
    vw_hbm,
    out_ref,
    kw_ref,
    vw_ref,
    scores_ref,
    dprobs_ref,
    probs_ref,
    dscores_ref,
    sems,
):
    weights = [
        pltpu.make_async_copy(kw_hbm, kw_ref, sems.at[0]),
        pltpu.make_async_copy(vw_hbm, vw_ref, sems.at[1]),
    ]
    for copy in weights:
        copy.start()
    scale = HD ** (-0.5)
    width = kv_ref.shape[1] // 2
    kv_local = width // HD
    parts = q_ref.shape[0] // LEN
    group = q_ref.shape[1] // HD // kv_local
    position = lax.broadcasted_iota(jnp.int32, (1, HD), 1)
    units = [(k, h, part) for k in range(kv_local) for h in range(group) for part in range(parts)]

    def place(unit):
        k, h, part = unit
        return pl.ds(part * LEN, LEN), pl.ds((k * group + h) * HD, HD)

    def products(i):
        k = units[i][0]
        where = place(units[i])
        keys = kv_ref[:, k * HD : (k + 1) * HD]
        values = kv_ref[:, width + k * HD : width + (k + 1) * HD]
        scores_ref[i % 2] = lax.dot_general(
            keys, q_ref[where], NT, preferred_element_type=jnp.float32
        )
        dprobs_ref[i % 2] = lax.dot_general(
            values, g_ref[where], NT, preferred_element_type=jnp.float32
        )

    products(0)
    for i, unit in enumerate(units):
        k, h, part = unit
        if i + 1 < len(units):
            products(i + 1)
        for start in range(0, LEN, HD):
            scores = scores_ref[i % 2, :, start : start + HD]
            dprobs = dprobs_ref[i % 2, :, start : start + HD]
            top = jnp.max(scores, axis=0, keepdims=True)
            expo = jnp.exp2((scores - top) * (scale * LOG2E))
            total = jnp.sum(expo, axis=0, keepdims=True)
            weighted = jnp.sum(expo * dprobs, axis=0, keepdims=True)
            inverse = 1.0 / total
            delta = weighted * inverse
            factor = jnp.where(position + start < lengths_ref[part], inverse, 0.0)
            probs = expo * factor
            at = (h * parts + part) * LEN + start
            probs_ref[k, :, at : at + HD] = probs.astype(jnp.bfloat16)
            dscores_ref[k, :, at : at + HD] = (probs * (dprobs - delta)).astype(jnp.bfloat16)
        if (h, part) == (group - 1, parts - 1):
            mine = [place(u) for u in units if u[0] == k]
            q_all = jnp.concatenate([q_ref[where] for where in mine], axis=0)
            g_all = jnp.concatenate([g_ref[where] for where in mine], axis=0)
            grad_k = jnp.dot(dscores_ref[k], q_all, preferred_element_type=jnp.float32) * scale
            grad_v = jnp.dot(probs_ref[k], g_all, preferred_element_type=jnp.float32)
            out_ref[:, k * HD : (k + 1) * HD] = grad_k.astype(out_ref.dtype)
            out_ref[:, width + k * HD : width + (k + 1) * HD] = grad_v.astype(out_ref.dtype)
    for copy in weights:
        copy.wait()


def project(low, kw_ref, vw_ref, owner, features):
    width = kw_ref.shape[1]
    rows = pl.ds(pl.multiple_of(owner * features, features), features)
    out = lax.dot_general(
        low[:, :width], kw_ref[rows, :], NT, preferred_element_type=jnp.float32
    )
    return out + lax.dot_general(
        low[:, width:], vw_ref[rows, :], NT, preferred_element_type=jnp.float32
    )


def first_projection_kernel(owner, parts_ref, kw_ref, vw_ref, low_ref, out_ref):
    total = parts_ref[0].astype(jnp.float32)
    for i in range(1, parts_ref.shape[0]):
        total += parts_ref[i].astype(jnp.float32)
    low = total.astype(jnp.bfloat16)
    low_ref[...] = low
    me = lax.axis_index("head")
    out = project(low, kw_ref, vw_ref, me ^ owner, out_ref.shape[1])
    out_ref[...] = out.astype(out_ref.dtype)


def second_projection_kernel(owner, low_ref, kw_ref, vw_ref, out_ref):
    me = lax.axis_index("head")
    out_ref[...] = project(low_ref[...], kw_ref, vw_ref, me ^ owner, out_ref.shape[1])


def last_projection_kernel(low_ref, kw_ref, vw_ref, after, out_ref, keep_ref, dk_ref, dv_ref):
    width = dk_ref.shape[1]
    low = low_ref[...]
    dk_ref[...] = low[:, :width]
    dv_ref[...] = low[:, width:]
    me = lax.axis_index("head")
    out = project(low, kw_ref, vw_ref, me ^ 1, out_ref.shape[1])
    out_ref[...] = out.astype(out_ref.dtype)
    keep_ref[...] = project(low, kw_ref, vw_ref, me, keep_ref.shape[1])


def swap(x, axis, count, bit):
    return lax.ppermute(x, axis, [(i, i ^ bit) for i in range(count)])


def body(resp, head, queries, d_out, prefix_keys, prefix_values, k_weight, v_weight, lengths):
    own, width = prefix_keys.shape
    features = k_weight.shape[0] // head
    vmem = pl.BlockSpec(memory_space=pltpu.VMEM)
    hbm = pl.BlockSpec(memory_space=pltpu.HBM)
    params = pltpu.CompilerParams(vmem_limit_bytes=VMEM_LIMIT)

    def in_hbm(*xs):
        return [pltpu.with_memory_space_constraint(x, pltpu.HBM) for x in xs]

    both = pl.pallas_call(
        join_kernel,
        out_shape=pltpu.VMEM((resp, own, 2 * width), jnp.bfloat16),
        in_specs=[hbm] * 2,
        out_specs=vmem,
        scratch_shapes=[
            pltpu.VMEM((own, 2 * width), jnp.bfloat16),
            pltpu.SemaphoreType.DMA((2,)),
        ],
        compiler_params=params,
        name="join",
    )(*in_hbm(prefix_keys, prefix_values))
    both = lax.all_to_all(both, "resp", 0, 0, tiled=True).reshape(resp * own, 2 * width)

    queries, d_out = pl.pallas_call(
        load_kernel,
        out_shape=[pltpu.VMEM(x.shape, x.dtype) for x in (queries, d_out)],
        in_specs=[hbm] * 2,
        out_specs=[vmem] * 2,
        scratch_shapes=[pltpu.SemaphoreType.DMA((2,))],
        compiler_params=params,
        cost_estimate=pl.CostEstimate(
            flops=0, transcendentals=0, bytes_accessed=4 * queries.size * 2
        ),
        name="load",
    )(*in_hbm(queries, d_out))

    tokens = resp * own
    kv_local = width // HD
    depth = queries.size // kv_local // HD
    partial, k_weight, v_weight = pl.pallas_call(
        attention_kernel,
        out_shape=[
            pltpu.VMEM((tokens, 2 * width), jnp.bfloat16),
            pltpu.VMEM(k_weight.shape, k_weight.dtype),
            pltpu.VMEM(v_weight.shape, v_weight.dtype),
        ],
        in_specs=[pl.BlockSpec(memory_space=pltpu.SMEM)] + [vmem] * 3 + [hbm] * 2,
        out_specs=[vmem] * 3,
        scratch_shapes=[
            pltpu.VMEM((2, tokens, LEN), jnp.float32),
            pltpu.VMEM((2, tokens, LEN), jnp.float32),
            pltpu.VMEM((kv_local, tokens, depth), jnp.bfloat16),
            pltpu.VMEM((kv_local, tokens, depth), jnp.bfloat16),
            pltpu.SemaphoreType.DMA((2,)),
        ],
        compiler_params=params,
        name="attention",
    )(lengths, both, queries, d_out, *in_hbm(k_weight, v_weight))

    shares = lax.all_to_all(
        partial.reshape(resp, own, 2 * width), "resp", 0, 0, tiled=True
    )

    block = (own, features)
    low, to_core = pl.pallas_call(
        functools.partial(first_projection_kernel, 3),
        out_shape=[
            pltpu.VMEM((own, 2 * width), jnp.bfloat16),
            pltpu.VMEM(block, jnp.bfloat16),
        ],
        in_specs=[vmem] * 3,
        out_specs=[vmem] * 2,
        compiler_params=params,
        name="projection_other_core",
    )(shares, k_weight, v_weight)
    cost = pl.CostEstimate(
        flops=4 * own * width * features, transcendentals=0, bytes_accessed=4 * width * features
    )
    far = pl.pallas_call(
        functools.partial(second_projection_kernel, 2),
        out_shape=pltpu.VMEM(block, jnp.float32),
        in_specs=[vmem] * 3,
        out_specs=vmem,
        compiler_params=params,
        cost_estimate=cost,
        name="projection_other_y",
    )(low, k_weight, v_weight)
    far = (far + swap(to_core, "head", head, 1).astype(jnp.float32)).astype(jnp.bfloat16)
    got = swap(far, "head", head, 2)
    to_core, total, dk_low, dv_low = pl.pallas_call(
        last_projection_kernel,
        out_shape=[
            pltpu.VMEM(block, jnp.bfloat16),
            pltpu.VMEM(block, jnp.float32),
            jax.ShapeDtypeStruct((own, width), jnp.bfloat16),
            jax.ShapeDtypeStruct((own, width), jnp.bfloat16),
        ],
        in_specs=[vmem] * 3 + [pl.BlockSpec(memory_space=pl.ANY)],
        out_specs=[vmem] * 4,
        compiler_params=params,
        cost_estimate=cost,
        name="projection_this_y",
    )(low, k_weight, v_weight, far)
    total = lax.optimization_barrier(total + got.astype(jnp.float32))
    total += swap(to_core, "head", head, 1).astype(jnp.float32)
    return dk_low, dv_low, total.astype(jnp.bfloat16)


def solution(mesh):
    placed = (
        P("resp", "head"),
        P("resp", "head"),
        P("resp", "head"),
        P("resp", "head"),
        P(None, "head"),
        P(None, "head"),
        P("resp"),
    )
    return jax.shard_map(
        functools.partial(body, mesh.shape["resp"], mesh.shape["head"]),
        mesh=mesh,
        in_specs=placed,
        out_specs=(P("resp", "head"), P("resp", "head"), P("resp", "head")),
        check_vma=False,
    )
```

```python
import functools

import jax
import jax.numpy as jnp
from jax import lax
from jax.experimental import pallas as pl
from jax.experimental.pallas import tpu as pltpu
from jax.sharding import PartitionSpec as P

HD = 128
LEN = 256
NT = (((1,), (1,)), ((), ()))
VMEM_LIMIT = 40 << 20
UNIT = 2
LOG2E = 1.4426950408889634


def join_kernel(k_hbm, v_hbm, out_hbm, sems):
    width = k_hbm.shape[1]
    copies = []
    for i in range(out_hbm.shape[0]):
        copies += [
            pltpu.make_async_copy(k_hbm, out_hbm.at[i, :, pl.ds(0, width)], sems.at[0, i]),
            pltpu.make_async_copy(v_hbm, out_hbm.at[i, :, pl.ds(width, width)], sems.at[1, i]),
        ]
    for copy in copies:
        copy.start()
    for copy in copies:
        copy.wait()


def load_kernel(q_hbm, g_hbm, q_ref, g_ref, sems):
    copies = [
        pltpu.make_async_copy(q_hbm, q_ref, sems.at[0]),
        pltpu.make_async_copy(g_hbm, g_ref, sems.at[1]),
    ]
    for copy in copies:
        copy.start()
    for copy in copies:
        copy.wait()


def attention_kernel(
    lengths_ref,
    kv_ref,
    q_ref,
    g_ref,
    kw_hbm,
    vw_hbm,
    out_ref,
    kw_ref,
    vw_ref,
    probs_ref,
    dscores_ref,
    sems,
):
    weights = [
        pltpu.make_async_copy(kw_hbm, kw_ref, sems.at[0]),
        pltpu.make_async_copy(vw_hbm, vw_ref, sems.at[1]),
    ]
    for copy in weights:
        copy.start()
    scale = HD ** (-0.5)
    width = kv_ref.shape[1] // 2
    kv_local = width // HD
    parts = q_ref.shape[0] // LEN
    group = q_ref.shape[1] // HD // kv_local
    position = lax.broadcasted_iota(jnp.int32, (1, UNIT * LEN), 1) % LEN
    units = [
        (k, part, h)
        for k in range(kv_local)
        for part in range(parts)
        for h in range(0, group, UNIT)
    ]

    def stack(ref, unit):
        k, part, h = unit
        heads = [
            ref[part * LEN : (part + 1) * LEN, at * HD : (at + 1) * HD]
            for at in range(k * group + h, k * group + h + UNIT)
        ]
        return jnp.concatenate(heads, axis=0)

    def products(unit):
        k = unit[0]
        keys = kv_ref[:, k * HD : (k + 1) * HD]
        values = kv_ref[:, width + k * HD : width + (k + 1) * HD]
        return (
            lax.dot_general(keys, stack(q_ref, unit), NT, preferred_element_type=jnp.float32),
            lax.dot_general(values, stack(g_ref, unit), NT, preferred_element_type=jnp.float32),
        )

    following = products(units[0])
    for i, unit in enumerate(units):
        k, part, h = unit
        scores, dprobs = following
        if i + 1 < len(units):
            following = products(units[i + 1])
        top = jnp.max(scores, axis=0, keepdims=True)
        expo = jnp.exp2((scores - top) * (scale * LOG2E))
        total = jnp.sum(expo, axis=0, keepdims=True)
        weighted = jnp.sum(expo * dprobs, axis=0, keepdims=True)
        inverse = 1.0 / total
        delta = weighted * inverse
        factor = jnp.where(position < lengths_ref[part], inverse, 0.0)
        probs = expo * factor
        mine = [u for u in units if u[0] == k]
        cols = pl.ds(mine.index(unit) * UNIT * LEN, UNIT * LEN)
        probs_ref[k, :, cols] = probs.astype(jnp.bfloat16)
        dscores_ref[k, :, cols] = (probs * (dprobs - delta)).astype(jnp.bfloat16)
        if unit == mine[-1]:
            q_all = jnp.concatenate([stack(q_ref, u) for u in mine], axis=0)
            g_all = jnp.concatenate([stack(g_ref, u) for u in mine], axis=0)
            grad_k = jnp.dot(dscores_ref[k], q_all, preferred_element_type=jnp.float32) * scale
            grad_v = jnp.dot(probs_ref[k], g_all, preferred_element_type=jnp.float32)
            out_ref[:, k * HD : (k + 1) * HD] = grad_k.astype(out_ref.dtype)
            out_ref[:, width + k * HD : width + (k + 1) * HD] = grad_v.astype(out_ref.dtype)
    for copy in weights:
        copy.wait()


def project(low, kw_ref, vw_ref, owner, features):
    width = kw_ref.shape[1]
    rows = pl.ds(pl.multiple_of(owner * features, features), features)
    out = lax.dot_general(
        low[:, :width], kw_ref[rows, :], NT, preferred_element_type=jnp.float32
    )
    return out + lax.dot_general(
        low[:, width:], vw_ref[rows, :], NT, preferred_element_type=jnp.float32
    )


def first_projection_kernel(owner, parts_ref, kw_ref, vw_ref, low_ref, out_ref):
    total = parts_ref[0].astype(jnp.float32)
    for i in range(1, parts_ref.shape[0]):
        total += parts_ref[i].astype(jnp.float32)
    low = total.astype(jnp.bfloat16)
    low_ref[...] = low
    me = lax.axis_index("head")
    out = project(low, kw_ref, vw_ref, me ^ owner, out_ref.shape[1])
    out_ref[...] = out.astype(out_ref.dtype)


def second_projection_kernel(owner, low_ref, kw_ref, vw_ref, out_ref):
    me = lax.axis_index("head")
    out_ref[...] = project(low_ref[...], kw_ref, vw_ref, me ^ owner, out_ref.shape[1])


def last_projection_kernel(low_ref, kw_ref, vw_ref, after, out_ref, keep_ref, dk_ref, dv_ref):
    width = dk_ref.shape[1]
    low = low_ref[...]
    dk_ref[...] = low[:, :width]
    dv_ref[...] = low[:, width:]
    me = lax.axis_index("head")
    out = project(low, kw_ref, vw_ref, me ^ 1, out_ref.shape[1])
    out_ref[...] = out.astype(out_ref.dtype)
    keep_ref[...] = project(low, kw_ref, vw_ref, me, keep_ref.shape[1])


def swap(x, axis, count, bit):
    return lax.ppermute(x, axis, [(i, i ^ bit) for i in range(count)])


def body(resp, head, queries, d_out, prefix_keys, prefix_values, k_weight, v_weight, lengths):
    own, width = prefix_keys.shape
    features = k_weight.shape[0] // head
    vmem = pl.BlockSpec(memory_space=pltpu.VMEM)
    hbm = pl.BlockSpec(memory_space=pltpu.HBM)
    params = pltpu.CompilerParams(vmem_limit_bytes=VMEM_LIMIT)

    def in_hbm(*xs):
        return [pltpu.with_memory_space_constraint(x, pltpu.HBM) for x in xs]

    both = pl.pallas_call(
        join_kernel,
        out_shape=jax.ShapeDtypeStruct((resp, own, 2 * width), jnp.bfloat16),
        in_specs=[hbm] * 2,
        out_specs=hbm,
        scratch_shapes=[pltpu.SemaphoreType.DMA((2, resp))],
        compiler_params=params,
        name="join",
    )(*in_hbm(prefix_keys, prefix_values))
    both = lax.all_to_all(both, "resp", 0, 0, tiled=True).reshape(resp * own, 2 * width)

    queries, d_out = pl.pallas_call(
        load_kernel,
        out_shape=[pltpu.VMEM(x.shape, x.dtype) for x in (queries, d_out)],
        in_specs=[hbm] * 2,
        out_specs=[vmem] * 2,
        scratch_shapes=[pltpu.SemaphoreType.DMA((2,))],
        compiler_params=params,
        cost_estimate=pl.CostEstimate(
            flops=0, transcendentals=0, bytes_accessed=4 * queries.size * 2
        ),
        name="load",
    )(*in_hbm(queries, d_out))

    tokens = resp * own
    kv_local = width // HD
    depth = queries.size // kv_local // HD
    partial, k_weight, v_weight = pl.pallas_call(
        attention_kernel,
        out_shape=[
            pltpu.VMEM((tokens, 2 * width), jnp.bfloat16),
            pltpu.VMEM(k_weight.shape, k_weight.dtype),
            pltpu.VMEM(v_weight.shape, v_weight.dtype),
        ],
        in_specs=[pl.BlockSpec(memory_space=pltpu.SMEM)] + [vmem] * 3 + [hbm] * 2,
        out_specs=[vmem] * 3,
        scratch_shapes=[
            pltpu.VMEM((kv_local, tokens, depth), jnp.bfloat16),
            pltpu.VMEM((kv_local, tokens, depth), jnp.bfloat16),
            pltpu.SemaphoreType.DMA((2,)),
        ],
        compiler_params=params,
        name="attention",
    )(lengths, both, queries, d_out, *in_hbm(k_weight, v_weight))

    shares = lax.all_to_all(
        partial.reshape(resp, own, 2 * width), "resp", 0, 0, tiled=True
    )

    block = (own, features)
    low, to_core = pl.pallas_call(
        functools.partial(first_projection_kernel, 3),
        out_shape=[
            pltpu.VMEM((own, 2 * width), jnp.bfloat16),
            pltpu.VMEM(block, jnp.bfloat16),
        ],
        in_specs=[vmem] * 3,
        out_specs=[vmem] * 2,
        compiler_params=params,
        name="projection_other_core",
    )(shares, k_weight, v_weight)
    cost = pl.CostEstimate(
        flops=4 * own * width * features, transcendentals=0, bytes_accessed=4 * width * features
    )
    far = pl.pallas_call(
        functools.partial(second_projection_kernel, 2),
        out_shape=pltpu.VMEM(block, jnp.float32),
        in_specs=[vmem] * 3,
        out_specs=vmem,
        compiler_params=params,
        cost_estimate=cost,
        name="projection_other_y",
    )(low, k_weight, v_weight)
    far = (far + swap(to_core, "head", head, 1).astype(jnp.float32)).astype(jnp.bfloat16)
    got = swap(far, "head", head, 2)
    to_core, total, dk_low, dv_low = pl.pallas_call(
        last_projection_kernel,
        out_shape=[
            pltpu.VMEM(block, jnp.bfloat16),
            pltpu.VMEM(block, jnp.float32),
            jax.ShapeDtypeStruct((own, width), jnp.bfloat16),
            jax.ShapeDtypeStruct((own, width), jnp.bfloat16),
        ],
        in_specs=[vmem] * 3 + [pl.BlockSpec(memory_space=pl.ANY)],
        out_specs=[vmem] * 4,
        compiler_params=params,
        cost_estimate=cost,
        name="projection_this_y",
    )(low, k_weight, v_weight, far)
    total = lax.optimization_barrier(total + got.astype(jnp.float32))
    total += swap(to_core, "head", head, 1).astype(jnp.float32)
    return dk_low, dv_low, total.astype(jnp.bfloat16)


def solution(mesh):
    placed = (
        P("resp", "head"),
        P("resp", "head"),
        P("resp", "head"),
        P("resp", "head"),
        P(None, "head"),
        P(None, "head"),
        P("resp"),
    )
    return jax.shard_map(
        functools.partial(body, mesh.shape["resp"], mesh.shape["head"]),
        mesh=mesh,
        in_specs=placed,
        out_specs=(P("resp", "head"), P("resp", "head"), P("resp", "head")),
        check_vma=False,
    )
```

```python
import functools

import jax
import jax.numpy as jnp
from jax import lax
from jax.experimental import pallas as pl
from jax.experimental.pallas import tpu as pltpu
from jax.sharding import PartitionSpec as P

HD = 128
LEN = 256
NT = (((1,), (1,)), ((), ()))
VMEM_LIMIT = 40 << 20
UNIT = 2
LOG2E = 1.4426950408889634


def join_kernel(k_hbm, v_hbm, out_ref, both_ref, sems):
    width = k_hbm.shape[1]
    copies = [
        pltpu.make_async_copy(k_hbm, both_ref.at[:, pl.ds(0, width)], sems.at[0]),
        pltpu.make_async_copy(v_hbm, both_ref.at[:, pl.ds(width, width)], sems.at[1]),
    ]
    for copy in copies:
        copy.start()
    for copy in copies:
        copy.wait()
    both = both_ref[...]
    for i in range(out_ref.shape[0]):
        out_ref[i] = both


def load_kernel(lengths_ref, *refs):
    count = (len(refs) - 2) // 2
    live_ref, sems = refs[2 * count :]
    copies = [
        pltpu.make_async_copy(refs[i], refs[count + i], sems.at[i]) for i in range(count)
    ]
    for copy in copies:
        copy.start()
    position = lax.broadcasted_iota(jnp.int32, live_ref.shape[1:], 1)
    for part in range(live_ref.shape[0]):
        live_ref[part] = jnp.where(position < lengths_ref[part], 1.0, 0.0)
    for copy in copies:
        copy.wait()


def attention_kernel(
    live_ref, kv_ref, q_ref, g_ref, vw_hbm, out_ref, vw_ref, probs_ref, dscores_ref, sem
):
    weight = pltpu.make_async_copy(vw_hbm, vw_ref, sem)
    weight.start()
    scale = HD ** (-0.5)
    width = kv_ref.shape[1] // 2
    kv_local = width // HD
    parts = q_ref.shape[0] // LEN
    group = q_ref.shape[1] // HD // kv_local
    units = [
        (k, part, h)
        for k in range(kv_local)
        for part in range(parts)
        for h in range(0, group, UNIT)
    ]

    def stack(ref, unit):
        k, part, h = unit
        heads = [
            ref[part * LEN : (part + 1) * LEN, at * HD : (at + 1) * HD]
            for at in range(k * group + h, k * group + h + UNIT)
        ]
        return jnp.concatenate(heads, axis=0)

    def products(unit):
        k = unit[0]
        keys = kv_ref[:, k * HD : (k + 1) * HD]
        values = kv_ref[:, width + k * HD : width + (k + 1) * HD]
        return (
            lax.dot_general(keys, stack(q_ref, unit), NT, preferred_element_type=jnp.float32),
            lax.dot_general(values, stack(g_ref, unit), NT, preferred_element_type=jnp.float32),
        )

    following = products(units[0])
    for i, unit in enumerate(units):
        k, part, h = unit
        scores, dprobs = following
        if i + 1 < len(units):
            following = products(units[i + 1])
        top = jnp.max(scores, axis=0, keepdims=True)
        expo = jnp.exp2((scores - top) * (scale * LOG2E))
        total = jnp.sum(expo, axis=0, keepdims=True)
        weighted = jnp.sum(expo * dprobs, axis=0, keepdims=True)
        inverse = 1.0 / total
        delta = weighted * inverse
        factor = inverse * jnp.concatenate([live_ref[part, :1]] * UNIT, axis=1)
        probs = expo * factor
        mine = [u for u in units if u[0] == k]
        cols = pl.ds(mine.index(unit) * UNIT * LEN, UNIT * LEN)
        probs_ref[k, :, cols] = probs.astype(jnp.bfloat16)
        dscores_ref[k, :, cols] = (probs * (dprobs - delta)).astype(jnp.bfloat16)
        if unit == mine[-1]:
            q_all = jnp.concatenate([stack(q_ref, u) for u in mine], axis=0)
            g_all = jnp.concatenate([stack(g_ref, u) for u in mine], axis=0)
            grad_k = jnp.dot(dscores_ref[k], q_all, preferred_element_type=jnp.float32) * scale
            grad_v = jnp.dot(probs_ref[k], g_all, preferred_element_type=jnp.float32)
            out_ref[:, k * HD : (k + 1) * HD] = grad_k.astype(out_ref.dtype)
            out_ref[:, width + k * HD : width + (k + 1) * HD] = grad_v.astype(out_ref.dtype)
    weight.wait()


def project(low, kw_ref, vw_ref, owner, features):
    width = kw_ref.shape[1]
    rows = pl.ds(pl.multiple_of(owner * features, features), features)
    out = lax.dot_general(
        low[:, :width], kw_ref[rows, :], NT, preferred_element_type=jnp.float32
    )
    return out + lax.dot_general(
        low[:, width:], vw_ref[rows, :], NT, preferred_element_type=jnp.float32
    )


def first_projection_kernel(owner, parts_ref, kw_ref, vw_ref, low_ref, out_ref):
    total = parts_ref[0].astype(jnp.float32)
    for i in range(1, parts_ref.shape[0]):
        total += parts_ref[i].astype(jnp.float32)
    low = total.astype(jnp.bfloat16)
    low_ref[...] = low
    me = lax.axis_index("head")
    out = project(low, kw_ref, vw_ref, me ^ owner, out_ref.shape[1])
    out_ref[...] = out.astype(out_ref.dtype)


def second_projection_kernel(owner, low_ref, kw_ref, vw_ref, out_ref):
    me = lax.axis_index("head")
    out_ref[...] = project(low_ref[...], kw_ref, vw_ref, me ^ owner, out_ref.shape[1])


def last_projection_kernel(low_ref, kw_ref, vw_ref, after, out_ref, keep_ref, dk_ref, dv_ref):
    width = dk_ref.shape[1]
    low = low_ref[...]
    dk_ref[...] = low[:, :width]
    dv_ref[...] = low[:, width:]
    me = lax.axis_index("head")
    out = project(low, kw_ref, vw_ref, me ^ 1, out_ref.shape[1])
    out_ref[...] = out.astype(out_ref.dtype)
    keep_ref[...] = project(low, kw_ref, vw_ref, me, keep_ref.shape[1])


def swap(x, axis, count, bit):
    return lax.ppermute(x, axis, [(i, i ^ bit) for i in range(count)])


def body(resp, head, queries, d_out, prefix_keys, prefix_values, k_weight, v_weight, lengths):
    own, width = prefix_keys.shape
    features = k_weight.shape[0] // head
    vmem = pl.BlockSpec(memory_space=pltpu.VMEM)
    hbm = pl.BlockSpec(memory_space=pltpu.HBM)
    params = pltpu.CompilerParams(vmem_limit_bytes=VMEM_LIMIT)

    def in_hbm(*xs):
        return [pltpu.with_memory_space_constraint(x, pltpu.HBM) for x in xs]

    both = pl.pallas_call(
        join_kernel,
        out_shape=jax.ShapeDtypeStruct((resp, own, 2 * width), jnp.bfloat16),
        in_specs=[hbm] * 2,
        out_specs=vmem,
        scratch_shapes=[
            pltpu.VMEM((own, 2 * width), jnp.bfloat16),
            pltpu.SemaphoreType.DMA((2,)),
        ],
        compiler_params=params,
        name="join",
    )(*in_hbm(prefix_keys, prefix_values))
    both = lax.all_to_all(both, "resp", 0, 0, tiled=True).reshape(resp * own, 2 * width)

    large = (queries, d_out, k_weight)
    responses = lengths.shape[0]
    queries, d_out, k_weight, live = pl.pallas_call(
        load_kernel,
        out_shape=[pltpu.VMEM(x.shape, x.dtype) for x in large]
        + [pltpu.VMEM((responses, 8, LEN), jnp.float32)],
        in_specs=[pl.BlockSpec(memory_space=pltpu.SMEM)] + [hbm] * len(large),
        out_specs=[vmem] * (len(large) + 1),
        scratch_shapes=[pltpu.SemaphoreType.DMA((len(large),))],
        compiler_params=params,
        cost_estimate=pl.CostEstimate(
            flops=0, transcendentals=0, bytes_accessed=sum(4 * x.size for x in large)
        ),
        name="load",
    )(lengths, *in_hbm(*large))

    tokens = resp * own
    kv_local = width // HD
    depth = queries.size // kv_local // HD
    partial, v_weight = pl.pallas_call(
        attention_kernel,
        out_shape=[
            pltpu.VMEM((tokens, 2 * width), jnp.bfloat16),
            pltpu.VMEM(v_weight.shape, v_weight.dtype),
        ],
        in_specs=[vmem] * 4 + [hbm],
        out_specs=[vmem] * 2,
        scratch_shapes=[
            pltpu.VMEM((kv_local, tokens, depth), jnp.bfloat16),
            pltpu.VMEM((kv_local, tokens, depth), jnp.bfloat16),
            pltpu.SemaphoreType.DMA,
        ],
        compiler_params=params,
        name="attention",
    )(live, both, queries, d_out, *in_hbm(v_weight))

    shares = lax.all_to_all(
        partial.reshape(resp, own, 2 * width), "resp", 0, 0, tiled=True
    )

    block = (own, features)
    low, to_core = pl.pallas_call(
        functools.partial(first_projection_kernel, 3),
        out_shape=[
            pltpu.VMEM((own, 2 * width), jnp.bfloat16),
            pltpu.VMEM(block, jnp.bfloat16),
        ],
        in_specs=[vmem] * 3,
        out_specs=[vmem] * 2,
        compiler_params=params,
        name="projection_other_core",
    )(shares, k_weight, v_weight)
    cost = pl.CostEstimate(
        flops=4 * own * width * features, transcendentals=0, bytes_accessed=4 * width * features
    )
    far = pl.pallas_call(
        functools.partial(second_projection_kernel, 2),
        out_shape=pltpu.VMEM(block, jnp.float32),
        in_specs=[vmem] * 3,
        out_specs=vmem,
        compiler_params=params,
        cost_estimate=cost,
        name="projection_other_y",
    )(low, k_weight, v_weight)
    far = (far + swap(to_core, "head", head, 1).astype(jnp.float32)).astype(jnp.bfloat16)
    got = swap(far, "head", head, 2)
    to_core, total, dk_low, dv_low = pl.pallas_call(
        last_projection_kernel,
        out_shape=[
            pltpu.VMEM(block, jnp.bfloat16),
            pltpu.VMEM(block, jnp.float32),
            jax.ShapeDtypeStruct((own, width), jnp.bfloat16),
            jax.ShapeDtypeStruct((own, width), jnp.bfloat16),
        ],
        in_specs=[vmem] * 3 + [pl.BlockSpec(memory_space=pl.ANY)],
        out_specs=[vmem] * 4,
        compiler_params=params,
        cost_estimate=cost,
        name="projection_this_y",
    )(low, k_weight, v_weight, far)
    total = lax.optimization_barrier(total + got.astype(jnp.float32))
    total += swap(to_core, "head", head, 1).astype(jnp.float32)
    return dk_low, dv_low, total.astype(jnp.bfloat16)


def solution(mesh):
    placed = (
        P("resp", "head"),
        P("resp", "head"),
        P("resp", "head"),
        P("resp", "head"),
        P(None, "head"),
        P(None, "head"),
        P("resp"),
    )
    return jax.shard_map(
        functools.partial(body, mesh.shape["resp"], mesh.shape["head"]),
        mesh=mesh,
        in_specs=placed,
        out_specs=(P("resp", "head"), P("resp", "head"), P("resp", "head")),
        check_vma=False,
    )
```

```python
import functools

import jax
import jax.numpy as jnp
from jax import lax
from jax.experimental import pallas as pl
from jax.experimental.pallas import tpu as pltpu
from jax.sharding import PartitionSpec as P

HD = 128
LEN = 256
NT = (((1,), (1,)), ((), ()))
UNIT = 2
LOG2E = 1.4426950408889634


def join_kernel(k_hbm, v_hbm, out_ref, both_ref, sems):
    width = k_hbm.shape[1]
    copies = [
        pltpu.make_async_copy(k_hbm, both_ref.at[:, pl.ds(0, width)], sems.at[0]),
        pltpu.make_async_copy(v_hbm, both_ref.at[:, pl.ds(width, width)], sems.at[1]),
    ]
    for copy in copies:
        copy.start()
    for copy in copies:
        copy.wait()
    both = both_ref[...]
    for i in range(out_ref.shape[0]):
        out_ref[i] = both


def load_kernel(lengths_ref, *refs):
    count = (len(refs) - 2) // 2
    live_ref, sems = refs[2 * count :]
    copies = [
        pltpu.make_async_copy(refs[i], refs[count + i], sems.at[i]) for i in range(count)
    ]
    for copy in copies:
        copy.start()
    position = lax.broadcasted_iota(jnp.int32, live_ref.shape[1:], 1)
    for part in range(live_ref.shape[0]):
        live_ref[part] = jnp.where(position < lengths_ref[part], 1.0, 0.0)
    for copy in copies:
        copy.wait()


def attention_kernel(
    live_ref,
    kv_ref,
    q_ref,
    g_ref,
    kw_ref,
    vw_hbm,
    out_ref,
    vw_ref,
    probs_ref,
    dscores_ref,
    sem,
):
    del kw_ref
    weight = pltpu.make_async_copy(vw_hbm, vw_ref, sem)
    weight.start()
    scale = HD ** (-0.5)
    width = kv_ref.shape[1] // 2
    kv_local = width // HD
    parts = q_ref.shape[0] // LEN
    group = q_ref.shape[1] // HD // kv_local
    units = [
        (k, part, h)
        for k in range(kv_local)
        for part in range(parts)
        for h in range(0, group, UNIT)
    ]

    def stack(ref, unit):
        k, part, h = unit
        heads = [
            ref[part * LEN : (part + 1) * LEN, at * HD : (at + 1) * HD]
            for at in range(k * group + h, k * group + h + UNIT)
        ]
        return jnp.concatenate(heads, axis=0)

    def products(unit):
        k = unit[0]
        keys = kv_ref[:, k * HD : (k + 1) * HD]
        values = kv_ref[:, width + k * HD : width + (k + 1) * HD]
        return (
            lax.dot_general(keys, stack(q_ref, unit), NT, preferred_element_type=jnp.float32),
            lax.dot_general(values, stack(g_ref, unit), NT, preferred_element_type=jnp.float32),
        )

    following = products(units[0])
    for i, unit in enumerate(units):
        k, part, h = unit
        scores, dprobs = following
        if i + 1 < len(units):
            following = products(units[i + 1])
        top = jnp.max(scores, axis=0, keepdims=True)
        expo = jnp.exp2((scores - top) * (scale * LOG2E))
        total = jnp.sum(expo, axis=0, keepdims=True)
        weighted = jnp.sum(expo * dprobs, axis=0, keepdims=True)
        inverse = 1.0 / total
        delta = weighted * inverse
        factor = inverse * jnp.concatenate([live_ref[part, :1]] * UNIT, axis=1)
        probs = expo * factor
        mine = [u for u in units if u[0] == k]
        cols = pl.ds(mine.index(unit) * UNIT * LEN, UNIT * LEN)
        probs_ref[k, :, cols] = probs.astype(jnp.bfloat16)
        dscores_ref[k, :, cols] = (probs * (dprobs - delta)).astype(jnp.bfloat16)
        if unit == mine[-1]:
            q_all = jnp.concatenate([stack(q_ref, u) for u in mine], axis=0)
            g_all = jnp.concatenate([stack(g_ref, u) for u in mine], axis=0)
            grad_k = jnp.dot(dscores_ref[k], q_all, preferred_element_type=jnp.float32) * scale
            grad_v = jnp.dot(probs_ref[k], g_all, preferred_element_type=jnp.float32)
            out_ref[:, k * HD : (k + 1) * HD] = grad_k.astype(out_ref.dtype)
            out_ref[:, width + k * HD : width + (k + 1) * HD] = grad_v.astype(out_ref.dtype)
    weight.wait()


def project(low, kw_ref, vw_ref, owner, features):
    width = kw_ref.shape[1]
    rows = pl.ds(pl.multiple_of(owner * features, features), features)
    out = lax.dot_general(
        low[:, :width], kw_ref[rows, :], NT, preferred_element_type=jnp.float32
    )
    return out + lax.dot_general(
        low[:, width:], vw_ref[rows, :], NT, preferred_element_type=jnp.float32
    )


def first_projection_kernel(owner, parts_ref, kw_ref, vw_ref, low_ref, out_ref):
    total = parts_ref[0].astype(jnp.float32)
    for i in range(1, parts_ref.shape[0]):
        total += parts_ref[i].astype(jnp.float32)
    low = total.astype(jnp.bfloat16)
    low_ref[...] = low
    me = lax.axis_index("head")
    out = project(low, kw_ref, vw_ref, me ^ owner, out_ref.shape[1])
    out_ref[...] = out.astype(out_ref.dtype)


def second_projection_kernel(owner, low_ref, kw_ref, vw_ref, out_ref):
    me = lax.axis_index("head")
    out_ref[...] = project(low_ref[...], kw_ref, vw_ref, me ^ owner, out_ref.shape[1])


def last_projection_kernel(low_ref, kw_ref, vw_ref, after, out_ref, keep_ref, dk_ref, dv_ref):
    width = dk_ref.shape[1]
    low = low_ref[...]
    dk_ref[...] = low[:, :width]
    dv_ref[...] = low[:, width:]
    me = lax.axis_index("head")
    out = project(low, kw_ref, vw_ref, me ^ 1, out_ref.shape[1])
    out_ref[...] = out.astype(out_ref.dtype)
    keep_ref[...] = project(low, kw_ref, vw_ref, me, keep_ref.shape[1])


def swap(x, axis, count, bit):
    return lax.ppermute(x, axis, [(i, i ^ bit) for i in range(count)])


def body(resp, head, queries, d_out, prefix_keys, prefix_values, k_weight, v_weight, lengths):
    own, width = prefix_keys.shape
    features = k_weight.shape[0] // head
    vmem = pl.BlockSpec(memory_space=pltpu.VMEM)
    hbm = pl.BlockSpec(memory_space=pltpu.HBM)
    params = pltpu.CompilerParams(vmem_limit_bytes=8 << 20)

    def in_hbm(*xs):
        return [pltpu.with_memory_space_constraint(x, pltpu.HBM) for x in xs]

    both = pl.pallas_call(
        join_kernel,
        out_shape=jax.ShapeDtypeStruct((resp, own, 2 * width), jnp.bfloat16),
        in_specs=[hbm] * 2,
        out_specs=vmem,
        scratch_shapes=[
            pltpu.VMEM((own, 2 * width), jnp.bfloat16),
            pltpu.SemaphoreType.DMA((2,)),
        ],
        compiler_params=params,
        name="join",
    )(*in_hbm(prefix_keys, prefix_values))
    both = lax.all_to_all(both, "resp", 0, 0, tiled=True).reshape(resp * own, 2 * width)

    large = (queries, d_out, k_weight)
    responses = lengths.shape[0]
    queries, d_out, k_weight, live = pl.pallas_call(
        load_kernel,
        out_shape=[pltpu.VMEM(x.shape, x.dtype) for x in large]
        + [pltpu.VMEM((responses, 8, LEN), jnp.float32)],
        in_specs=[pl.BlockSpec(memory_space=pltpu.SMEM)] + [hbm] * len(large),
        out_specs=[vmem] * (len(large) + 1),
        scratch_shapes=[pltpu.SemaphoreType.DMA((len(large),))],
        compiler_params=params,
        cost_estimate=pl.CostEstimate(
            flops=0, transcendentals=0, bytes_accessed=sum(4 * x.size for x in large)
        ),
        name="load",
    )(lengths, *in_hbm(*large))

    tokens = resp * own
    kv_local = width // HD
    depth = queries.size // kv_local // HD
    partial, v_weight = pl.pallas_call(
        attention_kernel,
        out_shape=[
            pltpu.VMEM((tokens, 2 * width), jnp.bfloat16),
            pltpu.VMEM(v_weight.shape, v_weight.dtype),
        ],
        in_specs=[vmem] * 5 + [hbm],
        out_specs=[vmem] * 2,
        scratch_shapes=[
            pltpu.VMEM((kv_local, tokens, depth), jnp.bfloat16),
            pltpu.VMEM((kv_local, tokens, depth), jnp.bfloat16),
            pltpu.SemaphoreType.DMA,
        ],
        compiler_params=pltpu.CompilerParams(
            vmem_limit_bytes=(8 << 20) + 8 * kv_local * tokens * depth
        ),
        name="attention",
    )(live, both, queries, d_out, k_weight, *in_hbm(v_weight))

    shares = lax.all_to_all(
        partial.reshape(resp, own, 2 * width), "resp", 0, 0, tiled=True
    )

    block = (own, features)
    low, to_core = pl.pallas_call(
        functools.partial(first_projection_kernel, 3),
        out_shape=[
            pltpu.VMEM((own, 2 * width), jnp.bfloat16),
            pltpu.VMEM(block, jnp.bfloat16),
        ],
        in_specs=[vmem] * 3,
        out_specs=[vmem] * 2,
        compiler_params=params,
        name="projection_other_core",
    )(shares, k_weight, v_weight)
    cost = pl.CostEstimate(
        flops=4 * own * width * features, transcendentals=0, bytes_accessed=4 * width * features
    )
    far = pl.pallas_call(
        functools.partial(second_projection_kernel, 2),
        out_shape=pltpu.VMEM(block, jnp.float32),
        in_specs=[vmem] * 3,
        out_specs=vmem,
        compiler_params=params,
        cost_estimate=cost,
        name="projection_other_y",
    )(low, k_weight, v_weight)
    far = (far + swap(to_core, "head", head, 1).astype(jnp.float32)).astype(jnp.bfloat16)
    got = swap(far, "head", head, 2)
    to_core, total, dk_low, dv_low = pl.pallas_call(
        last_projection_kernel,
        out_shape=[
            pltpu.VMEM(block, jnp.bfloat16),
            pltpu.VMEM(block, jnp.float32),
            jax.ShapeDtypeStruct((own, width), jnp.bfloat16),
            jax.ShapeDtypeStruct((own, width), jnp.bfloat16),
        ],
        in_specs=[vmem] * 3 + [pl.BlockSpec(memory_space=pl.ANY)],
        out_specs=[vmem] * 4,
        compiler_params=params,
        cost_estimate=cost,
        name="projection_this_y",
    )(low, k_weight, v_weight, far)
    total = lax.optimization_barrier(total + got.astype(jnp.float32))
    total += swap(to_core, "head", head, 1).astype(jnp.float32)
    return dk_low, dv_low, total.astype(jnp.bfloat16)


def solution(mesh):
    placed = (
        P("resp", "head"),
        P("resp", "head"),
        P("resp", "head"),
        P("resp", "head"),
        P(None, "head"),
        P(None, "head"),
        P("resp"),
    )
    return jax.shard_map(
        functools.partial(body, mesh.shape["resp"], mesh.shape["head"]),
        mesh=mesh,
        in_specs=placed,
        out_specs=(P("resp", "head"), P("resp", "head"), P("resp", "head")),
        check_vma=False,
    )
```

```python
import functools

import jax
import jax.numpy as jnp
from jax import lax
from jax.experimental import pallas as pl
from jax.experimental.pallas import tpu as pltpu
from jax.sharding import PartitionSpec as P

HD = 128
LEN = 256
NT = (((1,), (1,)), ((), ()))
UNIT = 2
LOG2E = 1.4426950408889634


def join_kernel(k_hbm, v_hbm, out_ref, both_ref, sems):
    width = k_hbm.shape[1]
    copies = [
        pltpu.make_async_copy(k_hbm, both_ref.at[:, pl.ds(0, width)], sems.at[0]),
        pltpu.make_async_copy(v_hbm, both_ref.at[:, pl.ds(width, width)], sems.at[1]),
    ]
    for copy in copies:
        copy.start()
    for copy in copies:
        copy.wait()
    both = both_ref[...]
    for i in range(out_ref.shape[0]):
        out_ref[i] = both


def load_kernel(lengths_ref, *refs):
    count = (len(refs) - 2) // 2
    live_ref, sems = refs[2 * count :]
    copies = [
        pltpu.make_async_copy(refs[i], refs[count + i], sems.at[i]) for i in range(count)
    ]
    for copy in copies:
        copy.start()
    position = lax.broadcasted_iota(jnp.int32, live_ref.shape[1:], 1)
    for part in range(live_ref.shape[0]):
        live_ref[part] = jnp.where(position < lengths_ref[part], 1.0, 0.0)
    for copy in copies:
        copy.wait()


def features_of(head_index, features):
    return pl.ds(pl.multiple_of(head_index * features, features), features)


def attention_kernel(
    live_ref,
    kv_ref,
    q_ref,
    g_ref,
    kw_hbm,
    vw_hbm,
    out_ref,
    kw_ref,
    vw_ref,
    probs_ref,
    dscores_ref,
    sems,
):
    rows = features_of((lax.axis_index("head") // 2) ^ 1, kw_ref.shape[0])
    weights = [
        pltpu.make_async_copy(kw_hbm.at[rows], kw_ref, sems.at[0]),
        pltpu.make_async_copy(vw_hbm.at[rows], vw_ref, sems.at[1]),
    ]
    for copy in weights:
        copy.start()
    scale = HD ** (-0.5)
    width = kv_ref.shape[1] // 2
    kv_local = width // HD
    parts = q_ref.shape[0] // LEN
    group = q_ref.shape[1] // HD // kv_local
    units = [
        (k, part, h)
        for k in range(kv_local)
        for part in range(parts)
        for h in range(0, group, UNIT)
    ]

    def stack(ref, unit):
        k, part, h = unit
        heads = [
            ref[part * LEN : (part + 1) * LEN, at * HD : (at + 1) * HD]
            for at in range(k * group + h, k * group + h + UNIT)
        ]
        return jnp.concatenate(heads, axis=0)

    def products(unit):
        k = unit[0]
        keys = kv_ref[:, k * HD : (k + 1) * HD]
        values = kv_ref[:, width + k * HD : width + (k + 1) * HD]
        return (
            lax.dot_general(keys, stack(q_ref, unit), NT, preferred_element_type=jnp.float32),
            lax.dot_general(values, stack(g_ref, unit), NT, preferred_element_type=jnp.float32),
        )

    following = products(units[0])
    for i, unit in enumerate(units):
        k, part, h = unit
        scores, dprobs = following
        if i + 1 < len(units):
            following = products(units[i + 1])
        top = jnp.max(scores, axis=0, keepdims=True)
        expo = jnp.exp2((scores - top) * (scale * LOG2E))
        total = jnp.sum(expo, axis=0, keepdims=True)
        weighted = jnp.sum(expo * dprobs, axis=0, keepdims=True)
        inverse = 1.0 / total
        delta = weighted * inverse
        factor = inverse * jnp.concatenate([live_ref[part, :1]] * UNIT, axis=1)
        probs = expo * factor
        mine = [u for u in units if u[0] == k]
        cols = pl.ds(mine.index(unit) * UNIT * LEN, UNIT * LEN)
        probs_ref[k, :, cols] = probs.astype(jnp.bfloat16)
        dscores_ref[k, :, cols] = (probs * (dprobs - delta)).astype(jnp.bfloat16)
        if unit == mine[-1]:
            q_all = jnp.concatenate([stack(q_ref, u) for u in mine], axis=0)
            g_all = jnp.concatenate([stack(g_ref, u) for u in mine], axis=0)
            grad_k = jnp.dot(dscores_ref[k], q_all, preferred_element_type=jnp.float32) * scale
            grad_v = jnp.dot(probs_ref[k], g_all, preferred_element_type=jnp.float32)
            out_ref[:, k * HD : (k + 1) * HD] = grad_k.astype(out_ref.dtype)
            out_ref[:, width + k * HD : width + (k + 1) * HD] = grad_v.astype(out_ref.dtype)
    for copy in weights:
        copy.wait()


def project(low, kw, vw):
    width = kw.shape[1]
    out = lax.dot_general(low[:, :width], kw, NT, preferred_element_type=jnp.float32)
    return out + lax.dot_general(low[:, width:], vw, NT, preferred_element_type=jnp.float32)


def first_projection_kernel(parts_ref, kw_ref, vw_ref, low_ref, out_ref):
    total = parts_ref[0].astype(jnp.float32)
    for i in range(1, parts_ref.shape[0]):
        total += parts_ref[i].astype(jnp.float32)
    low = total.astype(jnp.bfloat16)
    low_ref[...] = low
    rows = features_of((lax.axis_index("head") % 2) ^ 1, out_ref.shape[1])
    out_ref[...] = project(low, kw_ref[rows, :], vw_ref[rows, :]).astype(out_ref.dtype)


def second_projection_kernel(low_ref, kw_ref, vw_ref, out_ref):
    rows = features_of(lax.axis_index("head") % 2, out_ref.shape[1])
    out_ref[...] = project(low_ref[...], kw_ref[rows, :], vw_ref[rows, :])


def last_projection_kernel(
    low_ref, kw_hbm, vw_hbm, after, out_ref, keep_ref, dk_ref, dv_ref, weight_ref, sems
):
    del after
    features = out_ref.shape[1]
    me = lax.axis_index("head")
    copies = []
    for i in range(2):
        rows = features_of(me ^ (1 - i), features)
        for j, hbm in enumerate((kw_hbm, vw_hbm)):
            copies.append(
                pltpu.make_async_copy(hbm.at[rows], weight_ref.at[i, j], sems.at[i, j])
            )
    for copy in copies:
        copy.start()
    width = dk_ref.shape[1]
    low = low_ref[...]
    dk_ref[...] = low[:, :width]
    dv_ref[...] = low[:, width:]
    for i, ref in enumerate((out_ref, keep_ref)):
        copies[2 * i].wait()
        copies[2 * i + 1].wait()
        ref[...] = project(low, weight_ref[i, 0], weight_ref[i, 1]).astype(ref.dtype)


def swap(x, axis, count, bit):
    return lax.ppermute(x, axis, [(i, i ^ bit) for i in range(count)])


def body(resp, head, queries, d_out, prefix_keys, prefix_values, k_weight, v_weight, lengths):
    own, width = prefix_keys.shape
    features = k_weight.shape[0] // head
    vmem = pl.BlockSpec(memory_space=pltpu.VMEM)
    hbm = pl.BlockSpec(memory_space=pltpu.HBM)
    params = pltpu.CompilerParams(vmem_limit_bytes=8 << 20)

    def in_hbm(*xs):
        return [pltpu.with_memory_space_constraint(x, pltpu.HBM) for x in xs]

    both = pl.pallas_call(
        join_kernel,
        out_shape=jax.ShapeDtypeStruct((resp, own, 2 * width), jnp.bfloat16),
        in_specs=[hbm] * 2,
        out_specs=vmem,
        scratch_shapes=[
            pltpu.VMEM((own, 2 * width), jnp.bfloat16),
            pltpu.SemaphoreType.DMA((2,)),
        ],
        compiler_params=params,
        name="join",
    )(*in_hbm(prefix_keys, prefix_values))
    both = lax.all_to_all(both, "resp", 0, 0, tiled=True).reshape(resp * own, 2 * width)

    large = (queries, d_out)
    responses = lengths.shape[0]
    queries, d_out, live = pl.pallas_call(
        load_kernel,
        out_shape=[pltpu.VMEM(x.shape, x.dtype) for x in large]
        + [pltpu.VMEM((responses, 8, LEN), jnp.float32)],
        in_specs=[pl.BlockSpec(memory_space=pltpu.SMEM)] + [hbm] * len(large),
        out_specs=[vmem] * (len(large) + 1),
        scratch_shapes=[pltpu.SemaphoreType.DMA((len(large),))],
        compiler_params=params,
        cost_estimate=pl.CostEstimate(
            flops=0, transcendentals=0, bytes_accessed=sum(4 * x.size for x in large)
        ),
        name="load",
    )(lengths, *in_hbm(*large))

    tokens = resp * own
    kv_local = width // HD
    depth = queries.size // kv_local // HD
    weights = in_hbm(k_weight, v_weight)
    partial, far_k, far_v = pl.pallas_call(
        attention_kernel,
        out_shape=[
            pltpu.VMEM((tokens, 2 * width), jnp.bfloat16),
            pltpu.VMEM((2 * features, width), k_weight.dtype),
            pltpu.VMEM((2 * features, width), v_weight.dtype),
        ],
        in_specs=[vmem] * 4 + [hbm] * 2,
        out_specs=[vmem] * 3,
        scratch_shapes=[
            pltpu.VMEM((kv_local, tokens, depth), jnp.bfloat16),
            pltpu.VMEM((kv_local, tokens, depth), jnp.bfloat16),
            pltpu.SemaphoreType.DMA((2,)),
        ],
        compiler_params=pltpu.CompilerParams(
            vmem_limit_bytes=(8 << 20) + 8 * kv_local * tokens * depth
        ),
        name="attention",
    )(live, both, queries, d_out, *weights)

    shares = lax.all_to_all(
        partial.reshape(resp, own, 2 * width), "resp", 0, 0, tiled=True
    )

    block = (own, features)
    low, to_core = pl.pallas_call(
        first_projection_kernel,
        out_shape=[
            pltpu.VMEM((own, 2 * width), jnp.bfloat16),
            pltpu.VMEM(block, jnp.bfloat16),
        ],
        in_specs=[vmem] * 3,
        out_specs=[vmem] * 2,
        compiler_params=params,
        name="projection_other_core",
    )(shares, far_k, far_v)
    cost = pl.CostEstimate(
        flops=4 * own * width * features, transcendentals=0, bytes_accessed=4 * width * features
    )
    far = pl.pallas_call(
        second_projection_kernel,
        out_shape=pltpu.VMEM(block, jnp.float32),
        in_specs=[vmem] * 3,
        out_specs=vmem,
        compiler_params=params,
        cost_estimate=cost,
        name="projection_other_y",
    )(low, far_k, far_v)
    far = (far + swap(to_core, "head", head, 1).astype(jnp.float32)).astype(jnp.bfloat16)
    got = swap(far, "head", head, 2)
    to_core, total, dk_low, dv_low = pl.pallas_call(
        last_projection_kernel,
        out_shape=[
            pltpu.VMEM(block, jnp.bfloat16),
            pltpu.VMEM(block, jnp.float32),
            jax.ShapeDtypeStruct((own, width), jnp.bfloat16),
            jax.ShapeDtypeStruct((own, width), jnp.bfloat16),
        ],
        in_specs=[vmem, hbm, hbm, pl.BlockSpec(memory_space=pl.ANY)],
        out_specs=[vmem] * 4,
        scratch_shapes=[
            pltpu.VMEM((2, 2, features, width), k_weight.dtype),
            pltpu.SemaphoreType.DMA((2, 2)),
        ],
        compiler_params=pltpu.CompilerParams(
            vmem_limit_bytes=(8 << 20) + 8 * features * width
        ),
        cost_estimate=cost,
        name="projection_this_y",
    )(low, *weights, far)
    total = lax.optimization_barrier(total + got.astype(jnp.float32))
    total += swap(to_core, "head", head, 1).astype(jnp.float32)
    return dk_low, dv_low, total.astype(jnp.bfloat16)


def solution(mesh):
    placed = (
        P("resp", "head"),
        P("resp", "head"),
        P("resp", "head"),
        P("resp", "head"),
        P(None, "head"),
        P(None, "head"),
        P("resp"),
    )
    return jax.shard_map(
        functools.partial(body, mesh.shape["resp"], mesh.shape["head"]),
        mesh=mesh,
        in_specs=placed,
        out_specs=(P("resp", "head"), P("resp", "head"), P("resp", "head")),
        check_vma=False,
    )
```

```python
import functools

import jax
import jax.numpy as jnp
from jax import lax
from jax.experimental import pallas as pl
from jax.experimental.pallas import tpu as pltpu
from jax.sharding import PartitionSpec as P

HD = 128
LEN = 256
NT = (((1,), (1,)), ((), ()))
UNIT = 2
LOG2E = 1.4426950408889634


def join_kernel(k_hbm, v_hbm, out_ref, both_ref, sems):
    width = k_hbm.shape[1]
    copies = [
        pltpu.make_async_copy(k_hbm, both_ref.at[:, pl.ds(0, width)], sems.at[0]),
        pltpu.make_async_copy(v_hbm, both_ref.at[:, pl.ds(width, width)], sems.at[1]),
    ]
    for copy in copies:
        copy.start()
    for copy in copies:
        copy.wait()
    both = both_ref[...]
    for i in range(out_ref.shape[0]):
        out_ref[i] = both


def load_kernel(lengths_ref, *refs):
    count = (len(refs) - 2) // 2
    live_ref, sems = refs[2 * count :]
    copies = [
        pltpu.make_async_copy(refs[i], refs[count + i], sems.at[i]) for i in range(count)
    ]
    for copy in copies:
        copy.start()
    position = lax.broadcasted_iota(jnp.int32, live_ref.shape[1:], 1)
    for part in range(live_ref.shape[0]):
        live_ref[part] = jnp.where(position < lengths_ref[part], 1.0, 0.0)
    for copy in copies:
        copy.wait()


def attention_kernel(
    live_ref, kv_ref, q_ref, g_ref, vw_hbm, out_ref, vw_ref, probs_ref, dscores_ref, sem
):
    weight = pltpu.make_async_copy(vw_hbm, vw_ref, sem)
    weight.start()
    scale = HD ** (-0.5)
    width = kv_ref.shape[1] // 2
    kv_local = width // HD
    parts = q_ref.shape[0] // LEN
    group = q_ref.shape[1] // HD // kv_local
    units = [
        (k, part, h)
        for k in range(kv_local)
        for part in range(parts)
        for h in range(0, group, UNIT)
    ]

    def stack(ref, unit):
        k, part, h = unit
        heads = [
            ref[part * LEN : (part + 1) * LEN, at * HD : (at + 1) * HD]
            for at in range(k * group + h, k * group + h + UNIT)
        ]
        return jnp.concatenate(heads, axis=0)

    def products(unit):
        k = unit[0]
        keys = kv_ref[:, k * HD : (k + 1) * HD]
        values = kv_ref[:, width + k * HD : width + (k + 1) * HD]
        return (
            lax.dot_general(keys, stack(q_ref, unit), NT, preferred_element_type=jnp.float32),
            lax.dot_general(values, stack(g_ref, unit), NT, preferred_element_type=jnp.float32),
        )

    following = products(units[0])
    for i, unit in enumerate(units):
        k, part, h = unit
        scores, dprobs = following
        if i + 1 < len(units):
            following = products(units[i + 1])
        top = jnp.max(scores, axis=0, keepdims=True)
        expo = jnp.exp2((scores - top) * (scale * LOG2E))
        total = jnp.sum(expo, axis=0, keepdims=True)
        weighted = jnp.sum(expo * dprobs, axis=0, keepdims=True)
        inverse = 1.0 / total
        delta = weighted * inverse
        factor = inverse * jnp.concatenate([live_ref[part, :1]] * UNIT, axis=1)
        probs = expo * factor
        mine = [u for u in units if u[0] == k]
        cols = pl.ds(mine.index(unit) * UNIT * LEN, UNIT * LEN)
        probs_ref[k, :, cols] = probs.astype(jnp.bfloat16)
        dscores_ref[k, :, cols] = (probs * (dprobs - delta)).astype(jnp.bfloat16)
        if unit == mine[-1]:
            q_all = jnp.concatenate([stack(q_ref, u) for u in mine], axis=0)
            g_all = jnp.concatenate([stack(g_ref, u) for u in mine], axis=0)
            grad_k = jnp.dot(dscores_ref[k], q_all, preferred_element_type=jnp.float32) * scale
            grad_v = jnp.dot(probs_ref[k], g_all, preferred_element_type=jnp.float32)
            out_ref[:, k * HD : (k + 1) * HD] = grad_k.astype(out_ref.dtype)
            out_ref[:, width + k * HD : width + (k + 1) * HD] = grad_v.astype(out_ref.dtype)
    weight.wait()


def project(low, kw_ref, vw_ref, owner, features):
    width = kw_ref.shape[1]
    rows = pl.ds(pl.multiple_of(owner * features, features), features)
    out = lax.dot_general(
        low[:, :width], kw_ref[rows, :], NT, preferred_element_type=jnp.float32
    )
    return out + lax.dot_general(
        low[:, width:], vw_ref[rows, :], NT, preferred_element_type=jnp.float32
    )


def first_projection_kernel(parts_ref, kw_ref, vw_ref, low_ref, out_ref):
    total = parts_ref[0].astype(jnp.float32)
    for i in range(1, parts_ref.shape[0]):
        total += parts_ref[i].astype(jnp.float32)
    low = total.astype(jnp.bfloat16)
    low_ref[...] = low
    me = lax.axis_index("head")
    out = project(low, kw_ref, vw_ref, me ^ 3, out_ref.shape[1])
    out_ref[...] = out.astype(out_ref.dtype)


def second_projection_kernel(low_ref, kw_ref, vw_ref, out_ref):
    me = lax.axis_index("head")
    out_ref[...] = project(low_ref[...], kw_ref, vw_ref, me ^ 2, out_ref.shape[1])


def last_projection_kernel(low_ref, kw_ref, vw_ref, after, out_ref, keep_ref, dk_ref, dv_ref):
    del after
    width = dk_ref.shape[1]
    low = low_ref[...]
    dk_ref[...] = low[:, :width]
    dv_ref[...] = low[:, width:]
    me = lax.axis_index("head")
    out = project(low, kw_ref, vw_ref, me ^ 1, out_ref.shape[1])
    out_ref[...] = out.astype(out_ref.dtype)
    keep_ref[...] = project(low, kw_ref, vw_ref, me, keep_ref.shape[1])


def swap(x, axis, count, bit):
    return lax.ppermute(x, axis, [(i, i ^ bit) for i in range(count)])


def body(resp, head, queries, d_out, prefix_keys, prefix_values, k_weight, v_weight, lengths):
    own, width = prefix_keys.shape
    features = k_weight.shape[0] // head
    vmem = pl.BlockSpec(memory_space=pltpu.VMEM)
    hbm = pl.BlockSpec(memory_space=pltpu.HBM)
    params = pltpu.CompilerParams(vmem_limit_bytes=12 << 20)

    def in_hbm(*xs):
        return [pltpu.with_memory_space_constraint(x, pltpu.HBM) for x in xs]

    both = pl.pallas_call(
        join_kernel,
        out_shape=jax.ShapeDtypeStruct((resp, own, 2 * width), jnp.bfloat16),
        in_specs=[hbm] * 2,
        out_specs=vmem,
        scratch_shapes=[
            pltpu.VMEM((own, 2 * width), jnp.bfloat16),
            pltpu.SemaphoreType.DMA((2,)),
        ],
        compiler_params=params,
        name="join",
    )(*in_hbm(prefix_keys, prefix_values))
    both = lax.all_to_all(both, "resp", 0, 0, tiled=True).reshape(resp * own, 2 * width)

    large = (queries, d_out)
    responses = lengths.shape[0]
    queries, d_out, live = pl.pallas_call(
        load_kernel,
        out_shape=[pltpu.VMEM(x.shape, x.dtype) for x in large]
        + [pltpu.VMEM((responses, 8, LEN), jnp.float32)],
        in_specs=[pl.BlockSpec(memory_space=pltpu.SMEM)] + [hbm] * len(large),
        out_specs=[vmem] * (len(large) + 1),
        scratch_shapes=[pltpu.SemaphoreType.DMA((len(large),))],
        compiler_params=params,
        cost_estimate=pl.CostEstimate(
            flops=0, transcendentals=0, bytes_accessed=sum(4 * x.size for x in large)
        ),
        name="load",
    )(lengths, *in_hbm(*large))

    tokens = resp * own
    kv_local = width // HD
    depth = queries.size // kv_local // HD
    partial, v_weight = pl.pallas_call(
        attention_kernel,
        out_shape=[
            pltpu.VMEM((tokens, 2 * width), jnp.bfloat16),
            pltpu.VMEM(v_weight.shape, v_weight.dtype),
        ],
        in_specs=[vmem] * 4 + [hbm],
        out_specs=[vmem] * 2,
        scratch_shapes=[
            pltpu.VMEM((kv_local, tokens, depth), jnp.bfloat16),
            pltpu.VMEM((kv_local, tokens, depth), jnp.bfloat16),
            pltpu.SemaphoreType.DMA,
        ],
        compiler_params=pltpu.CompilerParams(
            vmem_limit_bytes=(8 << 20) + 8 * kv_local * tokens * depth
        ),
        cost_estimate=pl.CostEstimate(
            flops=8 * kv_local * tokens * depth * HD,
            transcendentals=kv_local * tokens * depth,
            bytes_accessed=4 * queries.size + 6 * tokens * width,
        ),
        name="attention",
    )(live, both, queries, d_out, *in_hbm(v_weight))

    shares = lax.all_to_all(
        partial.reshape(resp, own, 2 * width), "resp", 0, 0, tiled=True
    )

    block = (own, features)
    low, to_core = pl.pallas_call(
        first_projection_kernel,
        out_shape=[
            pltpu.VMEM((own, 2 * width), jnp.bfloat16),
            pltpu.VMEM(block, jnp.bfloat16),
        ],
        in_specs=[vmem] * 3,
        out_specs=[vmem] * 2,
        compiler_params=params,
        name="projection_other_core",
    )(shares, k_weight, v_weight)
    cost = pl.CostEstimate(
        flops=4 * own * width * features, transcendentals=0, bytes_accessed=4 * width * features
    )
    far = pl.pallas_call(
        second_projection_kernel,
        out_shape=pltpu.VMEM(block, jnp.float32),
        in_specs=[vmem] * 3,
        out_specs=vmem,
        compiler_params=params,
        cost_estimate=cost,
        name="projection_other_y",
    )(low, k_weight, v_weight)
    far = (far + swap(to_core, "head", head, 1).astype(jnp.float32)).astype(jnp.bfloat16)
    got = swap(far, "head", head, 2)
    to_core, total, dk_low, dv_low = pl.pallas_call(
        last_projection_kernel,
        out_shape=[
            pltpu.VMEM(block, jnp.bfloat16),
            pltpu.VMEM(block, jnp.float32),
            jax.ShapeDtypeStruct((own, width), jnp.bfloat16),
            jax.ShapeDtypeStruct((own, width), jnp.bfloat16),
        ],
        in_specs=[vmem] * 3 + [pl.BlockSpec(memory_space=pl.ANY)],
        out_specs=[vmem] * 4,
        compiler_params=params,
        cost_estimate=cost,
        name="projection_this_y",
    )(low, k_weight, v_weight, far)
    total = lax.optimization_barrier(total + got.astype(jnp.float32))
    total += swap(to_core, "head", head, 1).astype(jnp.float32)
    return dk_low, dv_low, total.astype(jnp.bfloat16)


def solution(mesh):
    placed = (
        P("resp", "head"),
        P("resp", "head"),
        P("resp", "head"),
        P("resp", "head"),
        P(None, "head"),
        P(None, "head"),
        P("resp"),
    )
    return jax.shard_map(
        functools.partial(body, mesh.shape["resp"], mesh.shape["head"]),
        mesh=mesh,
        in_specs=placed,
        out_specs=(P("resp", "head"), P("resp", "head"), P("resp", "head")),
        check_vma=False,
    )
```

```python
import functools

import jax
import jax.numpy as jnp
from jax import lax
from jax.experimental import pallas as pl
from jax.experimental.pallas import tpu as pltpu
from jax.sharding import PartitionSpec as P

HD = 128
LEN = 256
NT = (((1,), (1,)), ((), ()))
UNIT = 2
LOG2E = 1.4426950408889634


def join_kernel(k_hbm, v_hbm, out_ref, both_ref, sems):
    width = k_hbm.shape[1]
    copies = [
        pltpu.make_async_copy(k_hbm, both_ref.at[:, pl.ds(0, width)], sems.at[0]),
        pltpu.make_async_copy(v_hbm, both_ref.at[:, pl.ds(width, width)], sems.at[1]),
    ]
    for copy in copies:
        copy.start()
    for copy in copies:
        copy.wait()
    both = both_ref[...]
    for i in range(out_ref.shape[0]):
        out_ref[i] = both


def load_kernel(lengths_ref, *refs):
    count = (len(refs) - 2) // 2
    live_ref, sems = refs[2 * count :]
    copies = [
        pltpu.make_async_copy(refs[i], refs[count + i], sems.at[i]) for i in range(count)
    ]
    for copy in copies:
        copy.start()
    position = lax.broadcasted_iota(jnp.int32, live_ref.shape[1:], 1)
    for part in range(live_ref.shape[0]):
        live_ref[part] = jnp.where(position < lengths_ref[part], 1.0, 0.0)
    for copy in copies:
        copy.wait()


def attention_kernel(live_ref, kv_ref, q_ref, g_ref, out_ref, probs_ref, dscores_ref):
    scale = HD ** (-0.5)
    width = kv_ref.shape[1] // 2
    kv_local = width // HD
    parts = q_ref.shape[0] // LEN
    group = q_ref.shape[1] // HD // kv_local
    units = [
        (k, part, h)
        for k in range(kv_local)
        for part in range(parts)
        for h in range(0, group, UNIT)
    ]

    def stack(ref, unit):
        k, part, h = unit
        heads = [
            ref[part * LEN : (part + 1) * LEN, at * HD : (at + 1) * HD]
            for at in range(k * group + h, k * group + h + UNIT)
        ]
        return jnp.concatenate(heads, axis=0)

    def products(unit):
        k = unit[0]
        keys = kv_ref[:, k * HD : (k + 1) * HD]
        values = kv_ref[:, width + k * HD : width + (k + 1) * HD]
        return (
            lax.dot_general(keys, stack(q_ref, unit), NT, preferred_element_type=jnp.float32),
            lax.dot_general(values, stack(g_ref, unit), NT, preferred_element_type=jnp.float32),
        )

    following = products(units[0])
    for i, unit in enumerate(units):
        k, part, h = unit
        scores, dprobs = following
        if i + 1 < len(units):
            following = products(units[i + 1])
        top = jnp.max(scores, axis=0, keepdims=True)
        expo = jnp.exp2((scores - top) * (scale * LOG2E))
        total = jnp.sum(expo, axis=0, keepdims=True)
        weighted = jnp.sum(expo * dprobs, axis=0, keepdims=True)
        inverse = 1.0 / total
        delta = weighted * inverse
        factor = inverse * jnp.concatenate([live_ref[part, :1]] * UNIT, axis=1)
        probs = expo * factor
        mine = [u for u in units if u[0] == k]
        cols = pl.ds(mine.index(unit) * UNIT * LEN, UNIT * LEN)
        probs_ref[k, :, cols] = probs.astype(jnp.bfloat16)
        dscores_ref[k, :, cols] = (probs * (dprobs - delta)).astype(jnp.bfloat16)
        if unit == mine[-1]:
            q_all = jnp.concatenate([stack(q_ref, u) for u in mine], axis=0)
            g_all = jnp.concatenate([stack(g_ref, u) for u in mine], axis=0)
            grad_k = jnp.dot(dscores_ref[k], q_all, preferred_element_type=jnp.float32) * scale
            grad_v = jnp.dot(probs_ref[k], g_all, preferred_element_type=jnp.float32)
            out_ref[:, k * HD : (k + 1) * HD] = grad_k.astype(out_ref.dtype)
            out_ref[:, width + k * HD : width + (k + 1) * HD] = grad_v.astype(out_ref.dtype)


def project(low, kw_ref, vw_ref, owner, features):
    width = kw_ref.shape[1]
    rows = pl.ds(pl.multiple_of(owner * features, features), features)
    out = lax.dot_general(
        low[:, :width], kw_ref[rows, :], NT, preferred_element_type=jnp.float32
    )
    return out + lax.dot_general(
        low[:, width:], vw_ref[rows, :], NT, preferred_element_type=jnp.float32
    )


def first_projection_kernel(parts_ref, kw_ref, vw_ref, low_ref, out_ref):
    total = parts_ref[0].astype(jnp.float32)
    for i in range(1, parts_ref.shape[0]):
        total += parts_ref[i].astype(jnp.float32)
    low = total.astype(jnp.bfloat16)
    low_ref[...] = low
    me = lax.axis_index("head")
    out = project(low, kw_ref, vw_ref, me ^ 3, out_ref.shape[1])
    out_ref[...] = out.astype(out_ref.dtype)


def second_projection_kernel(low_ref, kw_ref, vw_ref, out_ref):
    me = lax.axis_index("head")
    out_ref[...] = project(low_ref[...], kw_ref, vw_ref, me ^ 2, out_ref.shape[1])


def last_projection_kernel(low_ref, kw_ref, vw_ref, after, out_ref, keep_ref, dk_ref, dv_ref):
    del after
    width = dk_ref.shape[1]
    low = low_ref[...]
    dk_ref[...] = low[:, :width]
    dv_ref[...] = low[:, width:]
    me = lax.axis_index("head")
    out = project(low, kw_ref, vw_ref, me ^ 1, out_ref.shape[1])
    out_ref[...] = out.astype(out_ref.dtype)
    keep_ref[...] = project(low, kw_ref, vw_ref, me, keep_ref.shape[1])


def swap(x, axis, count, bit):
    return lax.ppermute(x, axis, [(i, i ^ bit) for i in range(count)])


def body(resp, head, queries, d_out, prefix_keys, prefix_values, k_weight, v_weight, lengths):
    own, width = prefix_keys.shape
    features = k_weight.shape[0] // head
    vmem = pl.BlockSpec(memory_space=pltpu.VMEM)
    hbm = pl.BlockSpec(memory_space=pltpu.HBM)
    params = pltpu.CompilerParams(vmem_limit_bytes=12 << 20)

    def in_hbm(*xs):
        return [pltpu.with_memory_space_constraint(x, pltpu.HBM) for x in xs]

    both = pl.pallas_call(
        join_kernel,
        out_shape=jax.ShapeDtypeStruct((resp, own, 2 * width), jnp.bfloat16),
        in_specs=[hbm] * 2,
        out_specs=vmem,
        scratch_shapes=[
            pltpu.VMEM((own, 2 * width), jnp.bfloat16),
            pltpu.SemaphoreType.DMA((2,)),
        ],
        compiler_params=params,
        name="join",
    )(*in_hbm(prefix_keys, prefix_values))
    both = lax.all_to_all(both, "resp", 0, 0, tiled=True).reshape(resp * own, 2 * width)

    large = (queries, d_out)
    responses = lengths.shape[0]
    queries, d_out, live = pl.pallas_call(
        load_kernel,
        out_shape=[pltpu.VMEM(x.shape, x.dtype) for x in large]
        + [pltpu.VMEM((responses, 8, LEN), jnp.float32)],
        in_specs=[pl.BlockSpec(memory_space=pltpu.SMEM)] + [hbm] * len(large),
        out_specs=[vmem] * (len(large) + 1),
        scratch_shapes=[pltpu.SemaphoreType.DMA((len(large),))],
        compiler_params=params,
        cost_estimate=pl.CostEstimate(
            flops=0, transcendentals=0, bytes_accessed=sum(4 * x.size for x in large)
        ),
        name="load",
    )(lengths, *in_hbm(*large))

    tokens = resp * own
    kv_local = width // HD
    depth = queries.size // kv_local // HD
    partial = pl.pallas_call(
        attention_kernel,
        out_shape=pltpu.VMEM((tokens, 2 * width), jnp.bfloat16),
        in_specs=[vmem] * 4,
        out_specs=vmem,
        scratch_shapes=[
            pltpu.VMEM((kv_local, tokens, depth), jnp.bfloat16),
            pltpu.VMEM((kv_local, tokens, depth), jnp.bfloat16),
        ],
        compiler_params=pltpu.CompilerParams(
            vmem_limit_bytes=(8 << 20) + 8 * kv_local * tokens * depth
        ),
        cost_estimate=pl.CostEstimate(
            flops=64 * kv_local * tokens * depth * HD,
            transcendentals=kv_local * tokens * depth,
            bytes_accessed=4 * queries.size + 6 * tokens * width,
        ),
        name="attention",
    )(live, both, queries, d_out)

    shares = lax.all_to_all(
        partial.reshape(resp, own, 2 * width), "resp", 0, 0, tiled=True
    )

    block = (own, features)
    low, to_core = pl.pallas_call(
        first_projection_kernel,
        out_shape=[
            pltpu.VMEM((own, 2 * width), jnp.bfloat16),
            pltpu.VMEM(block, jnp.bfloat16),
        ],
        in_specs=[vmem] * 3,
        out_specs=[vmem] * 2,
        compiler_params=params,
        name="projection_other_core",
    )(shares, k_weight, v_weight)
    cost = pl.CostEstimate(
        flops=4 * own * width * features, transcendentals=0, bytes_accessed=4 * width * features
    )
    far = pl.pallas_call(
        second_projection_kernel,
        out_shape=pltpu.VMEM(block, jnp.float32),
        in_specs=[vmem] * 3,
        out_specs=vmem,
        compiler_params=params,
        cost_estimate=cost,
        name="projection_other_y",
    )(low, k_weight, v_weight)
    far = (far + swap(to_core, "head", head, 1).astype(jnp.float32)).astype(jnp.bfloat16)
    got = swap(far, "head", head, 2)
    to_core, total, dk_low, dv_low = pl.pallas_call(
        last_projection_kernel,
        out_shape=[
            pltpu.VMEM(block, jnp.bfloat16),
            pltpu.VMEM(block, jnp.float32),
            jax.ShapeDtypeStruct((own, width), jnp.bfloat16),
            jax.ShapeDtypeStruct((own, width), jnp.bfloat16),
        ],
        in_specs=[vmem] * 3 + [pl.BlockSpec(memory_space=pl.ANY)],
        out_specs=[vmem] * 4,
        compiler_params=params,
        cost_estimate=cost,
        name="projection_this_y",
    )(low, k_weight, v_weight, far)
    total = lax.optimization_barrier(total + got.astype(jnp.float32))
    total += swap(to_core, "head", head, 1).astype(jnp.float32)
    return dk_low, dv_low, total.astype(jnp.bfloat16)


def solution(mesh):
    placed = (
        P("resp", "head"),
        P("resp", "head"),
        P("resp", "head"),
        P("resp", "head"),
        P(None, "head"),
        P(None, "head"),
        P("resp"),
    )
    return jax.shard_map(
        functools.partial(body, mesh.shape["resp"], mesh.shape["head"]),
        mesh=mesh,
        in_specs=placed,
        out_specs=(P("resp", "head"), P("resp", "head"), P("resp", "head")),
        check_vma=False,
    )
```

```python
import functools

import jax
import jax.numpy as jnp
from jax import lax
from jax.experimental import pallas as pl
from jax.experimental.pallas import tpu as pltpu
from jax.sharding import PartitionSpec as P

HD = 128
LEN = 256
NT = (((1,), (1,)), ((), ()))
UNIT = 2
LOG2E = 1.4426950408889634


def join_kernel(k_hbm, v_hbm, out_ref, both_ref, sems):
    width = k_hbm.shape[1]
    copies = [
        pltpu.make_async_copy(k_hbm, both_ref.at[:, pl.ds(0, width)], sems.at[0]),
        pltpu.make_async_copy(v_hbm, both_ref.at[:, pl.ds(width, width)], sems.at[1]),
    ]
    for copy in copies:
        copy.start()
    for copy in copies:
        copy.wait()
    both = both_ref[...]
    for i in range(out_ref.shape[0]):
        out_ref[i] = both


def load_kernel(lengths_ref, *refs):
    count = (len(refs) - 2) // 2
    live_ref, sems = refs[2 * count :]
    copies = [
        pltpu.make_async_copy(refs[i], refs[count + i], sems.at[i]) for i in range(count)
    ]
    for copy in copies:
        copy.start()
    position = lax.broadcasted_iota(jnp.int32, live_ref.shape[1:], 1)
    for part in range(live_ref.shape[0]):
        live_ref[part] = jnp.where(position < lengths_ref[part], 1.0, 0.0)
    for copy in copies:
        copy.wait()


def attention_kernel(live_ref, kv_ref, q_ref, g_ref, out_ref, probs_ref, dscores_ref):
    scale = HD ** (-0.5)
    width = kv_ref.shape[1] // 2
    kv_local = width // HD
    parts = q_ref.shape[0] // LEN
    group = q_ref.shape[1] // HD // kv_local
    units = [
        (k, part, h)
        for k in range(kv_local)
        for part in range(parts)
        for h in range(0, group, UNIT)
    ]

    def stack(ref, unit):
        k, part, h = unit
        heads = [
            ref[part * LEN : (part + 1) * LEN, at * HD : (at + 1) * HD]
            for at in range(k * group + h, k * group + h + UNIT)
        ]
        return jnp.concatenate(heads, axis=0)

    def products(unit):
        k = unit[0]
        keys = kv_ref[:, k * HD : (k + 1) * HD]
        values = kv_ref[:, width + k * HD : width + (k + 1) * HD]
        return (
            lax.dot_general(keys, stack(q_ref, unit), NT, preferred_element_type=jnp.float32),
            lax.dot_general(values, stack(g_ref, unit), NT, preferred_element_type=jnp.float32),
        )

    def sums(i):
        unit = units[i]
        return (
            jnp.dot(dscores_ref[i % 2], stack(q_ref, unit), preferred_element_type=jnp.float32),
            jnp.dot(probs_ref[i % 2], stack(g_ref, unit), preferred_element_type=jnp.float32),
        )

    def finish(k, grad_k, grad_v):
        out_ref[:, k * HD : (k + 1) * HD] = (grad_k * scale).astype(out_ref.dtype)
        out_ref[:, width + k * HD : width + (k + 1) * HD] = grad_v.astype(out_ref.dtype)

    following = products(units[0])
    for i, unit in enumerate(units):
        k, part, h = unit
        scores, dprobs = following
        if i + 1 < len(units):
            following = products(units[i + 1])
        if i > 0:
            more_k, more_v = sums(i - 1)
            first = i == 1 or units[i - 2][0] != units[i - 1][0]
            grad_k = more_k if first else grad_k + more_k
            grad_v = more_v if first else grad_v + more_v
            if units[i - 1][0] != k:
                finish(units[i - 1][0], grad_k, grad_v)
        top = jnp.max(scores, axis=0, keepdims=True)
        expo = jnp.exp2((scores - top) * (scale * LOG2E))
        total = jnp.sum(expo, axis=0, keepdims=True)
        weighted = jnp.sum(expo * dprobs, axis=0, keepdims=True)
        inverse = 1.0 / total
        delta = weighted * inverse
        factor = inverse * jnp.concatenate([live_ref[part, :1]] * UNIT, axis=1)
        probs = expo * factor
        probs_ref[i % 2] = probs.astype(jnp.bfloat16)
        dscores_ref[i % 2] = (probs * (dprobs - delta)).astype(jnp.bfloat16)
    more_k, more_v = sums(len(units) - 1)
    finish(units[-1][0], grad_k + more_k, grad_v + more_v)


def project(low, kw_ref, vw_ref, owner, features):
    width = kw_ref.shape[1]
    rows = pl.ds(pl.multiple_of(owner * features, features), features)
    out = lax.dot_general(
        low[:, :width], kw_ref[rows, :], NT, preferred_element_type=jnp.float32
    )
    return out + lax.dot_general(
        low[:, width:], vw_ref[rows, :], NT, preferred_element_type=jnp.float32
    )


def sum_kernel(parts_ref, kw_ref, vw_ref, low_ref, out_ref):
    total = parts_ref[0].astype(jnp.float32)
    for i in range(1, parts_ref.shape[0]):
        total += parts_ref[i].astype(jnp.float32)
    low_ref[...] = total.astype(jnp.bfloat16)
    other_core_term(1, low_ref, kw_ref, vw_ref, out_ref)


def other_core_term(core, low_ref, kw_ref, vw_ref, out_ref):
    me = lax.axis_index("head")

    @pl.when(lax.rem(me, 2) == core)
    def _():
        out = project(low_ref[...], kw_ref, vw_ref, me ^ 3, out_ref.shape[1])
        out_ref[...] = out.astype(out_ref.dtype)


def second_projection_kernel(low_ref, kw_ref, vw_ref, after, out_ref):
    del after
    me = lax.axis_index("head")
    out_ref[...] = project(low_ref[...], kw_ref, vw_ref, me ^ 2, out_ref.shape[1])


def last_projection_kernel(low_ref, kw_ref, vw_ref, after, out_ref, keep_ref, dk_ref, dv_ref):
    del after
    width = dk_ref.shape[1]
    low = low_ref[...]
    dk_ref[...] = low[:, :width]
    dv_ref[...] = low[:, width:]
    me = lax.axis_index("head")
    out = project(low, kw_ref, vw_ref, me ^ 1, out_ref.shape[1])
    out_ref[...] = out.astype(out_ref.dtype)
    keep_ref[...] = project(low, kw_ref, vw_ref, me, keep_ref.shape[1])


def swap(x, axis, count, bit):
    return lax.ppermute(x, axis, [(i, i ^ bit) for i in range(count)])


def one_way(x, count, core):
    return lax.ppermute(x, "head", [(i, i ^ 1) for i in range(count) if i % 2 == core])


def body(resp, head, queries, d_out, prefix_keys, prefix_values, k_weight, v_weight, lengths):
    own, width = prefix_keys.shape
    features = k_weight.shape[0] // head
    vmem = pl.BlockSpec(memory_space=pltpu.VMEM)
    hbm = pl.BlockSpec(memory_space=pltpu.HBM)
    params = pltpu.CompilerParams(vmem_limit_bytes=12 << 20)

    def in_hbm(*xs):
        return [pltpu.with_memory_space_constraint(x, pltpu.HBM) for x in xs]

    both = pl.pallas_call(
        join_kernel,
        out_shape=jax.ShapeDtypeStruct((resp, own, 2 * width), jnp.bfloat16),
        in_specs=[hbm] * 2,
        out_specs=vmem,
        scratch_shapes=[
            pltpu.VMEM((own, 2 * width), jnp.bfloat16),
            pltpu.SemaphoreType.DMA((2,)),
        ],
        compiler_params=params,
        name="join",
    )(*in_hbm(prefix_keys, prefix_values))
    both = lax.all_to_all(both, "resp", 0, 0, tiled=True).reshape(resp * own, 2 * width)

    large = (queries, d_out)
    responses = lengths.shape[0]
    queries, d_out, live = pl.pallas_call(
        load_kernel,
        out_shape=[pltpu.VMEM(x.shape, x.dtype) for x in large]
        + [pltpu.VMEM((responses, 8, LEN), jnp.float32)],
        in_specs=[pl.BlockSpec(memory_space=pltpu.SMEM)] + [hbm] * len(large),
        out_specs=[vmem] * (len(large) + 1),
        scratch_shapes=[pltpu.SemaphoreType.DMA((len(large),))],
        compiler_params=params,
        cost_estimate=pl.CostEstimate(
            flops=0, transcendentals=0, bytes_accessed=sum(4 * x.size for x in large)
        ),
        name="load",
    )(lengths, *in_hbm(*large))

    tokens = resp * own
    kv_local = width // HD
    depth = queries.size // kv_local // HD
    partial = pl.pallas_call(
        attention_kernel,
        out_shape=pltpu.VMEM((tokens, 2 * width), jnp.bfloat16),
        in_specs=[vmem] * 4,
        out_specs=vmem,
        scratch_shapes=[
            pltpu.VMEM((2, tokens, UNIT * LEN), jnp.bfloat16),
            pltpu.VMEM((2, tokens, UNIT * LEN), jnp.bfloat16),
        ],
        compiler_params=pltpu.CompilerParams(
            vmem_limit_bytes=(8 << 20) + 40 * UNIT * LEN * tokens
        ),
        cost_estimate=pl.CostEstimate(
            flops=64 * kv_local * tokens * depth * HD,
            transcendentals=kv_local * tokens * depth,
            bytes_accessed=4 * queries.size + 6 * tokens * width,
        ),
        name="attention",
    )(live, both, queries, d_out)

    shares = lax.all_to_all(
        partial.reshape(resp, own, 2 * width), "resp", 0, 0, tiled=True
    )

    block = (own, features)
    low, from_one = pl.pallas_call(
        sum_kernel,
        out_shape=[
            pltpu.VMEM((own, 2 * width), jnp.bfloat16),
            pltpu.VMEM(block, jnp.bfloat16),
        ],
        in_specs=[vmem] * 3,
        out_specs=[vmem] * 2,
        compiler_params=params,
        name="sum_and_projection_core_1",
    )(shares, k_weight, v_weight)
    from_one = one_way(from_one, head, 1)
    cost = pl.CostEstimate(
        flops=4 * own * width * features, transcendentals=0, bytes_accessed=4 * width * features
    )
    from_zero = pl.pallas_call(
        functools.partial(other_core_term, 0),
        out_shape=pltpu.VMEM(block, jnp.bfloat16),
        in_specs=[vmem] * 3,
        out_specs=vmem,
        compiler_params=params,
        cost_estimate=cost,
        name="projection_core_0",
    )(low, k_weight, v_weight)
    far = pl.pallas_call(
        second_projection_kernel,
        out_shape=pltpu.VMEM(block, jnp.float32),
        in_specs=[vmem] * 3 + [pl.BlockSpec(memory_space=pl.ANY)],
        out_specs=vmem,
        compiler_params=params,
        cost_estimate=cost,
        name="projection_other_y",
    )(low, k_weight, v_weight, from_zero)
    from_zero = one_way(from_zero, head, 0)
    far = lax.optimization_barrier(far + from_one.astype(jnp.float32))
    far = (far + from_zero.astype(jnp.float32)).astype(jnp.bfloat16)
    got = swap(far, "head", head, 2)
    to_core, total, dk_low, dv_low = pl.pallas_call(
        last_projection_kernel,
        out_shape=[
            pltpu.VMEM(block, jnp.bfloat16),
            pltpu.VMEM(block, jnp.float32),
            jax.ShapeDtypeStruct((own, width), jnp.bfloat16),
            jax.ShapeDtypeStruct((own, width), jnp.bfloat16),
        ],
        in_specs=[vmem] * 3 + [pl.BlockSpec(memory_space=pl.ANY)],
        out_specs=[vmem] * 4,
        compiler_params=params,
        cost_estimate=cost,
        name="projection_this_y",
    )(low, k_weight, v_weight, far)
    total = lax.optimization_barrier(total + got.astype(jnp.float32))
    total += swap(to_core, "head", head, 1).astype(jnp.float32)
    return dk_low, dv_low, total.astype(jnp.bfloat16)


def solution(mesh):
    placed = (
        P("resp", "head"),
        P("resp", "head"),
        P("resp", "head"),
        P("resp", "head"),
        P(None, "head"),
        P(None, "head"),
        P("resp"),
    )
    return jax.shard_map(
        functools.partial(body, mesh.shape["resp"], mesh.shape["head"]),
        mesh=mesh,
        in_specs=placed,
        out_specs=(P("resp", "head"), P("resp", "head"), P("resp", "head")),
        check_vma=False,
    )
```

```python
import functools

import jax
import jax.numpy as jnp
from jax import lax
from jax.experimental import pallas as pl
from jax.experimental.pallas import tpu as pltpu
from jax.sharding import PartitionSpec as P

HD = 128
LEN = 256
NT = (((1,), (1,)), ((), ()))
UNIT = 2
LOG2E = 1.4426950408889634


def join_kernel(k_hbm, v_hbm, out_ref, both_ref, sems):
    width = k_hbm.shape[1]
    copies = [
        pltpu.make_async_copy(k_hbm, both_ref.at[:, pl.ds(0, width)], sems.at[0]),
        pltpu.make_async_copy(v_hbm, both_ref.at[:, pl.ds(width, width)], sems.at[1]),
    ]
    for copy in copies:
        copy.start()
    for copy in copies:
        copy.wait()
    both = both_ref[...]
    for i in range(out_ref.shape[0]):
        out_ref[i] = both


def load_kernel(lengths_ref, *refs):
    count = (len(refs) - 2) // 2
    live_ref, sems = refs[2 * count :]
    copies = [
        pltpu.make_async_copy(refs[i], refs[count + i], sems.at[i]) for i in range(count)
    ]
    for copy in copies:
        copy.start()
    position = lax.broadcasted_iota(jnp.int32, live_ref.shape[1:], 1)
    for part in range(live_ref.shape[0]):
        live_ref[part] = jnp.where(position < lengths_ref[part], 1.0, 0.0)
    for copy in copies:
        copy.wait()


def attention_kernel(live_ref, kv_ref, q_ref, g_ref, out_ref, blocks_ref, weights_ref):
    scale = HD ** (-0.5)
    tokens = kv_ref.shape[0]
    width = kv_ref.shape[1] // 2
    kv_local = width // HD
    parts = q_ref.shape[0] // LEN
    group = q_ref.shape[1] // HD // kv_local
    units = [
        (k, part, h)
        for k in range(kv_local)
        for part in range(parts)
        for h in range(0, group, UNIT)
    ]

    def stack(ref, unit):
        k, part, h = unit
        heads = [
            ref[part * LEN : (part + 1) * LEN, at * HD : (at + 1) * HD]
            for at in range(k * group + h, k * group + h + UNIT)
        ]
        return jnp.concatenate(heads, axis=0)

    blocks_ref[...] = jnp.zeros_like(blocks_ref)
    for k in range(kv_local):
        blocks_ref[k, :tokens, :HD] = kv_ref[:, k * HD : (k + 1) * HD]
        blocks_ref[k, tokens:, HD:] = kv_ref[:, width + k * HD : width + (k + 1) * HD]

    def products(unit):
        both = jnp.concatenate([stack(q_ref, unit), stack(g_ref, unit)], axis=1)
        out = lax.dot_general(blocks_ref[unit[0]], both, NT, preferred_element_type=jnp.float32)
        return out[:tokens], out[tokens:]

    following = products(units[0])
    for i, unit in enumerate(units):
        k, part, h = unit
        scores, dprobs = following
        if i + 1 < len(units):
            following = products(units[i + 1])
        top = jnp.max(scores, axis=0, keepdims=True)
        expo = jnp.exp2((scores - top) * (scale * LOG2E))
        total = jnp.sum(expo, axis=0, keepdims=True)
        weighted = jnp.sum(expo * dprobs, axis=0, keepdims=True)
        inverse = 1.0 / total
        delta = weighted * inverse
        factor = inverse * jnp.concatenate([live_ref[part, :1]] * UNIT, axis=1)
        probs = expo * factor
        mine = [u for u in units if u[0] == k]
        cols = pl.ds(mine.index(unit) * UNIT * LEN, UNIT * LEN)
        weights_ref[k, :tokens, cols] = probs.astype(jnp.bfloat16)
        weights_ref[k, tokens:, cols] = (probs * (dprobs - delta)).astype(jnp.bfloat16)
        if unit == mine[-1]:
            rows = [
                jnp.concatenate([stack(g_ref, u), stack(q_ref, u)], axis=1) for u in mine
            ]
            out = jnp.dot(
                weights_ref[k], jnp.concatenate(rows, axis=0), preferred_element_type=jnp.float32
            )
            grad_k = out[tokens:, HD:] * scale
            out_ref[:, k * HD : (k + 1) * HD] = grad_k.astype(out_ref.dtype)
            out_ref[:, width + k * HD : width + (k + 1) * HD] = out[:tokens, :HD].astype(
                out_ref.dtype
            )


def project(low, kw_ref, vw_ref, owner, features):
    width = kw_ref.shape[1]
    rows = pl.ds(pl.multiple_of(owner * features, features), features)
    out = lax.dot_general(
        low[:, :width], kw_ref[rows, :], NT, preferred_element_type=jnp.float32
    )
    return out + lax.dot_general(
        low[:, width:], vw_ref[rows, :], NT, preferred_element_type=jnp.float32
    )


def first_projection_kernel(parts_ref, kw_ref, vw_ref, low_ref, out_ref):
    total = parts_ref[0].astype(jnp.float32)
    for i in range(1, parts_ref.shape[0]):
        total += parts_ref[i].astype(jnp.float32)
    low = total.astype(jnp.bfloat16)
    low_ref[...] = low
    me = lax.axis_index("head")
    out = project(low, kw_ref, vw_ref, me ^ 3, out_ref.shape[1])
    out_ref[...] = out.astype(out_ref.dtype)


def second_projection_kernel(low_ref, kw_ref, vw_ref, out_ref):
    me = lax.axis_index("head")
    out_ref[...] = project(low_ref[...], kw_ref, vw_ref, me ^ 2, out_ref.shape[1])


def last_projection_kernel(low_ref, kw_ref, vw_ref, after, out_ref, keep_ref, dk_ref, dv_ref):
    del after
    width = dk_ref.shape[1]
    low = low_ref[...]
    dk_ref[...] = low[:, :width]
    dv_ref[...] = low[:, width:]
    me = lax.axis_index("head")
    out = project(low, kw_ref, vw_ref, me ^ 1, out_ref.shape[1])
    out_ref[...] = out.astype(out_ref.dtype)
    keep_ref[...] = project(low, kw_ref, vw_ref, me, keep_ref.shape[1])


def swap(x, axis, count, bit):
    return lax.ppermute(x, axis, [(i, i ^ bit) for i in range(count)])


def body(resp, head, queries, d_out, prefix_keys, prefix_values, k_weight, v_weight, lengths):
    own, width = prefix_keys.shape
    features = k_weight.shape[0] // head
    vmem = pl.BlockSpec(memory_space=pltpu.VMEM)
    hbm = pl.BlockSpec(memory_space=pltpu.HBM)
    params = pltpu.CompilerParams(vmem_limit_bytes=12 << 20)

    def in_hbm(*xs):
        return [pltpu.with_memory_space_constraint(x, pltpu.HBM) for x in xs]

    both = pl.pallas_call(
        join_kernel,
        out_shape=jax.ShapeDtypeStruct((resp, own, 2 * width), jnp.bfloat16),
        in_specs=[hbm] * 2,
        out_specs=vmem,
        scratch_shapes=[
            pltpu.VMEM((own, 2 * width), jnp.bfloat16),
            pltpu.SemaphoreType.DMA((2,)),
        ],
        compiler_params=params,
        name="join",
    )(*in_hbm(prefix_keys, prefix_values))
    both = lax.all_to_all(both, "resp", 0, 0, tiled=True).reshape(resp * own, 2 * width)

    large = (queries, d_out)
    responses = lengths.shape[0]
    queries, d_out, live = pl.pallas_call(
        load_kernel,
        out_shape=[pltpu.VMEM(x.shape, x.dtype) for x in large]
        + [pltpu.VMEM((responses, 8, LEN), jnp.float32)],
        in_specs=[pl.BlockSpec(memory_space=pltpu.SMEM)] + [hbm] * len(large),
        out_specs=[vmem] * (len(large) + 1),
        scratch_shapes=[pltpu.SemaphoreType.DMA((len(large),))],
        compiler_params=params,
        cost_estimate=pl.CostEstimate(
            flops=0, transcendentals=0, bytes_accessed=sum(4 * x.size for x in large)
        ),
        name="load",
    )(lengths, *in_hbm(*large))

    tokens = resp * own
    kv_local = width // HD
    depth = queries.size // kv_local // HD
    partial = pl.pallas_call(
        attention_kernel,
        out_shape=pltpu.VMEM((tokens, 2 * width), jnp.bfloat16),
        in_specs=[vmem] * 4,
        out_specs=vmem,
        scratch_shapes=[
            pltpu.VMEM((kv_local, 2 * tokens, 2 * HD), jnp.bfloat16),
            pltpu.VMEM((kv_local, 2 * tokens, depth), jnp.bfloat16),
        ],
        compiler_params=pltpu.CompilerParams(
            vmem_limit_bytes=(8 << 20) + 8 * kv_local * tokens * depth
        ),
        cost_estimate=pl.CostEstimate(
            flops=64 * kv_local * tokens * depth * HD,
            transcendentals=kv_local * tokens * depth,
            bytes_accessed=4 * queries.size + 6 * tokens * width,
        ),
        name="attention",
    )(live, both, queries, d_out)

    shares = lax.all_to_all(
        partial.reshape(resp, own, 2 * width), "resp", 0, 0, tiled=True
    )

    block = (own, features)
    low, to_core = pl.pallas_call(
        first_projection_kernel,
        out_shape=[
            pltpu.VMEM((own, 2 * width), jnp.bfloat16),
            pltpu.VMEM(block, jnp.bfloat16),
        ],
        in_specs=[vmem] * 3,
        out_specs=[vmem] * 2,
        compiler_params=params,
        name="projection_other_core",
    )(shares, k_weight, v_weight)
    cost = pl.CostEstimate(
        flops=4 * own * width * features, transcendentals=0, bytes_accessed=4 * width * features
    )
    far = pl.pallas_call(
        second_projection_kernel,
        out_shape=pltpu.VMEM(block, jnp.float32),
        in_specs=[vmem] * 3,
        out_specs=vmem,
        compiler_params=params,
        cost_estimate=cost,
        name="projection_other_y",
    )(low, k_weight, v_weight)
    far = (far + swap(to_core, "head", head, 1).astype(jnp.float32)).astype(jnp.bfloat16)
    got = swap(far, "head", head, 2)
    to_core, total, dk_low, dv_low = pl.pallas_call(
        last_projection_kernel,
        out_shape=[
            pltpu.VMEM(block, jnp.bfloat16),
            pltpu.VMEM(block, jnp.float32),
            jax.ShapeDtypeStruct((own, width), jnp.bfloat16),
            jax.ShapeDtypeStruct((own, width), jnp.bfloat16),
        ],
        in_specs=[vmem] * 3 + [pl.BlockSpec(memory_space=pl.ANY)],
        out_specs=[vmem] * 4,
        compiler_params=params,
        cost_estimate=cost,
        name="projection_this_y",
    )(low, k_weight, v_weight, far)
    total = lax.optimization_barrier(total + got.astype(jnp.float32))
    total += swap(to_core, "head", head, 1).astype(jnp.float32)
    return dk_low, dv_low, total.astype(jnp.bfloat16)


def solution(mesh):
    placed = (
        P("resp", "head"),
        P("resp", "head"),
        P("resp", "head"),
        P("resp", "head"),
        P(None, "head"),
        P(None, "head"),
        P("resp"),
    )
    return jax.shard_map(
        functools.partial(body, mesh.shape["resp"], mesh.shape["head"]),
        mesh=mesh,
        in_specs=placed,
        out_specs=(P("resp", "head"), P("resp", "head"), P("resp", "head")),
        check_vma=False,
    )
```

```python
import functools

import jax
import jax.numpy as jnp
from jax import lax
from jax.experimental import pallas as pl
from jax.experimental.pallas import tpu as pltpu
from jax.sharding import PartitionSpec as P

HD = 128
LEN = 256
NT = (((1,), (1,)), ((), ()))
CHUNK = 16
LOG2E = 1.4426950408889634


def join_kernel(k_hbm, v_hbm, out_ref, both_ref, sems):
    width = k_hbm.shape[1]
    copies = [
        pltpu.make_async_copy(k_hbm, both_ref.at[:, pl.ds(0, width)], sems.at[0]),
        pltpu.make_async_copy(v_hbm, both_ref.at[:, pl.ds(width, width)], sems.at[1]),
    ]
    for copy in copies:
        copy.start()
    for copy in copies:
        copy.wait()
    both = both_ref[...]
    for i in range(out_ref.shape[0]):
        out_ref[i] = both


def load_kernel(lengths_ref, *refs):
    count = (len(refs) - 2) // 2
    live_ref, sems = refs[2 * count :]
    copies = [
        pltpu.make_async_copy(refs[i], refs[count + i], sems.at[i]) for i in range(count)
    ]
    for copy in copies:
        copy.start()
    position = lax.broadcasted_iota(jnp.int32, live_ref.shape[1:], 1)
    for part in range(live_ref.shape[0]):
        live_ref[part] = jnp.where(position < lengths_ref[part], 1.0, 0.0)
    for copy in copies:
        copy.wait()


def attention_kernel(live_ref, kv_ref, q_ref, g_ref, out_ref, blocks_ref, products_ref, weights_ref):
    scale = HD ** (-0.5)
    tokens = kv_ref.shape[0]
    width = kv_ref.shape[1] // 2
    kv_local = width // HD
    parts = q_ref.shape[0] // LEN
    group = q_ref.shape[1] // HD // kv_local
    units = [
        (k, part, h) for k in range(kv_local) for part in range(parts) for h in range(group)
    ]
    blocks_ref[...] = jnp.zeros_like(blocks_ref)
    for k in range(kv_local):
        blocks_ref[k, :tokens, :HD] = kv_ref[:, k * HD : (k + 1) * HD]
        blocks_ref[k, tokens:, HD:] = kv_ref[:, width + k * HD : width + (k + 1) * HD]

    def beside(left_ref, right_ref, unit):
        k, part, h = unit
        at = (k * group + h) * HD
        rows = slice(part * LEN, (part + 1) * LEN)
        return jnp.concatenate(
            [left_ref[rows, at : at + HD], right_ref[rows, at : at + HD]], axis=1
        )

    def spread(row):
        return jnp.broadcast_to(row, (CHUNK, LEN))

    tops, factors, deltas = {}, {}, {}
    for step in range(len(units) + 3):
        largest, summing, last = step - 1, step - 2, step - 3
        if step < len(units):
            products_ref[step % 4] = lax.dot_general(
                blocks_ref[units[step][0]],
                beside(q_ref, g_ref, units[step]),
                NT,
                preferred_element_type=jnp.float32,
            )
        top = total = weighted = None
        for at in range(0, tokens, CHUNK):
            score_rows = slice(at, at + CHUNK)
            dprob_rows = slice(tokens + at, tokens + at + CHUNK)
            if 0 <= largest < len(units):
                scores = products_ref[largest % 4, score_rows]
                top = scores if top is None else jnp.maximum(top, scores)
            if 0 <= summing < len(units):
                scores = products_ref[summing % 4, score_rows]
                dprobs = products_ref[summing % 4, dprob_rows]
                expo = jnp.exp2((scores - tops[summing]) * (scale * LOG2E))
                total = expo if total is None else total + expo
                weighted = expo * dprobs if weighted is None else weighted + expo * dprobs
            if 0 <= last < len(units):
                k = units[last][0]
                cols = slice(last * LEN % weights_ref.shape[2], last * LEN % weights_ref.shape[2] + LEN)
                scores = products_ref[last % 4, score_rows]
                dprobs = products_ref[last % 4, dprob_rows]
                probs = jnp.exp2((scores - tops[last]) * (scale * LOG2E)) * factors[last]
                weights_ref[k, score_rows, cols] = probs.astype(jnp.bfloat16)
                weights_ref[k, dprob_rows, cols] = (probs * (dprobs - deltas[last])).astype(
                    jnp.bfloat16
                )
        if top is not None:
            tops[largest] = spread(jnp.max(top, axis=0, keepdims=True))
        if total is not None:
            inverse = 1.0 / jnp.sum(total, axis=0, keepdims=True)
            deltas[summing] = spread(jnp.sum(weighted, axis=0, keepdims=True) * inverse)
            factors[summing] = spread(inverse * live_ref[units[summing][1], :1])
        if last >= 0 and (last + 1 == len(units) or units[last + 1][0] != units[last][0]):
            k = units[last][0]
            rows = [beside(g_ref, q_ref, unit) for unit in units if unit[0] == k]
            out = jnp.dot(
                weights_ref[k], jnp.concatenate(rows, axis=0), preferred_element_type=jnp.float32
            )
            grad_k = out[tokens:, HD:] * scale
            grad_v = out[:tokens, :HD]
            out_ref[:, k * HD : (k + 1) * HD] = grad_k.astype(out_ref.dtype)
            out_ref[:, width + k * HD : width + (k + 1) * HD] = grad_v.astype(out_ref.dtype)


def project(low, kw_ref, vw_ref, owner, features):
    width = kw_ref.shape[1]
    rows = pl.ds(pl.multiple_of(owner * features, features), features)
    out = lax.dot_general(
        low[:, :width], kw_ref[rows, :], NT, preferred_element_type=jnp.float32
    )
    return out + lax.dot_general(
        low[:, width:], vw_ref[rows, :], NT, preferred_element_type=jnp.float32
    )


def first_projection_kernel(parts_ref, kw_ref, vw_ref, low_ref, out_ref):
    total = parts_ref[0].astype(jnp.float32)
    for i in range(1, parts_ref.shape[0]):
        total += parts_ref[i].astype(jnp.float32)
    low = total.astype(jnp.bfloat16)
    low_ref[...] = low
    me = lax.axis_index("head")
    out = project(low, kw_ref, vw_ref, me ^ 3, out_ref.shape[1])
    out_ref[...] = out.astype(out_ref.dtype)


def second_projection_kernel(low_ref, kw_ref, vw_ref, out_ref):
    me = lax.axis_index("head")
    out_ref[...] = project(low_ref[...], kw_ref, vw_ref, me ^ 2, out_ref.shape[1])


def last_projection_kernel(low_ref, kw_ref, vw_ref, after, out_ref, keep_ref, dk_ref, dv_ref):
    del after
    width = dk_ref.shape[1]
    low = low_ref[...]
    dk_ref[...] = low[:, :width]
    dv_ref[...] = low[:, width:]
    me = lax.axis_index("head")
    out = project(low, kw_ref, vw_ref, me ^ 1, out_ref.shape[1])
    out_ref[...] = out.astype(out_ref.dtype)
    keep_ref[...] = project(low, kw_ref, vw_ref, me, keep_ref.shape[1])


def swap(x, axis, count, bit):
    return lax.ppermute(x, axis, [(i, i ^ bit) for i in range(count)])


def body(resp, head, queries, d_out, prefix_keys, prefix_values, k_weight, v_weight, lengths):
    own, width = prefix_keys.shape
    features = k_weight.shape[0] // head
    vmem = pl.BlockSpec(memory_space=pltpu.VMEM)
    hbm = pl.BlockSpec(memory_space=pltpu.HBM)
    params = pltpu.CompilerParams(vmem_limit_bytes=12 << 20)

    def in_hbm(*xs):
        return [pltpu.with_memory_space_constraint(x, pltpu.HBM) for x in xs]

    both = pl.pallas_call(
        join_kernel,
        out_shape=jax.ShapeDtypeStruct((resp, own, 2 * width), jnp.bfloat16),
        in_specs=[hbm] * 2,
        out_specs=vmem,
        scratch_shapes=[
            pltpu.VMEM((own, 2 * width), jnp.bfloat16),
            pltpu.SemaphoreType.DMA((2,)),
        ],
        compiler_params=params,
        name="join",
    )(*in_hbm(prefix_keys, prefix_values))
    both = lax.all_to_all(both, "resp", 0, 0, tiled=True).reshape(resp * own, 2 * width)

    large = (queries, d_out)
    responses = lengths.shape[0]
    queries, d_out, live = pl.pallas_call(
        load_kernel,
        out_shape=[pltpu.VMEM(x.shape, x.dtype) for x in large]
        + [pltpu.VMEM((responses, 8, LEN), jnp.float32)],
        in_specs=[pl.BlockSpec(memory_space=pltpu.SMEM)] + [hbm] * len(large),
        out_specs=[vmem] * (len(large) + 1),
        scratch_shapes=[pltpu.SemaphoreType.DMA((len(large),))],
        compiler_params=params,
        cost_estimate=pl.CostEstimate(
            flops=0, transcendentals=0, bytes_accessed=sum(4 * x.size for x in large)
        ),
        name="load",
    )(lengths, *in_hbm(*large))

    tokens = resp * own
    kv_local = width // HD
    depth = queries.size // kv_local // HD
    partial = pl.pallas_call(
        attention_kernel,
        out_shape=pltpu.VMEM((tokens, 2 * width), jnp.bfloat16),
        in_specs=[vmem] * 4,
        out_specs=vmem,
        scratch_shapes=[
            pltpu.VMEM((kv_local, 2 * tokens, 2 * HD), jnp.bfloat16),
            pltpu.VMEM((4, 2 * tokens, LEN), jnp.float32),
            pltpu.VMEM((kv_local, 2 * tokens, depth), jnp.bfloat16),
        ],
        compiler_params=pltpu.CompilerParams(
            vmem_limit_bytes=(8 << 20) + 8 * kv_local * tokens * depth
        ),
        cost_estimate=pl.CostEstimate(
            flops=64 * kv_local * tokens * depth * HD,
            transcendentals=kv_local * tokens * depth,
            bytes_accessed=4 * queries.size + 6 * tokens * width,
        ),
        name="attention",
    )(live, both, queries, d_out)

    shares = lax.all_to_all(
        partial.reshape(resp, own, 2 * width), "resp", 0, 0, tiled=True
    )

    block = (own, features)
    low, to_core = pl.pallas_call(
        first_projection_kernel,
        out_shape=[
            pltpu.VMEM((own, 2 * width), jnp.bfloat16),
            pltpu.VMEM(block, jnp.bfloat16),
        ],
        in_specs=[vmem] * 3,
        out_specs=[vmem] * 2,
        compiler_params=params,
        name="projection_other_core",
    )(shares, k_weight, v_weight)
    cost = pl.CostEstimate(
        flops=4 * own * width * features, transcendentals=0, bytes_accessed=4 * width * features
    )
    far = pl.pallas_call(
        second_projection_kernel,
        out_shape=pltpu.VMEM(block, jnp.float32),
        in_specs=[vmem] * 3,
        out_specs=vmem,
        compiler_params=params,
        cost_estimate=cost,
        name="projection_other_y",
    )(low, k_weight, v_weight)
    far = (far + swap(to_core, "head", head, 1).astype(jnp.float32)).astype(jnp.bfloat16)
    got = swap(far, "head", head, 2)
    to_core, total, dk_low, dv_low = pl.pallas_call(
        last_projection_kernel,
        out_shape=[
            pltpu.VMEM(block, jnp.bfloat16),
            pltpu.VMEM(block, jnp.float32),
            jax.ShapeDtypeStruct((own, width), jnp.bfloat16),
            jax.ShapeDtypeStruct((own, width), jnp.bfloat16),
        ],
        in_specs=[vmem] * 3 + [pl.BlockSpec(memory_space=pl.ANY)],
        out_specs=[vmem] * 4,
        compiler_params=params,
        cost_estimate=cost,
        name="projection_this_y",
    )(low, k_weight, v_weight, far)
    total = lax.optimization_barrier(total + got.astype(jnp.float32))
    total += swap(to_core, "head", head, 1).astype(jnp.float32)
    return dk_low, dv_low, total.astype(jnp.bfloat16)


def solution(mesh):
    placed = (
        P("resp", "head"),
        P("resp", "head"),
        P("resp", "head"),
        P("resp", "head"),
        P(None, "head"),
        P(None, "head"),
        P("resp"),
    )
    return jax.shard_map(
        functools.partial(body, mesh.shape["resp"], mesh.shape["head"]),
        mesh=mesh,
        in_specs=placed,
        out_specs=(P("resp", "head"), P("resp", "head"), P("resp", "head")),
        check_vma=False,
    )
```

```python
import functools

import jax
import jax.numpy as jnp
from jax import lax
from jax.experimental import pallas as pl
from jax.experimental.pallas import tpu as pltpu
from jax.sharding import PartitionSpec as P

HD = 128
LEN = 256
NT = (((1,), (1,)), ((), ()))
UNIT = 2
LOG2E = 1.4426950408889634


def mask_kernel(lengths_ref, live_ref):
    position = lax.broadcasted_iota(jnp.int32, live_ref.shape[1:], 1)
    for part in range(live_ref.shape[0]):
        live_ref[part] = jnp.where(position < lengths_ref[part], 1.0, 0.0)


def join_kernel(live_ref, k_ref, v_ref, out_ref):
    del live_ref
    width = k_ref.shape[1]
    for i in range(out_ref.shape[0]):
        out_ref[i, :, :width] = k_ref[...]
        out_ref[i, :, width:] = v_ref[...]


def attention_kernel(live_ref, kv_ref, q_ref, g_ref, out_ref, blocks_ref, weights_ref):
    scale = HD ** (-0.5)
    tokens = kv_ref.shape[0]
    width = kv_ref.shape[1] // 2
    kv_local = width // HD
    parts = q_ref.shape[0] // LEN
    group = q_ref.shape[1] // HD // kv_local
    units = [
        (k, part, h)
        for k in range(kv_local)
        for part in range(parts)
        for h in range(0, group, UNIT)
    ]

    def stack(ref, unit):
        k, part, h = unit
        heads = [
            ref[part * LEN : (part + 1) * LEN, at * HD : (at + 1) * HD]
            for at in range(k * group + h, k * group + h + UNIT)
        ]
        return jnp.concatenate(heads, axis=0)

    blocks_ref[...] = jnp.zeros_like(blocks_ref)
    for k in range(kv_local):
        blocks_ref[k, :tokens, :HD] = kv_ref[:, k * HD : (k + 1) * HD]
        blocks_ref[k, tokens:, HD:] = kv_ref[:, width + k * HD : width + (k + 1) * HD]

    def products(unit):
        both = jnp.concatenate([stack(q_ref, unit), stack(g_ref, unit)], axis=1)
        out = lax.dot_general(blocks_ref[unit[0]], both, NT, preferred_element_type=jnp.float32)
        return out[:tokens], out[tokens:]

    following = products(units[0])
    for i, unit in enumerate(units):
        k, part, h = unit
        scores, dprobs = following
        if i + 1 < len(units):
            following = products(units[i + 1])
        top = jnp.max(scores, axis=0, keepdims=True)
        expo = jnp.exp2((scores - top) * (scale * LOG2E))
        total = jnp.sum(expo, axis=0, keepdims=True)
        weighted = jnp.sum(expo * dprobs, axis=0, keepdims=True)
        inverse = 1.0 / total
        delta = weighted * inverse
        factor = inverse * jnp.concatenate([live_ref[part, :1]] * UNIT, axis=1)
        probs = expo * factor
        mine = [u for u in units if u[0] == k]
        cols = pl.ds(mine.index(unit) * UNIT * LEN, UNIT * LEN)
        weights_ref[k, :tokens, cols] = probs.astype(jnp.bfloat16)
        weights_ref[k, tokens:, cols] = (probs * (dprobs - delta)).astype(jnp.bfloat16)
        if unit == mine[-1]:
            rows = [
                jnp.concatenate([stack(g_ref, u), stack(q_ref, u)], axis=1) for u in mine
            ]
            out = jnp.dot(
                weights_ref[k], jnp.concatenate(rows, axis=0), preferred_element_type=jnp.float32
            )
            grad_k = out[tokens:, HD:] * scale
            out_ref[:, k * HD : (k + 1) * HD] = grad_k.astype(out_ref.dtype)
            out_ref[:, width + k * HD : width + (k + 1) * HD] = out[:tokens, :HD].astype(
                out_ref.dtype
            )


def project(low, kw_ref, vw_ref, owner, features):
    width = kw_ref.shape[1]
    rows = pl.ds(pl.multiple_of(owner * features, features), features)
    out = lax.dot_general(
        low[:, :width], kw_ref[rows, :], NT, preferred_element_type=jnp.float32
    )
    return out + lax.dot_general(
        low[:, width:], vw_ref[rows, :], NT, preferred_element_type=jnp.float32
    )


def first_projection_kernel(parts_ref, kw_ref, vw_ref, low_ref, out_ref):
    total = parts_ref[0].astype(jnp.float32)
    for i in range(1, parts_ref.shape[0]):
        total += parts_ref[i].astype(jnp.float32)
    low = total.astype(jnp.bfloat16)
    low_ref[...] = low
    me = lax.axis_index("head")
    out = project(low, kw_ref, vw_ref, me ^ 3, out_ref.shape[1])
    out_ref[...] = out.astype(out_ref.dtype)


def second_projection_kernel(low_ref, kw_ref, vw_ref, out_ref):
    me = lax.axis_index("head")
    out_ref[...] = project(low_ref[...], kw_ref, vw_ref, me ^ 2, out_ref.shape[1])


def last_projection_kernel(low_ref, kw_ref, vw_ref, after, out_ref, keep_ref, dk_ref, dv_ref):
    del after
    width = dk_ref.shape[1]
    low = low_ref[...]
    dk_ref[...] = low[:, :width]
    dv_ref[...] = low[:, width:]
    me = lax.axis_index("head")
    out = project(low, kw_ref, vw_ref, me ^ 1, out_ref.shape[1])
    out_ref[...] = out.astype(out_ref.dtype)
    keep_ref[...] = project(low, kw_ref, vw_ref, me, keep_ref.shape[1])


def swap(x, axis, count, bit):
    return lax.ppermute(x, axis, [(i, i ^ bit) for i in range(count)])


def body(resp, head, queries, d_out, prefix_keys, prefix_values, k_weight, v_weight, lengths):
    own, width = prefix_keys.shape
    features = k_weight.shape[0] // head
    vmem = pl.BlockSpec(memory_space=pltpu.VMEM)
    params = pltpu.CompilerParams(vmem_limit_bytes=12 << 20)

    live = pl.pallas_call(
        mask_kernel,
        out_shape=pltpu.VMEM((lengths.shape[0], 8, LEN), jnp.float32),
        in_specs=[pl.BlockSpec(memory_space=pltpu.SMEM)],
        out_specs=vmem,
        compiler_params=params,
        cost_estimate=pl.CostEstimate(flops=1600000000, transcendentals=0, bytes_accessed=0),
        name="mask",
    )(lengths)
    both = pl.pallas_call(
        join_kernel,
        out_shape=pltpu.VMEM((resp, own, 2 * width), jnp.bfloat16),
        in_specs=[pl.BlockSpec(memory_space=pl.ANY)] + [vmem] * 2,
        out_specs=vmem,
        compiler_params=params,
        name="join",
    )(live, prefix_keys, prefix_values)
    both = lax.all_to_all(both, "resp", 0, 0, tiled=True).reshape(resp * own, 2 * width)

    tokens = resp * own
    kv_local = width // HD
    depth = queries.size // kv_local // HD
    partial = pl.pallas_call(
        attention_kernel,
        out_shape=pltpu.VMEM((tokens, 2 * width), jnp.bfloat16),
        in_specs=[vmem] * 4,
        out_specs=vmem,
        scratch_shapes=[
            pltpu.VMEM((kv_local, 2 * tokens, 2 * HD), jnp.bfloat16),
            pltpu.VMEM((kv_local, 2 * tokens, depth), jnp.bfloat16),
        ],
        compiler_params=pltpu.CompilerParams(
            vmem_limit_bytes=(8 << 20) + 8 * kv_local * tokens * depth
        ),
        cost_estimate=pl.CostEstimate(
            flops=64 * kv_local * tokens * depth * HD,
            transcendentals=kv_local * tokens * depth,
            bytes_accessed=4 * queries.size + 6 * tokens * width,
        ),
        name="attention",
    )(live, both, queries, d_out)

    shares = lax.all_to_all(
        partial.reshape(resp, own, 2 * width), "resp", 0, 0, tiled=True
    )

    block = (own, features)
    low, to_core = pl.pallas_call(
        first_projection_kernel,
        out_shape=[
            pltpu.VMEM((own, 2 * width), jnp.bfloat16),
            pltpu.VMEM(block, jnp.bfloat16),
        ],
        in_specs=[vmem] * 3,
        out_specs=[vmem] * 2,
        compiler_params=params,
        name="projection_other_core",
    )(shares, k_weight, v_weight)
    cost = pl.CostEstimate(
        flops=4 * own * width * features, transcendentals=0, bytes_accessed=4 * width * features
    )
    far = pl.pallas_call(
        second_projection_kernel,
        out_shape=pltpu.VMEM(block, jnp.float32),
        in_specs=[vmem] * 3,
        out_specs=vmem,
        compiler_params=params,
        cost_estimate=cost,
        name="projection_other_y",
    )(low, k_weight, v_weight)
    far = (far + swap(to_core, "head", head, 1).astype(jnp.float32)).astype(jnp.bfloat16)
    got = swap(far, "head", head, 2)
    to_core, total, dk_low, dv_low = pl.pallas_call(
        last_projection_kernel,
        out_shape=[
            pltpu.VMEM(block, jnp.bfloat16),
            pltpu.VMEM(block, jnp.float32),
            jax.ShapeDtypeStruct((own, width), jnp.bfloat16),
            jax.ShapeDtypeStruct((own, width), jnp.bfloat16),
        ],
        in_specs=[vmem] * 3 + [pl.BlockSpec(memory_space=pl.ANY)],
        out_specs=[vmem] * 4,
        compiler_params=params,
        cost_estimate=cost,
        name="projection_this_y",
    )(low, k_weight, v_weight, far)
    total = lax.optimization_barrier(total + got.astype(jnp.float32))
    total += swap(to_core, "head", head, 1).astype(jnp.float32)
    return dk_low, dv_low, total.astype(jnp.bfloat16)


def solution(mesh):
    placed = (
        P("resp", "head"),
        P("resp", "head"),
        P("resp", "head"),
        P("resp", "head"),
        P(None, "head"),
        P(None, "head"),
        P("resp"),
    )
    return jax.shard_map(
        functools.partial(body, mesh.shape["resp"], mesh.shape["head"]),
        mesh=mesh,
        in_specs=placed,
        out_specs=(P("resp", "head"), P("resp", "head"), P("resp", "head")),
        check_vma=False,
    )
```

```python
import functools

import jax
import jax.numpy as jnp
from jax import lax
from jax.experimental import pallas as pl
from jax.experimental.pallas import tpu as pltpu
from jax.sharding import PartitionSpec as P

HD = 128
LEN = 256
NT = (((1,), (1,)), ((), ()))
UNIT = 4
LOG2E = 1.4426950408889634


def mask_kernel(lengths_ref, live_ref):
    position = lax.broadcasted_iota(jnp.int32, live_ref.shape[1:], 1)
    for part in range(live_ref.shape[0]):
        live_ref[part] = jnp.where(position < lengths_ref[part], 1.0, 0.0)


def join_kernel(live_ref, k_ref, v_ref, out_ref):
    del live_ref
    width = k_ref.shape[1]
    for i in range(out_ref.shape[0]):
        out_ref[i, :, :width] = k_ref[...]
        out_ref[i, :, width:] = v_ref[...]


def attention_kernel(live_ref, kv_ref, q_ref, g_ref, out_ref, blocks_ref, weights_ref):
    scale = HD ** (-0.5)
    tokens = kv_ref.shape[0]
    width = kv_ref.shape[1] // 2
    kv_local = width // HD
    parts = q_ref.shape[0] // LEN
    group = q_ref.shape[1] // HD // kv_local
    units = [
        (k, part, h)
        for k in range(kv_local)
        for part in range(parts)
        for h in range(0, group, UNIT)
    ]

    def stack(ref, unit):
        k, part, h = unit
        heads = [
            ref[part * LEN : (part + 1) * LEN, at * HD : (at + 1) * HD]
            for at in range(k * group + h, k * group + h + UNIT)
        ]
        return jnp.concatenate(heads, axis=0)

    blocks_ref[...] = jnp.zeros_like(blocks_ref)
    for k in range(kv_local):
        blocks_ref[k, :tokens, :HD] = kv_ref[:, k * HD : (k + 1) * HD]
        blocks_ref[k, tokens:, HD:] = kv_ref[:, width + k * HD : width + (k + 1) * HD]

    def products(unit):
        both = jnp.concatenate([stack(q_ref, unit), stack(g_ref, unit)], axis=1)
        out = lax.dot_general(blocks_ref[unit[0]], both, NT, preferred_element_type=jnp.float32)
        return out[:tokens], out[tokens:]

    following = products(units[0])
    for i, unit in enumerate(units):
        k, part, h = unit
        scores, dprobs = following
        if i + 1 < len(units):
            following = products(units[i + 1])
        top = jnp.max(scores, axis=0, keepdims=True)
        expo = jnp.exp2((scores - top) * (scale * LOG2E))
        total = jnp.sum(expo, axis=0, keepdims=True)
        weighted = jnp.sum(expo * dprobs, axis=0, keepdims=True)
        inverse = 1.0 / total
        delta = weighted * inverse
        factor = inverse * jnp.concatenate([live_ref[part, :1]] * UNIT, axis=1)
        probs = expo * factor
        mine = [u for u in units if u[0] == k]
        cols = pl.ds(mine.index(unit) * UNIT * LEN, UNIT * LEN)
        weights_ref[k, :tokens, cols] = probs.astype(jnp.bfloat16)
        weights_ref[k, tokens:, cols] = (probs * (dprobs - delta)).astype(jnp.bfloat16)
        if unit == mine[-1]:
            rows = [
                jnp.concatenate([stack(g_ref, u), stack(q_ref, u)], axis=1) for u in mine
            ]
            out = jnp.dot(
                weights_ref[k], jnp.concatenate(rows, axis=0), preferred_element_type=jnp.float32
            )
            grad_k = out[tokens:, HD:] * scale
            out_ref[:, k * HD : (k + 1) * HD] = grad_k.astype(out_ref.dtype)
            out_ref[:, width + k * HD : width + (k + 1) * HD] = out[:tokens, :HD].astype(
                out_ref.dtype
            )


def project(low, kw_ref, vw_ref, owner, features):
    width = kw_ref.shape[1]
    rows = pl.ds(pl.multiple_of(owner * features, features), features)
    out = lax.dot_general(
        low[:, :width], kw_ref[rows, :], NT, preferred_element_type=jnp.float32
    )
    return out + lax.dot_general(
        low[:, width:], vw_ref[rows, :], NT, preferred_element_type=jnp.float32
    )


def first_projection_kernel(parts_ref, kw_ref, vw_ref, low_ref, out_ref):
    total = parts_ref[0].astype(jnp.float32)
    for i in range(1, parts_ref.shape[0]):
        total += parts_ref[i].astype(jnp.float32)
    low = total.astype(jnp.bfloat16)
    low_ref[...] = low
    me = lax.axis_index("head")
    out = project(low, kw_ref, vw_ref, me ^ 3, out_ref.shape[1])
    out_ref[...] = out.astype(out_ref.dtype)


def second_projection_kernel(low_ref, kw_ref, vw_ref, out_ref):
    me = lax.axis_index("head")
    out_ref[...] = project(low_ref[...], kw_ref, vw_ref, me ^ 2, out_ref.shape[1])


def last_projection_kernel(low_ref, kw_ref, vw_ref, after, out_ref, keep_ref, dk_ref, dv_ref):
    del after
    width = dk_ref.shape[1]
    low = low_ref[...]
    dk_ref[...] = low[:, :width]
    dv_ref[...] = low[:, width:]
    me = lax.axis_index("head")
    out = project(low, kw_ref, vw_ref, me ^ 1, out_ref.shape[1])
    out_ref[...] = out.astype(out_ref.dtype)
    keep_ref[...] = project(low, kw_ref, vw_ref, me, keep_ref.shape[1])


def swap(x, axis, count, bit):
    return lax.ppermute(x, axis, [(i, i ^ bit) for i in range(count)])


def body(resp, head, queries, d_out, prefix_keys, prefix_values, k_weight, v_weight, lengths):
    own, width = prefix_keys.shape
    features = k_weight.shape[0] // head
    vmem = pl.BlockSpec(memory_space=pltpu.VMEM)
    params = pltpu.CompilerParams(vmem_limit_bytes=12 << 20)

    live = pl.pallas_call(
        mask_kernel,
        out_shape=pltpu.VMEM((lengths.shape[0], 8, LEN), jnp.float32),
        in_specs=[pl.BlockSpec(memory_space=pltpu.SMEM)],
        out_specs=vmem,
        compiler_params=params,
        cost_estimate=pl.CostEstimate(flops=1600000000, transcendentals=0, bytes_accessed=0),
        name="mask",
    )(lengths)
    both = pl.pallas_call(
        join_kernel,
        out_shape=pltpu.VMEM((resp, own, 2 * width), jnp.bfloat16),
        in_specs=[pl.BlockSpec(memory_space=pl.ANY)] + [vmem] * 2,
        out_specs=vmem,
        compiler_params=params,
        name="join",
    )(live, prefix_keys, prefix_values)
    both = lax.all_to_all(both, "resp", 0, 0, tiled=True).reshape(resp * own, 2 * width)

    tokens = resp * own
    kv_local = width // HD
    depth = queries.size // kv_local // HD
    partial = pl.pallas_call(
        attention_kernel,
        out_shape=pltpu.VMEM((tokens, 2 * width), jnp.bfloat16),
        in_specs=[vmem] * 4,
        out_specs=vmem,
        scratch_shapes=[
            pltpu.VMEM((kv_local, 2 * tokens, 2 * HD), jnp.bfloat16),
            pltpu.VMEM((kv_local, 2 * tokens, depth), jnp.bfloat16),
        ],
        compiler_params=pltpu.CompilerParams(
            vmem_limit_bytes=(8 << 20) + 8 * kv_local * tokens * depth
        ),
        cost_estimate=pl.CostEstimate(
            flops=32 * kv_local * tokens * depth * HD,
            transcendentals=kv_local * tokens * depth,
            bytes_accessed=4 * queries.size + 6 * tokens * width,
        ),
        name="attention",
    )(live, both, queries, d_out)

    shares = lax.all_to_all(
        partial.reshape(resp, own, 2 * width), "resp", 0, 0, tiled=True
    )

    block = (own, features)
    low, to_core = pl.pallas_call(
        first_projection_kernel,
        out_shape=[
            pltpu.VMEM((own, 2 * width), jnp.bfloat16),
            pltpu.VMEM(block, jnp.bfloat16),
        ],
        in_specs=[vmem] * 3,
        out_specs=[vmem] * 2,
        compiler_params=params,
        name="projection_other_core",
    )(shares, k_weight, v_weight)
    cost = pl.CostEstimate(
        flops=4 * own * width * features, transcendentals=0, bytes_accessed=4 * width * features
    )
    far = pl.pallas_call(
        second_projection_kernel,
        out_shape=pltpu.VMEM(block, jnp.float32),
        in_specs=[vmem] * 3,
        out_specs=vmem,
        compiler_params=params,
        cost_estimate=cost,
        name="projection_other_y",
    )(low, k_weight, v_weight)
    far = (far + swap(to_core, "head", head, 1).astype(jnp.float32)).astype(jnp.bfloat16)
    got = swap(far, "head", head, 2)
    to_core, total, dk_low, dv_low = pl.pallas_call(
        last_projection_kernel,
        out_shape=[
            pltpu.VMEM(block, jnp.bfloat16),
            pltpu.VMEM(block, jnp.float32),
            jax.ShapeDtypeStruct((own, width), jnp.bfloat16),
            jax.ShapeDtypeStruct((own, width), jnp.bfloat16),
        ],
        in_specs=[vmem] * 3 + [pl.BlockSpec(memory_space=pl.ANY)],
        out_specs=[vmem] * 4,
        compiler_params=params,
        cost_estimate=cost,
        name="projection_this_y",
    )(low, k_weight, v_weight, far)
    total = lax.optimization_barrier(total + got.astype(jnp.float32))
    total += swap(to_core, "head", head, 1).astype(jnp.float32)
    return dk_low, dv_low, total.astype(jnp.bfloat16)


def solution(mesh):
    placed = (
        P("resp", "head"),
        P("resp", "head"),
        P("resp", "head"),
        P("resp", "head"),
        P(None, "head"),
        P(None, "head"),
        P("resp"),
    )
    return jax.shard_map(
        functools.partial(body, mesh.shape["resp"], mesh.shape["head"]),
        mesh=mesh,
        in_specs=placed,
        out_specs=(P("resp", "head"), P("resp", "head"), P("resp", "head")),
        check_vma=False,
    )
```

```python
import functools

import jax
import jax.numpy as jnp
from jax import lax
from jax.experimental import pallas as pl
from jax.experimental.pallas import tpu as pltpu
from jax.sharding import PartitionSpec as P

HD = 128
LEN = 256
NT = (((1,), (1,)), ((), ()))
LOG2E = 1.4426950408889634


def mask_kernel(lengths_ref, live_ref):
    position = lax.broadcasted_iota(jnp.int32, live_ref.shape[1:], 0)
    for part in range(live_ref.shape[0]):
        live_ref[part] = jnp.where(position < lengths_ref[part], 1.0, 0.0)


def join_kernel(live_ref, k_ref, v_ref, out_ref):
    del live_ref
    width = k_ref.shape[1]
    for i in range(out_ref.shape[0]):
        out_ref[i, :, :width] = k_ref[...]
        out_ref[i, :, width:] = v_ref[...]


def attention_kernel(live_ref, kv_ref, q_ref, g_ref, out_ref, blocks_ref, weights_ref):
    scale = HD ** (-0.5)
    tokens = kv_ref.shape[0]
    width = kv_ref.shape[1] // 2
    kv_local = width // HD
    parts = q_ref.shape[0] // LEN
    group = q_ref.shape[1] // HD // kv_local
    blocks_ref[...] = jnp.zeros_like(blocks_ref)
    for k in range(kv_local):
        blocks_ref[k, :tokens, :HD] = kv_ref[:, k * HD : (k + 1) * HD]
        blocks_ref[k, tokens:, HD:] = kv_ref[:, width + k * HD : width + (k + 1) * HD]

    def beside(left_ref, right_ref, unit):
        k, part, h = unit
        at = (k * group + h) * HD
        rows = slice(part * LEN, (part + 1) * LEN)
        return jnp.concatenate(
            [left_ref[rows, at : at + HD], right_ref[rows, at : at + HD]], axis=1
        )

    def products(unit):
        return lax.dot_general(
            beside(q_ref, g_ref, unit),
            blocks_ref[unit[0]],
            NT,
            preferred_element_type=jnp.float32,
        )

    units = [
        (k, part, h) for k in range(kv_local) for part in range(parts) for h in range(group)
    ]
    following = products(units[0])
    for i, unit in enumerate(units):
        k, part, h = unit
        scores, dprobs = following[:, :tokens], following[:, tokens:]
        if i + 1 < len(units):
            following = products(units[i + 1])
        top = jnp.max(scores, axis=1, keepdims=True)
        expo = jnp.exp2((scores - top) * (scale * LOG2E))
        total = jnp.sum(expo, axis=1, keepdims=True)
        weighted = jnp.sum(expo * dprobs, axis=1, keepdims=True)
        inverse = 1.0 / total
        delta = weighted * inverse
        factor = inverse * live_ref[part][:, :1]
        probs = expo * factor
        mine = [u for u in units if u[0] == k]
        at = mine.index(unit) * LEN
        weights_ref[k, at : at + LEN, :tokens] = probs.astype(jnp.bfloat16)
        weights_ref[k, at : at + LEN, tokens:] = (probs * (dprobs - delta)).astype(jnp.bfloat16)
        if unit == mine[-1]:
            rows = jnp.concatenate([beside(g_ref, q_ref, u) for u in mine], axis=0)
            out = lax.dot_general(
                rows,
                weights_ref[k],
                (((0,), (0,)), ((), ())),
                preferred_element_type=jnp.float32,
            )
            grad_v = out[:HD, :tokens].T
            grad_k = out[HD:, tokens:].T * scale
            out_ref[:, k * HD : (k + 1) * HD] = grad_k.astype(out_ref.dtype)
            out_ref[:, width + k * HD : width + (k + 1) * HD] = grad_v.astype(out_ref.dtype)


def project(low, kw_ref, vw_ref, owner, features):
    width = kw_ref.shape[1]
    rows = pl.ds(pl.multiple_of(owner * features, features), features)
    out = lax.dot_general(
        low[:, :width], kw_ref[rows, :], NT, preferred_element_type=jnp.float32
    )
    return out + lax.dot_general(
        low[:, width:], vw_ref[rows, :], NT, preferred_element_type=jnp.float32
    )


def first_projection_kernel(parts_ref, kw_ref, vw_ref, low_ref, out_ref):
    total = parts_ref[0].astype(jnp.float32)
    for i in range(1, parts_ref.shape[0]):
        total += parts_ref[i].astype(jnp.float32)
    low = total.astype(jnp.bfloat16)
    low_ref[...] = low
    me = lax.axis_index("head")
    out = project(low, kw_ref, vw_ref, me ^ 3, out_ref.shape[1])
    out_ref[...] = out.astype(out_ref.dtype)


def second_projection_kernel(low_ref, kw_ref, vw_ref, out_ref):
    me = lax.axis_index("head")
    out_ref[...] = project(low_ref[...], kw_ref, vw_ref, me ^ 2, out_ref.shape[1])


def last_projection_kernel(low_ref, kw_ref, vw_ref, after, out_ref, keep_ref, dk_ref, dv_ref):
    del after
    width = dk_ref.shape[1]
    low = low_ref[...]
    dk_ref[...] = low[:, :width]
    dv_ref[...] = low[:, width:]
    me = lax.axis_index("head")
    out = project(low, kw_ref, vw_ref, me ^ 1, out_ref.shape[1])
    out_ref[...] = out.astype(out_ref.dtype)
    keep_ref[...] = project(low, kw_ref, vw_ref, me, keep_ref.shape[1])


def swap(x, axis, count, bit):
    return lax.ppermute(x, axis, [(i, i ^ bit) for i in range(count)])


def body(resp, head, queries, d_out, prefix_keys, prefix_values, k_weight, v_weight, lengths):
    own, width = prefix_keys.shape
    features = k_weight.shape[0] // head
    vmem = pl.BlockSpec(memory_space=pltpu.VMEM)
    params = pltpu.CompilerParams(vmem_limit_bytes=12 << 20)

    live = pl.pallas_call(
        mask_kernel,
        out_shape=pltpu.VMEM((lengths.shape[0], LEN, 128), jnp.float32),
        in_specs=[pl.BlockSpec(memory_space=pltpu.SMEM)],
        out_specs=vmem,
        compiler_params=params,
        cost_estimate=pl.CostEstimate(flops=1600000000, transcendentals=0, bytes_accessed=0),
        name="mask",
    )(lengths)
    both = pl.pallas_call(
        join_kernel,
        out_shape=pltpu.VMEM((resp, own, 2 * width), jnp.bfloat16),
        in_specs=[pl.BlockSpec(memory_space=pl.ANY)] + [vmem] * 2,
        out_specs=vmem,
        compiler_params=params,
        name="join",
    )(live, prefix_keys, prefix_values)
    both = lax.all_to_all(both, "resp", 0, 0, tiled=True).reshape(resp * own, 2 * width)

    tokens = resp * own
    kv_local = width // HD
    depth = queries.size // kv_local // HD
    partial = pl.pallas_call(
        attention_kernel,
        out_shape=pltpu.VMEM((tokens, 2 * width), jnp.bfloat16),
        in_specs=[vmem] * 4,
        out_specs=vmem,
        scratch_shapes=[
            pltpu.VMEM((kv_local, 2 * tokens, 2 * HD), jnp.bfloat16),
            pltpu.VMEM((kv_local, depth, 2 * tokens), jnp.bfloat16),
        ],
        compiler_params=pltpu.CompilerParams(
            vmem_limit_bytes=(8 << 20) + 8 * kv_local * tokens * depth
        ),
        cost_estimate=pl.CostEstimate(
            flops=64 * kv_local * tokens * depth * HD,
            transcendentals=kv_local * tokens * depth,
            bytes_accessed=4 * queries.size + 6 * tokens * width,
        ),
        name="attention",
    )(live, both, queries, d_out)

    shares = lax.all_to_all(
        partial.reshape(resp, own, 2 * width), "resp", 0, 0, tiled=True
    )

    block = (own, features)
    low, to_core = pl.pallas_call(
        first_projection_kernel,
        out_shape=[
            pltpu.VMEM((own, 2 * width), jnp.bfloat16),
            pltpu.VMEM(block, jnp.bfloat16),
        ],
        in_specs=[vmem] * 3,
        out_specs=[vmem] * 2,
        compiler_params=params,
        name="projection_other_core",
    )(shares, k_weight, v_weight)
    cost = pl.CostEstimate(
        flops=4 * own * width * features, transcendentals=0, bytes_accessed=4 * width * features
    )
    far = pl.pallas_call(
        second_projection_kernel,
        out_shape=pltpu.VMEM(block, jnp.float32),
        in_specs=[vmem] * 3,
        out_specs=vmem,
        compiler_params=params,
        cost_estimate=cost,
        name="projection_other_y",
    )(low, k_weight, v_weight)
    far = (far + swap(to_core, "head", head, 1).astype(jnp.float32)).astype(jnp.bfloat16)
    got = swap(far, "head", head, 2)
    to_core, total, dk_low, dv_low = pl.pallas_call(
        last_projection_kernel,
        out_shape=[
            pltpu.VMEM(block, jnp.bfloat16),
            pltpu.VMEM(block, jnp.float32),
            jax.ShapeDtypeStruct((own, width), jnp.bfloat16),
            jax.ShapeDtypeStruct((own, width), jnp.bfloat16),
        ],
        in_specs=[vmem] * 3 + [pl.BlockSpec(memory_space=pl.ANY)],
        out_specs=[vmem] * 4,
        compiler_params=params,
        cost_estimate=cost,
        name="projection_this_y",
    )(low, k_weight, v_weight, far)
    total = lax.optimization_barrier(total + got.astype(jnp.float32))
    total += swap(to_core, "head", head, 1).astype(jnp.float32)
    return dk_low, dv_low, total.astype(jnp.bfloat16)


def solution(mesh):
    placed = (
        P("resp", "head"),
        P("resp", "head"),
        P("resp", "head"),
        P("resp", "head"),
        P(None, "head"),
        P(None, "head"),
        P("resp"),
    )
    return jax.shard_map(
        functools.partial(body, mesh.shape["resp"], mesh.shape["head"]),
        mesh=mesh,
        in_specs=placed,
        out_specs=(P("resp", "head"), P("resp", "head"), P("resp", "head")),
        check_vma=False,
    )
```

```python
import functools

import jax
import jax.numpy as jnp
from jax import lax
from jax.experimental import pallas as pl
from jax.experimental.pallas import tpu as pltpu
from jax.sharding import PartitionSpec as P

HD = 128
LEN = 256
NT = (((1,), (1,)), ((), ()))
UNIT = 2
LOG2E = 1.4426950408889634


def mask_kernel(lengths_ref, live_ref):
    position = lax.broadcasted_iota(jnp.int32, live_ref.shape[1:], 1)
    for part in range(live_ref.shape[0]):
        live_ref[part] = jnp.where(position < lengths_ref[part], 1.0, 0.0)


def join_kernel(live_ref, k_ref, v_ref, out_ref):
    del live_ref
    width = k_ref.shape[1]
    for i in range(out_ref.shape[0]):
        out_ref[i, :, :width] = k_ref[...]
        out_ref[i, :, width:] = v_ref[...]


def attention_kernel(live_ref, kv_ref, q_ref, g_ref, out_ref, blocks_ref, weights_ref):
    scale = HD ** (-0.5)
    tokens = kv_ref.shape[0]
    width = kv_ref.shape[1] // 2
    kv_local = width // HD
    parts = q_ref.shape[0] // LEN
    group = q_ref.shape[1] // HD // kv_local
    units = [
        (k, part, h)
        for k in range(kv_local)
        for part in range(parts)
        for h in range(0, group, UNIT)
    ]

    def stack(ref, unit):
        k, part, h = unit
        heads = [
            ref[part * LEN : (part + 1) * LEN, at * HD : (at + 1) * HD]
            for at in range(k * group + h, k * group + h + UNIT)
        ]
        return jnp.concatenate(heads, axis=0)

    blocks_ref[...] = jnp.zeros_like(blocks_ref)
    for k in range(kv_local):
        blocks_ref[k, :tokens, :HD] = kv_ref[:, k * HD : (k + 1) * HD]
        blocks_ref[k, tokens:, HD:] = kv_ref[:, width + k * HD : width + (k + 1) * HD]

    def products(unit):
        both = jnp.concatenate([stack(q_ref, unit), stack(g_ref, unit)], axis=1)
        out = lax.dot_general(blocks_ref[unit[0]], both, NT, preferred_element_type=jnp.float32)
        return out[:tokens], out[tokens:]

    following = products(units[0])
    for i, unit in enumerate(units):
        k, part, h = unit
        scores, dprobs = following
        if i + 1 < len(units):
            following = products(units[i + 1])
        top = jnp.max(scores, axis=0, keepdims=True)
        expo = jnp.exp2((scores - top) * (scale * LOG2E))
        total = jnp.sum(expo, axis=0, keepdims=True)
        weighted = jnp.sum(expo * dprobs, axis=0, keepdims=True)
        inverse = 1.0 / total
        delta = weighted * inverse
        factor = inverse * jnp.concatenate([live_ref[part, :1]] * UNIT, axis=1)
        probs = expo * factor
        mine = [u for u in units if u[0] == k]
        cols = pl.ds(mine.index(unit) * UNIT * LEN, UNIT * LEN)
        weights_ref[k, :tokens, cols] = probs.astype(jnp.bfloat16)
        weights_ref[k, tokens:, cols] = (probs * (dprobs - delta)).astype(jnp.bfloat16)
        if unit == mine[-1]:
            rows = [
                jnp.concatenate([stack(g_ref, u), stack(q_ref, u)], axis=1) for u in mine
            ]
            out = jnp.dot(
                weights_ref[k], jnp.concatenate(rows, axis=0), preferred_element_type=jnp.float32
            )
            grad_k = out[tokens:, HD:] * scale
            out_ref[:, k * HD : (k + 1) * HD] = grad_k.astype(out_ref.dtype)
            out_ref[:, width + k * HD : width + (k + 1) * HD] = out[:tokens, :HD].astype(
                out_ref.dtype
            )


def project(low, kw_ref, vw_ref, owner, features):
    width = kw_ref.shape[1]
    rows = pl.ds(pl.multiple_of(owner * features, features), features)
    out = lax.dot_general(
        low[:, :width], kw_ref[rows, :], NT, preferred_element_type=jnp.float32
    )
    return out + lax.dot_general(
        low[:, width:], vw_ref[rows, :], NT, preferred_element_type=jnp.float32
    )


def first_projection_kernel(parts_ref, kw_ref, vw_ref, low_ref, out_ref):
    total = parts_ref[0].astype(jnp.float32)
    for i in range(1, parts_ref.shape[0]):
        total += parts_ref[i].astype(jnp.float32)
    low = total.astype(jnp.bfloat16)
    low_ref[...] = low
    me = lax.axis_index("head")
    out = project(low, kw_ref, vw_ref, me ^ 3, out_ref.shape[1])
    out_ref[...] = out.astype(out_ref.dtype)


def second_projection_kernel(low_ref, kw_ref, vw_ref, out_ref):
    me = lax.axis_index("head")
    out_ref[...] = project(low_ref[...], kw_ref, vw_ref, me ^ 2, out_ref.shape[1])


def last_projection_kernel(low_ref, kw_ref, vw_ref, after, out_ref, keep_ref, dk_ref, dv_ref):
    del after
    width = dk_ref.shape[1]
    low = low_ref[...]
    dk_ref[...] = low[:, :width]
    dv_ref[...] = low[:, width:]
    me = lax.axis_index("head")
    out = project(low, kw_ref, vw_ref, me ^ 1, out_ref.shape[1])
    out_ref[...] = out.astype(out_ref.dtype)
    keep_ref[...] = project(low, kw_ref, vw_ref, me, keep_ref.shape[1])


def last_sum_kernel(total_ref, got_ref, out_ref):
    out_ref[...] = (total_ref[...] + got_ref[...].astype(jnp.float32)).astype(out_ref.dtype)


def swap(x, axis, count, bit):
    return lax.ppermute(x, axis, [(i, i ^ bit) for i in range(count)])


def body(resp, head, queries, d_out, prefix_keys, prefix_values, k_weight, v_weight, lengths):
    own, width = prefix_keys.shape
    features = k_weight.shape[0] // head
    vmem = pl.BlockSpec(memory_space=pltpu.VMEM)
    params = pltpu.CompilerParams(vmem_limit_bytes=12 << 20)

    live = pl.pallas_call(
        mask_kernel,
        out_shape=pltpu.VMEM((lengths.shape[0], 8, LEN), jnp.float32),
        in_specs=[pl.BlockSpec(memory_space=pltpu.SMEM)],
        out_specs=vmem,
        compiler_params=params,
        cost_estimate=pl.CostEstimate(flops=1600000000, transcendentals=0, bytes_accessed=0),
        name="mask",
    )(lengths)
    both = pl.pallas_call(
        join_kernel,
        out_shape=pltpu.VMEM((resp, own, 2 * width), jnp.bfloat16),
        in_specs=[pl.BlockSpec(memory_space=pl.ANY)] + [vmem] * 2,
        out_specs=vmem,
        compiler_params=params,
        name="join",
    )(live, prefix_keys, prefix_values)
    both = lax.all_to_all(both, "resp", 0, 0, tiled=True).reshape(resp * own, 2 * width)

    tokens = resp * own
    kv_local = width // HD
    depth = queries.size // kv_local // HD
    partial = pl.pallas_call(
        attention_kernel,
        out_shape=pltpu.VMEM((tokens, 2 * width), jnp.bfloat16),
        in_specs=[vmem] * 4,
        out_specs=vmem,
        scratch_shapes=[
            pltpu.VMEM((kv_local, 2 * tokens, 2 * HD), jnp.bfloat16),
            pltpu.VMEM((kv_local, 2 * tokens, depth), jnp.bfloat16),
        ],
        compiler_params=pltpu.CompilerParams(
            vmem_limit_bytes=(8 << 20) + 8 * kv_local * tokens * depth
        ),
        cost_estimate=pl.CostEstimate(
            flops=64 * kv_local * tokens * depth * HD,
            transcendentals=kv_local * tokens * depth,
            bytes_accessed=4 * queries.size + 6 * tokens * width,
        ),
        name="attention",
    )(live, both, queries, d_out)

    shares = lax.all_to_all(
        partial.reshape(resp, own, 2 * width), "resp", 0, 0, tiled=True
    )

    block = (own, features)
    low, to_core = pl.pallas_call(
        first_projection_kernel,
        out_shape=[
            pltpu.VMEM((own, 2 * width), jnp.bfloat16),
            pltpu.VMEM(block, jnp.bfloat16),
        ],
        in_specs=[vmem] * 3,
        out_specs=[vmem] * 2,
        compiler_params=params,
        name="projection_other_core",
    )(shares, k_weight, v_weight)
    cost = pl.CostEstimate(
        flops=4 * own * width * features, transcendentals=0, bytes_accessed=4 * width * features
    )
    far = pl.pallas_call(
        second_projection_kernel,
        out_shape=pltpu.VMEM(block, jnp.float32),
        in_specs=[vmem] * 3,
        out_specs=vmem,
        compiler_params=params,
        cost_estimate=cost,
        name="projection_other_y",
    )(low, k_weight, v_weight)
    far = (far + swap(to_core, "head", head, 1).astype(jnp.float32)).astype(jnp.bfloat16)
    got = swap(far, "head", head, 2)
    to_core, total, dk_low, dv_low = pl.pallas_call(
        last_projection_kernel,
        out_shape=[
            pltpu.VMEM(block, jnp.bfloat16),
            pltpu.VMEM(block, jnp.float32),
            jax.ShapeDtypeStruct((own, width), jnp.bfloat16),
            jax.ShapeDtypeStruct((own, width), jnp.bfloat16),
        ],
        in_specs=[vmem] * 3 + [pl.BlockSpec(memory_space=pl.ANY)],
        out_specs=[vmem] * 4,
        compiler_params=params,
        cost_estimate=cost,
        name="projection_this_y",
    )(low, k_weight, v_weight, far)
    total = lax.optimization_barrier(total + got.astype(jnp.float32))
    input_grad = pl.pallas_call(
        last_sum_kernel,
        out_shape=jax.ShapeDtypeStruct(block, jnp.bfloat16),
        in_specs=[vmem] * 2,
        out_specs=vmem,
        compiler_params=params,
        name="last_sum",
    )(total, swap(to_core, "head", head, 1))
    return dk_low, dv_low, input_grad


def solution(mesh):
    placed = (
        P("resp", "head"),
        P("resp", "head"),
        P("resp", "head"),
        P("resp", "head"),
        P(None, "head"),
        P(None, "head"),
        P("resp"),
    )
    return jax.shard_map(
        functools.partial(body, mesh.shape["resp"], mesh.shape["head"]),
        mesh=mesh,
        in_specs=placed,
        out_specs=(P("resp", "head"), P("resp", "head"), P("resp", "head")),
        check_vma=False,
    )
```

```python
import functools

import jax
import jax.numpy as jnp
from jax import lax
from jax.experimental import pallas as pl
from jax.experimental.pallas import tpu as pltpu
from jax.sharding import PartitionSpec as P

HD = 128
LEN = 256
NT = (((1,), (1,)), ((), ()))
UNIT = 2
LOG2E = 1.4426950408889634


def mask_kernel(lengths_ref, live_ref):
    position = lax.broadcasted_iota(jnp.int32, live_ref.shape[1:], 1)
    for part in range(live_ref.shape[0]):
        live_ref[part] = jnp.where(position < lengths_ref[part], 1.0, 0.0)


def join_kernel(live_ref, k_ref, v_ref, out_ref):
    del live_ref
    width = k_ref.shape[1]
    for i in range(out_ref.shape[0]):
        out_ref[i, :, :width] = k_ref[...]
        out_ref[i, :, width:] = v_ref[...]


def attention_kernel(live_ref, kv_ref, q_ref, g_ref, out_ref, blocks_ref, weights_ref):
    scale = HD ** (-0.5)
    tokens = kv_ref.shape[0]
    width = kv_ref.shape[1] // 2
    kv_local = width // HD
    parts = q_ref.shape[0] // LEN
    group = q_ref.shape[1] // HD // kv_local
    units = [
        (k, part, h)
        for k in range(kv_local)
        for part in range(parts)
        for h in range(0, group, UNIT)
    ]

    def stack(ref, unit):
        k, part, h = unit
        heads = [
            ref[part * LEN : (part + 1) * LEN, at * HD : (at + 1) * HD]
            for at in range(k * group + h, k * group + h + UNIT)
        ]
        return jnp.concatenate(heads, axis=0)

    blocks_ref[...] = jnp.zeros_like(blocks_ref)
    for k in range(kv_local):
        blocks_ref[k, :tokens, :HD] = kv_ref[:, k * HD : (k + 1) * HD]
        blocks_ref[k, tokens:, HD:] = kv_ref[:, width + k * HD : width + (k + 1) * HD]

    def products(unit):
        both = jnp.concatenate([stack(q_ref, unit), stack(g_ref, unit)], axis=1)
        out = lax.dot_general(blocks_ref[unit[0]], both, NT, preferred_element_type=jnp.float32)
        return out[:tokens], out[tokens:]

    following = products(units[0])
    for i, unit in enumerate(units):
        k, part, h = unit
        scores, dprobs = following
        if i + 1 < len(units):
            following = products(units[i + 1])
        top = jnp.max(scores, axis=0, keepdims=True)
        expo = jnp.exp2((scores - top) * (scale * LOG2E))
        total = jnp.sum(expo, axis=0, keepdims=True)
        weighted = jnp.sum(expo * dprobs, axis=0, keepdims=True)
        inverse = 1.0 / total
        delta = weighted * inverse
        factor = inverse * jnp.concatenate([live_ref[part, :1]] * UNIT, axis=1)
        probs = expo * factor
        mine = [u for u in units if u[0] == k]
        cols = pl.ds(mine.index(unit) * UNIT * LEN, UNIT * LEN)
        weights_ref[k, :tokens, cols] = probs.astype(jnp.bfloat16)
        weights_ref[k, tokens:, cols] = (probs * (dprobs - delta)).astype(jnp.bfloat16)
        if unit == mine[-1]:
            rows = [
                jnp.concatenate([stack(g_ref, u), stack(q_ref, u)], axis=1) for u in mine
            ]
            out = jnp.dot(
                weights_ref[k], jnp.concatenate(rows, axis=0), preferred_element_type=jnp.float32
            )
            grad_k = out[tokens:, HD:] * scale
            out_ref[:, k * HD : (k + 1) * HD] = grad_k.astype(out_ref.dtype)
            out_ref[:, width + k * HD : width + (k + 1) * HD] = out[:tokens, :HD].astype(
                out_ref.dtype
            )


def project(low, kw_ref, vw_ref, owner, features):
    width = kw_ref.shape[1]
    rows = pl.ds(pl.multiple_of(owner * features, features), features)
    out = lax.dot_general(
        low[:, :width], kw_ref[rows, :], NT, preferred_element_type=jnp.float32
    )
    return out + lax.dot_general(
        low[:, width:], vw_ref[rows, :], NT, preferred_element_type=jnp.float32
    )


def first_projection_kernel(keep_ref, got_ref, kw_ref, vw_ref, low_ref, out_ref):
    total = keep_ref[...] + got_ref[...].astype(jnp.float32)
    low = total.astype(jnp.bfloat16)
    low_ref[...] = low
    me = lax.axis_index("head")
    out = project(low, kw_ref, vw_ref, me ^ 3, out_ref.shape[1])
    out_ref[...] = out.astype(out_ref.dtype)


def second_projection_kernel(low_ref, kw_ref, vw_ref, out_ref):
    me = lax.axis_index("head")
    out_ref[...] = project(low_ref[...], kw_ref, vw_ref, me ^ 2, out_ref.shape[1])


def last_projection_kernel(low_ref, kw_ref, vw_ref, after, out_ref, keep_ref, dk_ref, dv_ref):
    del after
    width = dk_ref.shape[1]
    low = low_ref[...]
    dk_ref[...] = low[:, :width]
    dv_ref[...] = low[:, width:]
    me = lax.axis_index("head")
    out = project(low, kw_ref, vw_ref, me ^ 1, out_ref.shape[1])
    out_ref[...] = out.astype(out_ref.dtype)
    keep_ref[...] = project(low, kw_ref, vw_ref, me, keep_ref.shape[1])


def last_sum_kernel(total_ref, got_ref, out_ref):
    out_ref[...] = (total_ref[...] + got_ref[...].astype(jnp.float32)).astype(out_ref.dtype)


def swap(x, axis, count, bit):
    return lax.ppermute(x, axis, [(i, i ^ bit) for i in range(count)])


def body(resp, head, queries, d_out, prefix_keys, prefix_values, k_weight, v_weight, lengths):
    own, width = prefix_keys.shape
    features = k_weight.shape[0] // head
    vmem = pl.BlockSpec(memory_space=pltpu.VMEM)
    params = pltpu.CompilerParams(vmem_limit_bytes=12 << 20)

    live = pl.pallas_call(
        mask_kernel,
        out_shape=pltpu.VMEM((lengths.shape[0], 8, LEN), jnp.float32),
        in_specs=[pl.BlockSpec(memory_space=pltpu.SMEM)],
        out_specs=vmem,
        compiler_params=params,
        cost_estimate=pl.CostEstimate(flops=1600000000, transcendentals=0, bytes_accessed=0),
        name="mask",
    )(lengths)
    both = pl.pallas_call(
        join_kernel,
        out_shape=pltpu.VMEM((resp, own, 2 * width), jnp.bfloat16),
        in_specs=[pl.BlockSpec(memory_space=pl.ANY)] + [vmem] * 2,
        out_specs=vmem,
        compiler_params=params,
        name="join",
    )(live, prefix_keys, prefix_values)
    both = lax.all_to_all(both, "resp", 0, 0, tiled=True).reshape(resp * own, 2 * width)

    tokens = resp * own
    kv_local = width // HD
    depth = queries.size // kv_local // HD
    partial = pl.pallas_call(
        attention_kernel,
        out_shape=pltpu.VMEM((tokens, 2 * width), jnp.bfloat16),
        in_specs=[vmem] * 4,
        out_specs=vmem,
        scratch_shapes=[
            pltpu.VMEM((kv_local, 2 * tokens, 2 * HD), jnp.bfloat16),
            pltpu.VMEM((kv_local, 2 * tokens, depth), jnp.bfloat16),
        ],
        compiler_params=pltpu.CompilerParams(
            vmem_limit_bytes=(8 << 20) + 8 * kv_local * tokens * depth
        ),
        cost_estimate=pl.CostEstimate(
            flops=64 * kv_local * tokens * depth * HD,
            transcendentals=kv_local * tokens * depth,
            bytes_accessed=4 * queries.size + 6 * tokens * width,
        ),
        name="attention",
    )(live, both, queries, d_out)

    pairs = resp // 2
    shares = lax.all_to_all(
        partial.reshape(pairs, 2 * own, 2 * width),
        "resp",
        0,
        0,
        axis_index_groups=[list(range(i, resp, 2)) for i in range(2)],
        tiled=True,
    )
    total = jnp.sum(shares.astype(jnp.float32), axis=0)
    odd = (lax.axis_index("resp") & 1) == 1
    send = jnp.where(odd, total[:own], total[own:]).astype(jnp.bfloat16)
    keep = jnp.where(odd, total[own:], total[:own])
    got = swap(send, "resp", resp, 1)

    block = (own, features)
    low, to_core = pl.pallas_call(
        first_projection_kernel,
        out_shape=[
            pltpu.VMEM((own, 2 * width), jnp.bfloat16),
            pltpu.VMEM(block, jnp.bfloat16),
        ],
        in_specs=[vmem] * 4,
        out_specs=[vmem] * 2,
        compiler_params=params,
        name="projection_other_core",
    )(keep, got, k_weight, v_weight)
    cost = pl.CostEstimate(
        flops=4 * own * width * features, transcendentals=0, bytes_accessed=4 * width * features
    )
    far = pl.pallas_call(
        second_projection_kernel,
        out_shape=pltpu.VMEM(block, jnp.float32),
        in_specs=[vmem] * 3,
        out_specs=vmem,
        compiler_params=params,
        cost_estimate=cost,
        name="projection_other_y",
    )(low, k_weight, v_weight)
    far = (far + swap(to_core, "head", head, 1).astype(jnp.float32)).astype(jnp.bfloat16)
    got = swap(far, "head", head, 2)
    to_core, total, dk_low, dv_low = pl.pallas_call(
        last_projection_kernel,
        out_shape=[
            pltpu.VMEM(block, jnp.bfloat16),
            pltpu.VMEM(block, jnp.float32),
            jax.ShapeDtypeStruct((own, width), jnp.bfloat16),
            jax.ShapeDtypeStruct((own, width), jnp.bfloat16),
        ],
        in_specs=[vmem] * 3 + [pl.BlockSpec(memory_space=pl.ANY)],
        out_specs=[vmem] * 4,
        compiler_params=params,
        cost_estimate=cost,
        name="projection_this_y",
    )(low, k_weight, v_weight, far)
    total = lax.optimization_barrier(total + got.astype(jnp.float32))
    input_grad = pl.pallas_call(
        last_sum_kernel,
        out_shape=jax.ShapeDtypeStruct(block, jnp.bfloat16),
        in_specs=[vmem] * 2,
        out_specs=vmem,
        compiler_params=params,
        name="last_sum",
    )(total, swap(to_core, "head", head, 1))
    return dk_low, dv_low, input_grad


def solution(mesh):
    placed = (
        P("resp", "head"),
        P("resp", "head"),
        P("resp", "head"),
        P("resp", "head"),
        P(None, "head"),
        P(None, "head"),
        P("resp"),
    )
    return jax.shard_map(
        functools.partial(body, mesh.shape["resp"], mesh.shape["head"]),
        mesh=mesh,
        in_specs=placed,
        out_specs=(P("resp", "head"), P("resp", "head"), P("resp", "head")),
        check_vma=False,
    )
```

```python
import functools

import jax
import jax.numpy as jnp
from jax import lax
from jax.experimental import pallas as pl
from jax.experimental.pallas import tpu as pltpu
from jax.sharding import PartitionSpec as P

HD = 128
LEN = 256
NT = (((1,), (1,)), ((), ()))
UNIT = 2
LOG2E = 1.4426950408889634


def mask_kernel(lengths_ref, live_ref):
    position = lax.broadcasted_iota(jnp.int32, live_ref.shape[1:], 1)
    for part in range(live_ref.shape[0]):
        live_ref[part] = jnp.where(position < lengths_ref[part], 1.0, 0.0)


def join_kernel(live_ref, k_ref, v_ref, out_ref):
    del live_ref
    width = k_ref.shape[1]
    for i in range(out_ref.shape[0]):
        out_ref[i, :, :width] = k_ref[...]
        out_ref[i, :, width:] = v_ref[...]


def attention_kernel(live_ref, kv_ref, q_ref, g_ref, out_ref, probs_ref, dscores_ref):
    scale = HD ** (-0.5)
    width = kv_ref.shape[1] // 2
    kv_local = width // HD
    parts = q_ref.shape[0] // LEN
    group = q_ref.shape[1] // HD // kv_local
    units = [
        (k, part, h)
        for k in range(kv_local)
        for part in range(parts)
        for h in range(0, group, UNIT)
    ]

    def stack(ref, unit):
        k, part, h = unit
        heads = [
            ref[part * LEN : (part + 1) * LEN, at * HD : (at + 1) * HD]
            for at in range(k * group + h, k * group + h + UNIT)
        ]
        return jnp.concatenate(heads, axis=0)

    def products(unit):
        k = unit[0]
        keys = kv_ref[:, k * HD : (k + 1) * HD]
        values = kv_ref[:, width + k * HD : width + (k + 1) * HD]
        return (
            lax.dot_general(keys, stack(q_ref, unit), NT, preferred_element_type=jnp.float32),
            lax.dot_general(values, stack(g_ref, unit), NT, preferred_element_type=jnp.float32),
        )

    following = products(units[0])
    for i, unit in enumerate(units):
        k, part, h = unit
        scores, dprobs = following
        if i + 1 < len(units):
            following = products(units[i + 1])
        top = jnp.max(scores, axis=0, keepdims=True)
        expo = jnp.exp2((scores - top) * (scale * LOG2E))
        total = jnp.sum(expo, axis=0, keepdims=True)
        weighted = jnp.sum(expo * dprobs, axis=0, keepdims=True)
        inverse = 1.0 / total
        delta = weighted * inverse
        factor = inverse * jnp.concatenate([live_ref[part, :1]] * UNIT, axis=1)
        probs = expo * factor
        mine = [u for u in units if u[0] == k]
        cols = pl.ds(mine.index(unit) * UNIT * LEN, UNIT * LEN)
        probs_ref[k, :, cols] = probs.astype(jnp.bfloat16)
        dscores_ref[k, :, cols] = (probs * (dprobs - delta)).astype(jnp.bfloat16)
        if unit == mine[-1]:
            q_all = jnp.concatenate([stack(q_ref, u) for u in mine], axis=0)
            g_all = jnp.concatenate([stack(g_ref, u) for u in mine], axis=0)
            grad_k = jnp.dot(dscores_ref[k], q_all, preferred_element_type=jnp.float32) * scale
            grad_v = jnp.dot(probs_ref[k], g_all, preferred_element_type=jnp.float32)
            out_ref[:, k * HD : (k + 1) * HD] = grad_k.astype(out_ref.dtype)
            out_ref[:, width + k * HD : width + (k + 1) * HD] = grad_v.astype(out_ref.dtype)


def project(low, kw_ref, vw_ref, owner, features):
    width = kw_ref.shape[1]
    rows = pl.ds(pl.multiple_of(owner * features, features), features)
    out = lax.dot_general(
        low[:, :width], kw_ref[rows, :], NT, preferred_element_type=jnp.float32
    )
    return out + lax.dot_general(
        low[:, width:], vw_ref[rows, :], NT, preferred_element_type=jnp.float32
    )


def first_projection_kernel(parts_ref, kw_ref, vw_ref, low_ref, out_ref):
    total = parts_ref[0].astype(jnp.float32)
    for i in range(1, parts_ref.shape[0]):
        total += parts_ref[i].astype(jnp.float32)
    low = total.astype(jnp.bfloat16)
    low_ref[...] = low
    me = lax.axis_index("head")
    out = project(low, kw_ref, vw_ref, me ^ 3, out_ref.shape[1])
    out_ref[...] = out.astype(out_ref.dtype)


def second_projection_kernel(low_ref, kw_ref, vw_ref, out_ref):
    me = lax.axis_index("head")
    out_ref[...] = project(low_ref[...], kw_ref, vw_ref, me ^ 2, out_ref.shape[1])


def last_projection_kernel(low_ref, kw_ref, vw_ref, after, out_ref, keep_ref, dk_ref, dv_ref):
    del after
    width = dk_ref.shape[1]
    low = low_ref[...]
    dk_ref[...] = low[:, :width]
    dv_ref[...] = low[:, width:]
    me = lax.axis_index("head")
    out = project(low, kw_ref, vw_ref, me ^ 1, out_ref.shape[1])
    out_ref[...] = out.astype(out_ref.dtype)
    keep_ref[...] = project(low, kw_ref, vw_ref, me, keep_ref.shape[1])


def last_sum_kernel(total_ref, got_ref, out_ref):
    out_ref[...] = (total_ref[...] + got_ref[...].astype(jnp.float32)).astype(out_ref.dtype)


def swap(x, axis, count, bit):
    return lax.ppermute(x, axis, [(i, i ^ bit) for i in range(count)])


def body(resp, head, queries, d_out, prefix_keys, prefix_values, k_weight, v_weight, lengths):
    own, width = prefix_keys.shape
    features = k_weight.shape[0] // head
    vmem = pl.BlockSpec(memory_space=pltpu.VMEM)
    params = pltpu.CompilerParams(vmem_limit_bytes=12 << 20)

    live = pl.pallas_call(
        mask_kernel,
        out_shape=pltpu.VMEM((lengths.shape[0], 8, LEN), jnp.float32),
        in_specs=[pl.BlockSpec(memory_space=pltpu.SMEM)],
        out_specs=vmem,
        compiler_params=params,
        cost_estimate=pl.CostEstimate(flops=1600000000, transcendentals=0, bytes_accessed=0),
        name="mask",
    )(lengths)
    both = pl.pallas_call(
        join_kernel,
        out_shape=pltpu.VMEM((resp, own, 2 * width), jnp.bfloat16),
        in_specs=[pl.BlockSpec(memory_space=pl.ANY)] + [vmem] * 2,
        out_specs=vmem,
        compiler_params=params,
        cost_estimate=pl.CostEstimate(flops=1600000000, transcendentals=0, bytes_accessed=0),
        name="join",
    )(live, prefix_keys, prefix_values)
    both = lax.all_to_all(both, "resp", 0, 0, tiled=True).reshape(resp * own, 2 * width)

    tokens = resp * own
    kv_local = width // HD
    depth = queries.size // kv_local // HD
    partial = pl.pallas_call(
        attention_kernel,
        out_shape=pltpu.VMEM((tokens, 2 * width), jnp.bfloat16),
        in_specs=[vmem] * 4,
        out_specs=vmem,
        scratch_shapes=[
            pltpu.VMEM((kv_local, tokens, depth), jnp.bfloat16),
            pltpu.VMEM((kv_local, tokens, depth), jnp.bfloat16),
        ],
        compiler_params=pltpu.CompilerParams(
            vmem_limit_bytes=(8 << 20) + 8 * kv_local * tokens * depth
        ),
        cost_estimate=pl.CostEstimate(
            flops=64 * kv_local * tokens * depth * HD,
            transcendentals=kv_local * tokens * depth,
            bytes_accessed=4 * queries.size + 6 * tokens * width,
        ),
        name="attention",
    )(live, both, queries, d_out)

    shares = lax.all_to_all(
        partial.reshape(resp, own, 2 * width), "resp", 0, 0, tiled=True
    )

    block = (own, features)
    low, to_core = pl.pallas_call(
        first_projection_kernel,
        out_shape=[
            pltpu.VMEM((own, 2 * width), jnp.bfloat16),
            pltpu.VMEM(block, jnp.bfloat16),
        ],
        in_specs=[vmem] * 3,
        out_specs=[vmem] * 2,
        compiler_params=params,
        name="projection_other_core",
    )(shares, k_weight, v_weight)
    cost = pl.CostEstimate(
        flops=4 * own * width * features, transcendentals=0, bytes_accessed=4 * width * features
    )
    far = pl.pallas_call(
        second_projection_kernel,
        out_shape=pltpu.VMEM(block, jnp.float32),
        in_specs=[vmem] * 3,
        out_specs=vmem,
        compiler_params=params,
        cost_estimate=cost,
        name="projection_other_y",
    )(low, k_weight, v_weight)
    far = (far + swap(to_core, "head", head, 1).astype(jnp.float32)).astype(jnp.bfloat16)
    got = swap(far, "head", head, 2)
    to_core, total, dk_low, dv_low = pl.pallas_call(
        last_projection_kernel,
        out_shape=[
            pltpu.VMEM(block, jnp.bfloat16),
            pltpu.VMEM(block, jnp.float32),
            jax.ShapeDtypeStruct((own, width), jnp.bfloat16),
            jax.ShapeDtypeStruct((own, width), jnp.bfloat16),
        ],
        in_specs=[vmem] * 3 + [pl.BlockSpec(memory_space=pl.ANY)],
        out_specs=[vmem] * 4,
        compiler_params=params,
        cost_estimate=cost,
        name="projection_this_y",
    )(low, k_weight, v_weight, far)
    total = lax.optimization_barrier(total + got.astype(jnp.float32))
    input_grad = pl.pallas_call(
        last_sum_kernel,
        out_shape=jax.ShapeDtypeStruct(block, jnp.bfloat16),
        in_specs=[vmem] * 2,
        out_specs=vmem,
        compiler_params=params,
        name="last_sum",
    )(total, swap(to_core, "head", head, 1))
    return dk_low, dv_low, input_grad


def solution(mesh):
    placed = (
        P("resp", "head"),
        P("resp", "head"),
        P("resp", "head"),
        P("resp", "head"),
        P(None, "head"),
        P(None, "head"),
        P("resp"),
    )
    return jax.shard_map(
        functools.partial(body, mesh.shape["resp"], mesh.shape["head"]),
        mesh=mesh,
        in_specs=placed,
        out_specs=(P("resp", "head"), P("resp", "head"), P("resp", "head")),
        check_vma=False,
    )
```

```python
import functools

import jax
import jax.numpy as jnp
from jax import lax
from jax.experimental import pallas as pl
from jax.experimental.pallas import tpu as pltpu
from jax.sharding import PartitionSpec as P

HD = 128
LEN = 256
NT = (((1,), (1,)), ((), ()))
UNIT = 2
LOG2E = 1.4426950408889634


def mask_kernel(lengths_ref, live_ref):
    position = lax.broadcasted_iota(jnp.int32, live_ref.shape[1:], 1)
    for part in range(live_ref.shape[0]):
        live_ref[part] = jnp.where(position < lengths_ref[part], 1.0, 0.0)


def join_kernel(live_ref, k_ref, v_ref, out_ref):
    del live_ref
    width = k_ref.shape[1]
    for i in range(out_ref.shape[0]):
        out_ref[i, :, :width] = k_ref[...]
        out_ref[i, :, width:] = v_ref[...]


def attention_kernel(live_ref, kv_ref, q_ref, g_ref, out_ref, blocks_ref, weights_ref):
    scale = HD ** (-0.5)
    tokens = kv_ref.shape[0]
    width = kv_ref.shape[1] // 2
    kv_local = width // HD
    parts = q_ref.shape[0] // LEN
    group = q_ref.shape[1] // HD // kv_local
    units = [
        (k, part, h)
        for k in range(kv_local)
        for part in range(parts)
        for h in range(0, group, UNIT)
    ]

    def stack(ref, unit):
        k, part, h = unit
        heads = [
            ref[part * LEN : (part + 1) * LEN, at * HD : (at + 1) * HD]
            for at in range(k * group + h, k * group + h + UNIT)
        ]
        return jnp.concatenate(heads, axis=0)

    blocks_ref[...] = jnp.zeros_like(blocks_ref)
    for k in range(kv_local):
        blocks_ref[k, :tokens, :HD] = kv_ref[:, k * HD : (k + 1) * HD]
        blocks_ref[k, tokens:, HD:] = kv_ref[:, width + k * HD : width + (k + 1) * HD]

    def products(unit):
        both = jnp.concatenate([stack(q_ref, unit), stack(g_ref, unit)], axis=1)
        out = lax.dot_general(blocks_ref[unit[0]], both, NT, preferred_element_type=jnp.float32)
        return out[:tokens], out[tokens:]

    following = products(units[0])
    for i, unit in enumerate(units):
        k, part, h = unit
        scores, dprobs = following
        if i + 1 < len(units):
            following = products(units[i + 1])
        top = jnp.max(scores, axis=0, keepdims=True)
        expo = jnp.exp2((scores - top) * (scale * LOG2E))
        total = jnp.sum(expo, axis=0, keepdims=True)
        weighted = jnp.sum(expo * dprobs, axis=0, keepdims=True)
        inverse = 1.0 / total
        delta = weighted * inverse
        factor = inverse * jnp.concatenate([live_ref[part, :1]] * UNIT, axis=1)
        probs = expo * factor
        mine = [u for u in units if u[0] == k]
        cols = pl.ds(mine.index(unit) * UNIT * LEN, UNIT * LEN)
        weights_ref[k, :tokens, cols] = probs.astype(jnp.bfloat16)
        weights_ref[k, tokens:, cols] = (probs * (dprobs - delta)).astype(jnp.bfloat16)
        if unit == mine[-1]:
            rows = [
                jnp.concatenate([stack(g_ref, u), stack(q_ref, u)], axis=1) for u in mine
            ]
            out = jnp.dot(
                weights_ref[k], jnp.concatenate(rows, axis=0), preferred_element_type=jnp.float32
            )
            grad_k = out[tokens:, HD:] * scale
            out_ref[:, k * HD : (k + 1) * HD] = grad_k.astype(out_ref.dtype)
            out_ref[:, width + k * HD : width + (k + 1) * HD] = out[:tokens, :HD].astype(
                out_ref.dtype
            )


def project(low, kw_ref, vw_ref, owner, features):
    rows = pl.ds(pl.multiple_of(owner * features, features), features)
    weights = jnp.concatenate([kw_ref[rows, :], vw_ref[rows, :]], axis=1)
    return lax.dot_general(low, weights, NT, preferred_element_type=jnp.float32)


def first_projection_kernel(parts_ref, kw_ref, vw_ref, low_ref, out_ref):
    total = parts_ref[0].astype(jnp.float32)
    for i in range(1, parts_ref.shape[0]):
        total += parts_ref[i].astype(jnp.float32)
    low = total.astype(jnp.bfloat16)
    low_ref[...] = low
    me = lax.axis_index("head")
    out = project(low, kw_ref, vw_ref, me ^ 3, out_ref.shape[1])
    out_ref[...] = out.astype(out_ref.dtype)


def second_projection_kernel(low_ref, kw_ref, vw_ref, out_ref):
    me = lax.axis_index("head")
    out_ref[...] = project(low_ref[...], kw_ref, vw_ref, me ^ 2, out_ref.shape[1])


def last_projection_kernel(low_ref, kw_ref, vw_ref, after, out_ref, keep_ref, dk_ref, dv_ref):
    del after
    width = dk_ref.shape[1]
    low = low_ref[...]
    dk_ref[...] = low[:, :width]
    dv_ref[...] = low[:, width:]
    me = lax.axis_index("head")
    out = project(low, kw_ref, vw_ref, me ^ 1, out_ref.shape[1])
    out_ref[...] = out.astype(out_ref.dtype)
    keep_ref[...] = project(low, kw_ref, vw_ref, me, keep_ref.shape[1])


def last_sum_kernel(total_ref, got_ref, out_ref):
    out_ref[...] = (total_ref[...] + got_ref[...].astype(jnp.float32)).astype(out_ref.dtype)


def swap(x, axis, count, bit):
    return lax.ppermute(x, axis, [(i, i ^ bit) for i in range(count)])


def body(resp, head, queries, d_out, prefix_keys, prefix_values, k_weight, v_weight, lengths):
    own, width = prefix_keys.shape
    features = k_weight.shape[0] // head
    vmem = pl.BlockSpec(memory_space=pltpu.VMEM)
    params = pltpu.CompilerParams(vmem_limit_bytes=12 << 20)

    live = pl.pallas_call(
        mask_kernel,
        out_shape=pltpu.VMEM((lengths.shape[0], 8, LEN), jnp.float32),
        in_specs=[pl.BlockSpec(memory_space=pltpu.SMEM)],
        out_specs=vmem,
        compiler_params=params,
        cost_estimate=pl.CostEstimate(flops=1600000000, transcendentals=0, bytes_accessed=0),
        name="mask",
    )(lengths)
    both = pl.pallas_call(
        join_kernel,
        out_shape=pltpu.VMEM((resp, own, 2 * width), jnp.bfloat16),
        in_specs=[pl.BlockSpec(memory_space=pl.ANY)] + [vmem] * 2,
        out_specs=vmem,
        compiler_params=params,
        name="join",
    )(live, prefix_keys, prefix_values)
    both = lax.all_to_all(both, "resp", 0, 0, tiled=True).reshape(resp * own, 2 * width)

    tokens = resp * own
    kv_local = width // HD
    depth = queries.size // kv_local // HD
    partial = pl.pallas_call(
        attention_kernel,
        out_shape=pltpu.VMEM((tokens, 2 * width), jnp.bfloat16),
        in_specs=[vmem] * 4,
        out_specs=vmem,
        scratch_shapes=[
            pltpu.VMEM((kv_local, 2 * tokens, 2 * HD), jnp.bfloat16),
            pltpu.VMEM((kv_local, 2 * tokens, depth), jnp.bfloat16),
        ],
        compiler_params=pltpu.CompilerParams(
            vmem_limit_bytes=(8 << 20) + 8 * kv_local * tokens * depth
        ),
        cost_estimate=pl.CostEstimate(
            flops=64 * kv_local * tokens * depth * HD,
            transcendentals=kv_local * tokens * depth,
            bytes_accessed=4 * queries.size + 6 * tokens * width,
        ),
        name="attention",
    )(live, both, queries, d_out)

    shares = lax.all_to_all(
        partial.reshape(resp, own, 2 * width), "resp", 0, 0, tiled=True
    )

    block = (own, features)
    low, to_core = pl.pallas_call(
        first_projection_kernel,
        out_shape=[
            pltpu.VMEM((own, 2 * width), jnp.bfloat16),
            pltpu.VMEM(block, jnp.bfloat16),
        ],
        in_specs=[vmem] * 3,
        out_specs=[vmem] * 2,
        compiler_params=params,
        name="projection_other_core",
    )(shares, k_weight, v_weight)
    cost = pl.CostEstimate(
        flops=4 * own * width * features, transcendentals=0, bytes_accessed=4 * width * features
    )
    far = pl.pallas_call(
        second_projection_kernel,
        out_shape=pltpu.VMEM(block, jnp.float32),
        in_specs=[vmem] * 3,
        out_specs=vmem,
        compiler_params=params,
        cost_estimate=cost,
        name="projection_other_y",
    )(low, k_weight, v_weight)
    far = (far + swap(to_core, "head", head, 1).astype(jnp.float32)).astype(jnp.bfloat16)
    got = swap(far, "head", head, 2)
    to_core, total, dk_low, dv_low = pl.pallas_call(
        last_projection_kernel,
        out_shape=[
            pltpu.VMEM(block, jnp.bfloat16),
            pltpu.VMEM(block, jnp.float32),
            jax.ShapeDtypeStruct((own, width), jnp.bfloat16),
            jax.ShapeDtypeStruct((own, width), jnp.bfloat16),
        ],
        in_specs=[vmem] * 3 + [pl.BlockSpec(memory_space=pl.ANY)],
        out_specs=[vmem] * 4,
        compiler_params=params,
        cost_estimate=cost,
        name="projection_this_y",
    )(low, k_weight, v_weight, far)
    total = lax.optimization_barrier(total + got.astype(jnp.float32))
    input_grad = pl.pallas_call(
        last_sum_kernel,
        out_shape=jax.ShapeDtypeStruct(block, jnp.bfloat16),
        in_specs=[vmem] * 2,
        out_specs=vmem,
        compiler_params=params,
        name="last_sum",
    )(total, swap(to_core, "head", head, 1))
    return dk_low, dv_low, input_grad


def solution(mesh):
    placed = (
        P("resp", "head"),
        P("resp", "head"),
        P("resp", "head"),
        P("resp", "head"),
        P(None, "head"),
        P(None, "head"),
        P("resp"),
    )
    return jax.shard_map(
        functools.partial(body, mesh.shape["resp"], mesh.shape["head"]),
        mesh=mesh,
        in_specs=placed,
        out_specs=(P("resp", "head"), P("resp", "head"), P("resp", "head")),
        check_vma=False,
    )
```

```python
import functools

import jax
import jax.numpy as jnp
from jax import lax
from jax.experimental import pallas as pl
from jax.experimental.pallas import tpu as pltpu
from jax.sharding import PartitionSpec as P

HD = 128
LEN = 256
NT = (((1,), (1,)), ((), ()))
UNIT = 1
LOG2E = 1.4426950408889634


def mask_kernel(lengths_ref, live_ref):
    position = lax.broadcasted_iota(jnp.int32, live_ref.shape[1:], 1)
    for part in range(live_ref.shape[0]):
        live_ref[part] = jnp.where(position < lengths_ref[part], 1.0, 0.0)


def join_kernel(live_ref, k_ref, v_ref, out_ref):
    del live_ref
    width = k_ref.shape[1]
    for i in range(out_ref.shape[0]):
        out_ref[i, :, :width] = k_ref[...]
        out_ref[i, :, width:] = v_ref[...]


def attention_kernel(live_ref, kv_ref, q_ref, g_ref, out_ref, blocks_ref, weights_ref):
    scale = HD ** (-0.5)
    tokens = kv_ref.shape[0]
    width = kv_ref.shape[1] // 2
    kv_local = width // HD
    parts = q_ref.shape[0] // LEN
    group = q_ref.shape[1] // HD // kv_local
    units = [
        (k, part, h)
        for k in range(kv_local)
        for part in range(parts)
        for h in range(0, group, UNIT)
    ]

    def stack(ref, unit):
        k, part, h = unit
        heads = [
            ref[part * LEN : (part + 1) * LEN, at * HD : (at + 1) * HD]
            for at in range(k * group + h, k * group + h + UNIT)
        ]
        return jnp.concatenate(heads, axis=0)

    blocks_ref[...] = jnp.zeros_like(blocks_ref)
    for k in range(kv_local):
        blocks_ref[k, :tokens, :HD] = kv_ref[:, k * HD : (k + 1) * HD]
        blocks_ref[k, tokens:, HD:] = kv_ref[:, width + k * HD : width + (k + 1) * HD]

    def products(unit):
        both = jnp.concatenate([stack(q_ref, unit), stack(g_ref, unit)], axis=1)
        out = lax.dot_general(blocks_ref[unit[0]], both, NT, preferred_element_type=jnp.float32)
        return out[:tokens], out[tokens:]

    following = products(units[0])
    for i, unit in enumerate(units):
        k, part, h = unit
        scores, dprobs = following
        if i + 1 < len(units):
            following = products(units[i + 1])
        top = jnp.max(scores, axis=0, keepdims=True)
        expo = jnp.exp2((scores - top) * (scale * LOG2E))
        total = jnp.sum(expo, axis=0, keepdims=True)
        weighted = jnp.sum(expo * dprobs, axis=0, keepdims=True)
        inverse = 1.0 / total
        delta = weighted * inverse
        factor = inverse * jnp.concatenate([live_ref[part, :1]] * UNIT, axis=1)
        probs = expo * factor
        mine = [u for u in units if u[0] == k]
        cols = pl.ds(mine.index(unit) * UNIT * LEN, UNIT * LEN)
        weights_ref[k, :tokens, cols] = probs.astype(jnp.bfloat16)
        weights_ref[k, tokens:, cols] = (probs * (dprobs - delta)).astype(jnp.bfloat16)
        if unit == mine[-1]:
            rows = [
                jnp.concatenate([stack(g_ref, u), stack(q_ref, u)], axis=1) for u in mine
            ]
            out = jnp.dot(
                weights_ref[k], jnp.concatenate(rows, axis=0), preferred_element_type=jnp.float32
            )
            grad_k = out[tokens:, HD:] * scale
            out_ref[:, k * HD : (k + 1) * HD] = grad_k.astype(out_ref.dtype)
            out_ref[:, width + k * HD : width + (k + 1) * HD] = out[:tokens, :HD].astype(
                out_ref.dtype
            )


def project(low, kw_ref, vw_ref, owner, features):
    rows = pl.ds(pl.multiple_of(owner * features, features), features)
    weights = jnp.concatenate([kw_ref[rows, :], vw_ref[rows, :]], axis=1)
    return lax.dot_general(low, weights, NT, preferred_element_type=jnp.float32)


def first_projection_kernel(parts_ref, kw_ref, vw_ref, low_ref, out_ref):
    total = parts_ref[0].astype(jnp.float32)
    for i in range(1, parts_ref.shape[0]):
        total += parts_ref[i].astype(jnp.float32)
    low = total.astype(jnp.bfloat16)
    low_ref[...] = low
    me = lax.axis_index("head")
    out = project(low, kw_ref, vw_ref, me ^ 3, out_ref.shape[1])
    out_ref[...] = out.astype(out_ref.dtype)


def second_projection_kernel(low_ref, kw_ref, vw_ref, out_ref):
    me = lax.axis_index("head")
    out_ref[...] = project(low_ref[...], kw_ref, vw_ref, me ^ 2, out_ref.shape[1])


def last_projection_kernel(low_ref, kw_ref, vw_ref, after, out_ref, keep_ref, dk_ref, dv_ref):
    del after
    width = dk_ref.shape[1]
    low = low_ref[...]
    dk_ref[...] = low[:, :width]
    dv_ref[...] = low[:, width:]
    me = lax.axis_index("head")
    out = project(low, kw_ref, vw_ref, me ^ 1, out_ref.shape[1])
    out_ref[...] = out.astype(out_ref.dtype)
    keep_ref[...] = project(low, kw_ref, vw_ref, me, keep_ref.shape[1])


def last_sum_kernel(total_ref, got_ref, out_ref):
    out_ref[...] = (total_ref[...] + got_ref[...].astype(jnp.float32)).astype(out_ref.dtype)


def swap(x, axis, count, bit):
    return lax.ppermute(x, axis, [(i, i ^ bit) for i in range(count)])


def body(resp, head, queries, d_out, prefix_keys, prefix_values, k_weight, v_weight, lengths):
    own, width = prefix_keys.shape
    features = k_weight.shape[0] // head
    vmem = pl.BlockSpec(memory_space=pltpu.VMEM)
    params = pltpu.CompilerParams(vmem_limit_bytes=12 << 20)

    live = pl.pallas_call(
        mask_kernel,
        out_shape=pltpu.VMEM((lengths.shape[0], 8, LEN), jnp.float32),
        in_specs=[pl.BlockSpec(memory_space=pltpu.SMEM)],
        out_specs=vmem,
        compiler_params=params,
        cost_estimate=pl.CostEstimate(flops=1600000000, transcendentals=0, bytes_accessed=0),
        name="mask",
    )(lengths)
    both = pl.pallas_call(
        join_kernel,
        out_shape=pltpu.VMEM((resp, own, 2 * width), jnp.bfloat16),
        in_specs=[pl.BlockSpec(memory_space=pl.ANY)] + [vmem] * 2,
        out_specs=vmem,
        compiler_params=params,
        name="join",
    )(live, prefix_keys, prefix_values)
    both = lax.all_to_all(both, "resp", 0, 0, tiled=True).reshape(resp * own, 2 * width)

    tokens = resp * own
    kv_local = width // HD
    depth = queries.size // kv_local // HD
    partial = pl.pallas_call(
        attention_kernel,
        out_shape=pltpu.VMEM((tokens, 2 * width), jnp.bfloat16),
        in_specs=[vmem] * 4,
        out_specs=vmem,
        scratch_shapes=[
            pltpu.VMEM((kv_local, 2 * tokens, 2 * HD), jnp.bfloat16),
            pltpu.VMEM((kv_local, 2 * tokens, depth), jnp.bfloat16),
        ],
        compiler_params=pltpu.CompilerParams(
            vmem_limit_bytes=(8 << 20) + 8 * kv_local * tokens * depth
        ),
        cost_estimate=pl.CostEstimate(
            flops=64 * kv_local * tokens * depth * HD,
            transcendentals=kv_local * tokens * depth,
            bytes_accessed=4 * queries.size + 6 * tokens * width,
        ),
        name="attention",
    )(live, both, queries, d_out)

    shares = lax.all_to_all(
        partial.reshape(resp, own, 2 * width), "resp", 0, 0, tiled=True
    )

    block = (own, features)
    low, to_core = pl.pallas_call(
        first_projection_kernel,
        out_shape=[
            pltpu.VMEM((own, 2 * width), jnp.bfloat16),
            pltpu.VMEM(block, jnp.bfloat16),
        ],
        in_specs=[vmem] * 3,
        out_specs=[vmem] * 2,
        compiler_params=params,
        name="projection_other_core",
    )(shares, k_weight, v_weight)
    cost = pl.CostEstimate(
        flops=4 * own * width * features, transcendentals=0, bytes_accessed=4 * width * features
    )
    far = pl.pallas_call(
        second_projection_kernel,
        out_shape=pltpu.VMEM(block, jnp.float32),
        in_specs=[vmem] * 3,
        out_specs=vmem,
        compiler_params=params,
        cost_estimate=cost,
        name="projection_other_y",
    )(low, k_weight, v_weight)
    far = (far + swap(to_core, "head", head, 1).astype(jnp.float32)).astype(jnp.bfloat16)
    got = swap(far, "head", head, 2)
    to_core, total, dk_low, dv_low = pl.pallas_call(
        last_projection_kernel,
        out_shape=[
            pltpu.VMEM(block, jnp.bfloat16),
            pltpu.VMEM(block, jnp.float32),
            jax.ShapeDtypeStruct((own, width), jnp.bfloat16),
            jax.ShapeDtypeStruct((own, width), jnp.bfloat16),
        ],
        in_specs=[vmem] * 3 + [pl.BlockSpec(memory_space=pl.ANY)],
        out_specs=[vmem] * 4,
        compiler_params=params,
        cost_estimate=cost,
        name="projection_this_y",
    )(low, k_weight, v_weight, far)
    total = lax.optimization_barrier(total + got.astype(jnp.float32))
    input_grad = pl.pallas_call(
        last_sum_kernel,
        out_shape=jax.ShapeDtypeStruct(block, jnp.bfloat16),
        in_specs=[vmem] * 2,
        out_specs=vmem,
        compiler_params=params,
        name="last_sum",
    )(total, swap(to_core, "head", head, 1))
    return dk_low, dv_low, input_grad


def solution(mesh):
    placed = (
        P("resp", "head"),
        P("resp", "head"),
        P("resp", "head"),
        P("resp", "head"),
        P(None, "head"),
        P(None, "head"),
        P("resp"),
    )
    return jax.shard_map(
        functools.partial(body, mesh.shape["resp"], mesh.shape["head"]),
        mesh=mesh,
        in_specs=placed,
        out_specs=(P("resp", "head"), P("resp", "head"), P("resp", "head")),
        check_vma=False,
    )
```

```python
import functools

import jax
import jax.numpy as jnp
from jax import lax
from jax.experimental import pallas as pl
from jax.experimental.pallas import tpu as pltpu
from jax.sharding import PartitionSpec as P

HD = 128
LEN = 256
NT = (((1,), (1,)), ((), ()))
UNIT = 2
LOG2E = 1.4426950408889634


def mask_kernel(lengths_ref, live_ref):
    position = lax.broadcasted_iota(jnp.int32, live_ref.shape[1:], 1)
    for part in range(live_ref.shape[0]):
        live_ref[part] = jnp.where(position < lengths_ref[part], 1.0, 0.0)


def join_kernel(live_ref, k_ref, v_ref, out_ref):
    del live_ref
    width = k_ref.shape[1]
    for i in range(out_ref.shape[0]):
        out_ref[i, :, :width] = k_ref[...]
        out_ref[i, :, width:] = v_ref[...]


def attention_kernel(live_ref, kv_ref, q_ref, g_ref, out_ref, blocks_ref, weights_ref):
    scale = HD ** (-0.5)
    tokens = kv_ref.shape[0]
    width = kv_ref.shape[1] // 2
    kv_local = width // HD
    parts = q_ref.shape[0] // LEN
    group = q_ref.shape[1] // HD // kv_local
    units = [
        (k, part, h)
        for k in range(kv_local)
        for part in range(parts)
        for h in range(0, group, UNIT)
    ]

    def stack(ref, unit):
        k, part, h = unit
        heads = [
            ref[part * LEN : (part + 1) * LEN, at * HD : (at + 1) * HD]
            for at in range(k * group + h, k * group + h + UNIT)
        ]
        return jnp.concatenate(heads, axis=0)

    blocks_ref[...] = jnp.zeros_like(blocks_ref)
    for k in range(kv_local):
        blocks_ref[k, :tokens, :HD] = kv_ref[:, k * HD : (k + 1) * HD]
        blocks_ref[k, tokens:, HD:] = kv_ref[:, width + k * HD : width + (k + 1) * HD]

    def products(unit):
        both = jnp.concatenate([stack(q_ref, unit), stack(g_ref, unit)], axis=1)
        out = lax.dot_general(blocks_ref[unit[0]], both, NT, preferred_element_type=jnp.float32)
        scores = out[:tokens]
        return scores, out[tokens:], jnp.max(scores, axis=0, keepdims=True)

    def sums(scores, dprobs, top):
        expo = jnp.exp2((scores - top) * (scale * LOG2E))
        total = jnp.sum(expo, axis=0, keepdims=True)
        weighted = jnp.sum(expo * dprobs, axis=0, keepdims=True)
        return expo, dprobs, total, weighted

    def write(unit, expo, dprobs, total, weighted):
        k, part, h = unit
        inverse = 1.0 / total
        delta = weighted * inverse
        factor = inverse * jnp.concatenate([live_ref[part, :1]] * UNIT, axis=1)
        probs = expo * factor
        mine = [u for u in units if u[0] == k]
        cols = pl.ds(mine.index(unit) * UNIT * LEN, UNIT * LEN)
        weights_ref[k, :tokens, cols] = probs.astype(jnp.bfloat16)
        weights_ref[k, tokens:, cols] = (probs * (dprobs - delta)).astype(jnp.bfloat16)
        if unit == mine[-1]:
            rows = [
                jnp.concatenate([stack(g_ref, u), stack(q_ref, u)], axis=1) for u in mine
            ]
            out = jnp.dot(
                weights_ref[k], jnp.concatenate(rows, axis=0), preferred_element_type=jnp.float32
            )
            grad_k = out[tokens:, HD:] * scale
            out_ref[:, k * HD : (k + 1) * HD] = grad_k.astype(out_ref.dtype)
            out_ref[:, width + k * HD : width + (k + 1) * HD] = out[:tokens, :HD].astype(
                out_ref.dtype
            )

    made, summed = {0: products(units[0])}, {}
    for i in range(len(units)):
        if i + 1 < len(units):
            made[i + 1] = products(units[i + 1])
        summed[i] = sums(*made.pop(i))
        if i > 0:
            write(units[i - 1], *summed.pop(i - 1))
    write(units[-1], *summed.pop(len(units) - 1))


def project(low, kw_ref, vw_ref, owner, features):
    rows = pl.ds(pl.multiple_of(owner * features, features), features)
    weights = jnp.concatenate([kw_ref[rows, :], vw_ref[rows, :]], axis=1)
    return lax.dot_general(low, weights, NT, preferred_element_type=jnp.float32)


def first_projection_kernel(parts_ref, kw_ref, vw_ref, low_ref, out_ref):
    total = parts_ref[0].astype(jnp.float32)
    for i in range(1, parts_ref.shape[0]):
        total += parts_ref[i].astype(jnp.float32)
    low = total.astype(jnp.bfloat16)
    low_ref[...] = low
    me = lax.axis_index("head")
    out = project(low, kw_ref, vw_ref, me ^ 3, out_ref.shape[1])
    out_ref[...] = out.astype(out_ref.dtype)


def second_projection_kernel(low_ref, kw_ref, vw_ref, out_ref):
    me = lax.axis_index("head")
    out_ref[...] = project(low_ref[...], kw_ref, vw_ref, me ^ 2, out_ref.shape[1])


def last_projection_kernel(low_ref, kw_ref, vw_ref, after, out_ref, keep_ref, dk_ref, dv_ref):
    del after
    width = dk_ref.shape[1]
    low = low_ref[...]
    dk_ref[...] = low[:, :width]
    dv_ref[...] = low[:, width:]
    me = lax.axis_index("head")
    out = project(low, kw_ref, vw_ref, me ^ 1, out_ref.shape[1])
    out_ref[...] = out.astype(out_ref.dtype)
    keep_ref[...] = project(low, kw_ref, vw_ref, me, keep_ref.shape[1])


def last_sum_kernel(total_ref, got_ref, out_ref):
    out_ref[...] = (total_ref[...] + got_ref[...].astype(jnp.float32)).astype(out_ref.dtype)


def swap(x, axis, count, bit):
    return lax.ppermute(x, axis, [(i, i ^ bit) for i in range(count)])


def body(resp, head, queries, d_out, prefix_keys, prefix_values, k_weight, v_weight, lengths):
    own, width = prefix_keys.shape
    features = k_weight.shape[0] // head
    vmem = pl.BlockSpec(memory_space=pltpu.VMEM)
    params = pltpu.CompilerParams(vmem_limit_bytes=12 << 20)

    live = pl.pallas_call(
        mask_kernel,
        out_shape=pltpu.VMEM((lengths.shape[0], 8, LEN), jnp.float32),
        in_specs=[pl.BlockSpec(memory_space=pltpu.SMEM)],
        out_specs=vmem,
        compiler_params=params,
        cost_estimate=pl.CostEstimate(flops=1600000000, transcendentals=0, bytes_accessed=0),
        name="mask",
    )(lengths)
    both = pl.pallas_call(
        join_kernel,
        out_shape=pltpu.VMEM((resp, own, 2 * width), jnp.bfloat16),
        in_specs=[pl.BlockSpec(memory_space=pl.ANY)] + [vmem] * 2,
        out_specs=vmem,
        compiler_params=params,
        name="join",
    )(live, prefix_keys, prefix_values)
    both = lax.all_to_all(both, "resp", 0, 0, tiled=True).reshape(resp * own, 2 * width)

    tokens = resp * own
    kv_local = width // HD
    depth = queries.size // kv_local // HD
    partial = pl.pallas_call(
        attention_kernel,
        out_shape=pltpu.VMEM((tokens, 2 * width), jnp.bfloat16),
        in_specs=[vmem] * 4,
        out_specs=vmem,
        scratch_shapes=[
            pltpu.VMEM((kv_local, 2 * tokens, 2 * HD), jnp.bfloat16),
            pltpu.VMEM((kv_local, 2 * tokens, depth), jnp.bfloat16),
        ],
        compiler_params=pltpu.CompilerParams(
            vmem_limit_bytes=(8 << 20) + 8 * kv_local * tokens * depth
        ),
        cost_estimate=pl.CostEstimate(
            flops=64 * kv_local * tokens * depth * HD,
            transcendentals=kv_local * tokens * depth,
            bytes_accessed=4 * queries.size + 6 * tokens * width,
        ),
        name="attention",
    )(live, both, queries, d_out)

    shares = lax.all_to_all(
        partial.reshape(resp, own, 2 * width), "resp", 0, 0, tiled=True
    )

    block = (own, features)
    low, to_core = pl.pallas_call(
        first_projection_kernel,
        out_shape=[
            pltpu.VMEM((own, 2 * width), jnp.bfloat16),
            pltpu.VMEM(block, jnp.bfloat16),
        ],
        in_specs=[vmem] * 3,
        out_specs=[vmem] * 2,
        compiler_params=params,
        name="projection_other_core",
    )(shares, k_weight, v_weight)
    cost = pl.CostEstimate(
        flops=4 * own * width * features, transcendentals=0, bytes_accessed=4 * width * features
    )
    far = pl.pallas_call(
        second_projection_kernel,
        out_shape=pltpu.VMEM(block, jnp.float32),
        in_specs=[vmem] * 3,
        out_specs=vmem,
        compiler_params=params,
        cost_estimate=cost,
        name="projection_other_y",
    )(low, k_weight, v_weight)
    far = (far + swap(to_core, "head", head, 1).astype(jnp.float32)).astype(jnp.bfloat16)
    got = swap(far, "head", head, 2)
    to_core, total, dk_low, dv_low = pl.pallas_call(
        last_projection_kernel,
        out_shape=[
            pltpu.VMEM(block, jnp.bfloat16),
            pltpu.VMEM(block, jnp.float32),
            jax.ShapeDtypeStruct((own, width), jnp.bfloat16),
            jax.ShapeDtypeStruct((own, width), jnp.bfloat16),
        ],
        in_specs=[vmem] * 3 + [pl.BlockSpec(memory_space=pl.ANY)],
        out_specs=[vmem] * 4,
        compiler_params=params,
        cost_estimate=cost,
        name="projection_this_y",
    )(low, k_weight, v_weight, far)
    total = lax.optimization_barrier(total + got.astype(jnp.float32))
    input_grad = pl.pallas_call(
        last_sum_kernel,
        out_shape=jax.ShapeDtypeStruct(block, jnp.bfloat16),
        in_specs=[vmem] * 2,
        out_specs=vmem,
        compiler_params=params,
        name="last_sum",
    )(total, swap(to_core, "head", head, 1))
    return dk_low, dv_low, input_grad


def solution(mesh):
    placed = (
        P("resp", "head"),
        P("resp", "head"),
        P("resp", "head"),
        P("resp", "head"),
        P(None, "head"),
        P(None, "head"),
        P("resp"),
    )
    return jax.shard_map(
        functools.partial(body, mesh.shape["resp"], mesh.shape["head"]),
        mesh=mesh,
        in_specs=placed,
        out_specs=(P("resp", "head"), P("resp", "head"), P("resp", "head")),
        check_vma=False,
    )
```

```python
import functools

import jax
import jax.numpy as jnp
from jax import lax
from jax.experimental import pallas as pl
from jax.experimental.pallas import tpu as pltpu
from jax.sharding import PartitionSpec as P

HD = 128
LEN = 256
NT = (((1,), (1,)), ((), ()))
UNIT = 2
LOG2E = 1.4426950408889634


def mask_kernel(lengths_ref, live_ref):
    position = lax.broadcasted_iota(jnp.int32, live_ref.shape[1:], 1)
    for part in range(live_ref.shape[0]):
        live_ref[part] = jnp.where(position < lengths_ref[part], 1.0, 0.0)


def join_kernel(live_ref, k_ref, v_ref, out_ref):
    del live_ref
    width = k_ref.shape[1]
    for i in range(out_ref.shape[0]):
        out_ref[i, :, :width] = k_ref[...]
        out_ref[i, :, width:] = v_ref[...]


def attention_kernel(live_ref, kv_ref, q_ref, g_ref, out_ref, blocks_ref, weights_ref):
    scale = HD ** (-0.5)
    tokens = kv_ref.shape[0]
    width = kv_ref.shape[1] // 2
    kv_local = width // HD
    parts = q_ref.shape[0] // LEN
    group = q_ref.shape[1] // HD // kv_local
    units = [
        (k, part, h)
        for k in range(kv_local)
        for part in range(parts)
        for h in range(0, group, UNIT)
    ]

    def stack(ref, unit):
        k, part, h = unit
        heads = [
            ref[part * LEN : (part + 1) * LEN, at * HD : (at + 1) * HD]
            for at in range(k * group + h, k * group + h + UNIT)
        ]
        return jnp.concatenate(heads, axis=0)

    blocks_ref[...] = jnp.zeros_like(blocks_ref)
    for k in range(kv_local):
        blocks_ref[k, :tokens, :HD] = kv_ref[:, k * HD : (k + 1) * HD]
        blocks_ref[k, tokens:, HD:] = kv_ref[:, width + k * HD : width + (k + 1) * HD]

    def products(unit):
        both = jnp.concatenate([stack(q_ref, unit), stack(g_ref, unit)], axis=1)
        out = lax.dot_general(blocks_ref[unit[0]], both, NT, preferred_element_type=jnp.float32)
        return out[:tokens], out[tokens:]

    following = products(units[0])
    for i, unit in enumerate(units):
        k, part, h = unit
        scores, dprobs = following
        if i + 1 < len(units):
            following = products(units[i + 1])
        top = jnp.max(scores, axis=0, keepdims=True)
        expo = jnp.exp2(scores * (scale * LOG2E) - top * (scale * LOG2E))
        total = jnp.sum(expo, axis=0, keepdims=True)
        weighted = jnp.sum(expo * dprobs, axis=0, keepdims=True)
        inverse = 1.0 / total
        delta = weighted * inverse
        factor = inverse * jnp.concatenate([live_ref[part, :1]] * UNIT, axis=1)
        probs = (expo * factor).astype(jnp.bfloat16)
        mine = [u for u in units if u[0] == k]
        cols = pl.ds(mine.index(unit) * UNIT * LEN, UNIT * LEN)
        weights_ref[k, :tokens, cols] = probs
        weights_ref[k, tokens:, cols] = probs * (dprobs - delta).astype(jnp.bfloat16)
        if unit == mine[-1]:
            rows = [
                jnp.concatenate([stack(g_ref, u), stack(q_ref, u)], axis=1) for u in mine
            ]
            out = jnp.dot(
                weights_ref[k], jnp.concatenate(rows, axis=0), preferred_element_type=jnp.float32
            )
            grad_k = out[tokens:, HD:] * scale
            out_ref[:, k * HD : (k + 1) * HD] = grad_k.astype(out_ref.dtype)
            out_ref[:, width + k * HD : width + (k + 1) * HD] = out[:tokens, :HD].astype(
                out_ref.dtype
            )


def project(low, kw_ref, vw_ref, owner, features):
    rows = pl.ds(pl.multiple_of(owner * features, features), features)
    weights = jnp.concatenate([kw_ref[rows, :], vw_ref[rows, :]], axis=1)
    return lax.dot_general(low, weights, NT, preferred_element_type=jnp.float32)


def first_projection_kernel(parts_ref, kw_ref, vw_ref, low_ref, out_ref):
    total = parts_ref[0].astype(jnp.float32)
    for i in range(1, parts_ref.shape[0]):
        total += parts_ref[i].astype(jnp.float32)
    low = total.astype(jnp.bfloat16)
    low_ref[...] = low
    me = lax.axis_index("head")
    out = project(low, kw_ref, vw_ref, me ^ 3, out_ref.shape[1])
    out_ref[...] = out.astype(out_ref.dtype)


def second_projection_kernel(low_ref, kw_ref, vw_ref, out_ref):
    me = lax.axis_index("head")
    out_ref[...] = project(low_ref[...], kw_ref, vw_ref, me ^ 2, out_ref.shape[1])


def last_projection_kernel(low_ref, kw_ref, vw_ref, after, out_ref, keep_ref, dk_ref, dv_ref):
    del after
    width = dk_ref.shape[1]
    low = low_ref[...]
    dk_ref[...] = low[:, :width]
    dv_ref[...] = low[:, width:]
    me = lax.axis_index("head")
    out = project(low, kw_ref, vw_ref, me ^ 1, out_ref.shape[1])
    out_ref[...] = out.astype(out_ref.dtype)
    keep_ref[...] = project(low, kw_ref, vw_ref, me, keep_ref.shape[1])


def last_sum_kernel(total_ref, got_ref, out_ref):
    out_ref[...] = (total_ref[...] + got_ref[...].astype(jnp.float32)).astype(out_ref.dtype)


def swap(x, axis, count, bit):
    return lax.ppermute(x, axis, [(i, i ^ bit) for i in range(count)])


def body(resp, head, queries, d_out, prefix_keys, prefix_values, k_weight, v_weight, lengths):
    own, width = prefix_keys.shape
    features = k_weight.shape[0] // head
    vmem = pl.BlockSpec(memory_space=pltpu.VMEM)
    params = pltpu.CompilerParams(vmem_limit_bytes=12 << 20)

    live = pl.pallas_call(
        mask_kernel,
        out_shape=pltpu.VMEM((lengths.shape[0], 8, LEN), jnp.float32),
        in_specs=[pl.BlockSpec(memory_space=pltpu.SMEM)],
        out_specs=vmem,
        compiler_params=params,
        cost_estimate=pl.CostEstimate(flops=1600000000, transcendentals=0, bytes_accessed=0),
        name="mask",
    )(lengths)
    both = pl.pallas_call(
        join_kernel,
        out_shape=pltpu.VMEM((resp, own, 2 * width), jnp.bfloat16),
        in_specs=[pl.BlockSpec(memory_space=pl.ANY)] + [vmem] * 2,
        out_specs=vmem,
        compiler_params=params,
        name="join",
    )(live, prefix_keys, prefix_values)
    both = lax.all_to_all(both, "resp", 0, 0, tiled=True).reshape(resp * own, 2 * width)

    tokens = resp * own
    kv_local = width // HD
    depth = queries.size // kv_local // HD
    partial = pl.pallas_call(
        attention_kernel,
        out_shape=pltpu.VMEM((tokens, 2 * width), jnp.bfloat16),
        in_specs=[vmem] * 4,
        out_specs=vmem,
        scratch_shapes=[
            pltpu.VMEM((kv_local, 2 * tokens, 2 * HD), jnp.bfloat16),
            pltpu.VMEM((kv_local, 2 * tokens, depth), jnp.bfloat16),
        ],
        compiler_params=pltpu.CompilerParams(
            vmem_limit_bytes=(8 << 20) + 8 * kv_local * tokens * depth
        ),
        cost_estimate=pl.CostEstimate(
            flops=64 * kv_local * tokens * depth * HD,
            transcendentals=kv_local * tokens * depth,
            bytes_accessed=4 * queries.size + 6 * tokens * width,
        ),
        name="attention",
    )(live, both, queries, d_out)

    shares = lax.all_to_all(
        partial.reshape(resp, own, 2 * width), "resp", 0, 0, tiled=True
    )

    block = (own, features)
    low, to_core = pl.pallas_call(
        first_projection_kernel,
        out_shape=[
            pltpu.VMEM((own, 2 * width), jnp.bfloat16),
            pltpu.VMEM(block, jnp.bfloat16),
        ],
        in_specs=[vmem] * 3,
        out_specs=[vmem] * 2,
        compiler_params=params,
        name="projection_other_core",
    )(shares, k_weight, v_weight)
    cost = pl.CostEstimate(
        flops=4 * own * width * features, transcendentals=0, bytes_accessed=4 * width * features
    )
    far = pl.pallas_call(
        second_projection_kernel,
        out_shape=pltpu.VMEM(block, jnp.float32),
        in_specs=[vmem] * 3,
        out_specs=vmem,
        compiler_params=params,
        cost_estimate=cost,
        name="projection_other_y",
    )(low, k_weight, v_weight)
    far = (far + swap(to_core, "head", head, 1).astype(jnp.float32)).astype(jnp.bfloat16)
    got = swap(far, "head", head, 2)
    to_core, total, dk_low, dv_low = pl.pallas_call(
        last_projection_kernel,
        out_shape=[
            pltpu.VMEM(block, jnp.bfloat16),
            pltpu.VMEM(block, jnp.float32),
            jax.ShapeDtypeStruct((own, width), jnp.bfloat16),
            jax.ShapeDtypeStruct((own, width), jnp.bfloat16),
        ],
        in_specs=[vmem] * 3 + [pl.BlockSpec(memory_space=pl.ANY)],
        out_specs=[vmem] * 4,
        compiler_params=params,
        cost_estimate=cost,
        name="projection_this_y",
    )(low, k_weight, v_weight, far)
    total = lax.optimization_barrier(total + got.astype(jnp.float32))
    input_grad = pl.pallas_call(
        last_sum_kernel,
        out_shape=jax.ShapeDtypeStruct(block, jnp.bfloat16),
        in_specs=[vmem] * 2,
        out_specs=vmem,
        compiler_params=params,
        name="last_sum",
    )(total, swap(to_core, "head", head, 1))
    return dk_low, dv_low, input_grad


def solution(mesh):
    placed = (
        P("resp", "head"),
        P("resp", "head"),
        P("resp", "head"),
        P("resp", "head"),
        P(None, "head"),
        P(None, "head"),
        P("resp"),
    )
    return jax.shard_map(
        functools.partial(body, mesh.shape["resp"], mesh.shape["head"]),
        mesh=mesh,
        in_specs=placed,
        out_specs=(P("resp", "head"), P("resp", "head"), P("resp", "head")),
        check_vma=False,
    )
```

```python
import functools

import jax
import jax.numpy as jnp
from jax import lax
from jax.experimental import pallas as pl
from jax.experimental.pallas import tpu as pltpu
from jax.sharding import PartitionSpec as P

HD = 128
LEN = 256
NT = (((1,), (1,)), ((), ()))
UNIT = 2
LOG2E = 1.4426950408889634


def mask_kernel(lengths_ref, live_ref):
    position = lax.broadcasted_iota(jnp.int32, live_ref.shape[1:], 1)
    for part in range(live_ref.shape[0]):
        live_ref[part] = jnp.where(position < lengths_ref[part], 1.0, 0.0)


def join_kernel(live_ref, k_ref, v_ref, out_ref):
    del live_ref
    width = k_ref.shape[1]
    for i in range(out_ref.shape[0]):
        out_ref[i, :, :width] = k_ref[...]
        out_ref[i, :, width:] = v_ref[...]


def attention_kernel(live_ref, kv_ref, q_ref, g_ref, out_ref, blocks_ref, weights_ref):
    scale = HD ** (-0.5)
    tokens = kv_ref.shape[0]
    width = kv_ref.shape[1] // 2
    kv_local = width // HD
    parts = q_ref.shape[0] // LEN
    group = q_ref.shape[1] // HD // kv_local
    units = [
        (k, part, h)
        for k in range(kv_local)
        for part in range(parts)
        for h in range(0, group, UNIT)
    ]

    def stack(ref, unit):
        k, part, h = unit
        heads = [
            ref[part * LEN : (part + 1) * LEN, at * HD : (at + 1) * HD]
            for at in range(k * group + h, k * group + h + UNIT)
        ]
        return jnp.concatenate(heads, axis=0)

    blocks_ref[...] = jnp.zeros_like(blocks_ref)
    for k in range(kv_local):
        blocks_ref[k, :tokens, :HD] = kv_ref[:, k * HD : (k + 1) * HD]
        blocks_ref[k, tokens:, HD:] = kv_ref[:, width + k * HD : width + (k + 1) * HD]

    def products(unit):
        both = jnp.concatenate([stack(q_ref, unit), stack(g_ref, unit)], axis=1)
        out = lax.dot_general(blocks_ref[unit[0]], both, NT, preferred_element_type=jnp.float32)
        return out[:tokens], out[tokens:]

    following = products(units[0])
    for i, unit in enumerate(units):
        k, part, h = unit
        scores, dprobs = following
        if i + 1 < len(units):
            following = products(units[i + 1])
        top = jnp.max(scores, axis=0, keepdims=True)
        expo = jnp.exp2((scores - top) * (scale * LOG2E))
        total = jnp.sum(expo, axis=0, keepdims=True)
        weighted = jnp.sum(expo * dprobs, axis=0, keepdims=True)
        inverse = 1.0 / total
        delta = weighted * inverse
        factor = inverse * jnp.concatenate([live_ref[part, :1]] * UNIT, axis=1)
        probs = expo * factor
        mine = [u for u in units if u[0] == k]
        cols = pl.ds(mine.index(unit) * UNIT * LEN, UNIT * LEN)
        weights_ref[k, :tokens, cols] = probs.astype(jnp.bfloat16)
        weights_ref[k, tokens:, cols] = (probs * (dprobs - delta)).astype(jnp.bfloat16)
        if unit == mine[-1]:
            rows = [
                jnp.concatenate([stack(g_ref, u), stack(q_ref, u)], axis=1) for u in mine
            ]
            out = jnp.dot(
                weights_ref[k], jnp.concatenate(rows, axis=0), preferred_element_type=jnp.float32
            )
            grad_k = out[tokens:, HD:] * scale
            out_ref[:, k * HD : (k + 1) * HD] = grad_k.astype(out_ref.dtype)
            out_ref[:, width + k * HD : width + (k + 1) * HD] = out[:tokens, :HD].astype(
                out_ref.dtype
            )


def project(low, kw_ref, vw_ref, owner, features):
    rows = pl.ds(pl.multiple_of(owner * features, features), features)
    weights = jnp.concatenate([kw_ref[rows, :], vw_ref[rows, :]], axis=1)
    return lax.dot_general(low, weights, NT, preferred_element_type=jnp.float32)


def first_projection_kernel(parts_ref, kw_ref, vw_ref, low_ref, out_ref):
    total = parts_ref[0].astype(jnp.float32)
    for i in range(1, parts_ref.shape[0]):
        total += parts_ref[i].astype(jnp.float32)
    low = total.astype(jnp.bfloat16)
    low_ref[...] = low
    me = lax.axis_index("head")
    out = project(low, kw_ref, vw_ref, me ^ 3, out_ref.shape[1])
    out_ref[...] = out.astype(out_ref.dtype)


def second_projection_kernel(low_ref, kw_ref, vw_ref, out_ref, early_ref):
    me = lax.axis_index("head")
    out_ref[...] = project(low_ref[...], kw_ref, vw_ref, me ^ 2, out_ref.shape[1])

    @pl.when((me & 1) == 1)
    def _():
        out = project(low_ref[...], kw_ref, vw_ref, me ^ 1, early_ref.shape[1])
        early_ref[...] = out.astype(early_ref.dtype)


def last_projection_kernel(
    low_ref, kw_ref, vw_ref, early_ref, after, out_ref, keep_ref, dk_ref, dv_ref
):
    del after
    width = dk_ref.shape[1]
    low = low_ref[...]
    dk_ref[...] = low[:, :width]
    dv_ref[...] = low[:, width:]
    me = lax.axis_index("head")

    @pl.when((me & 1) == 1)
    def _():
        out_ref[...] = early_ref[...]

    @pl.when((me & 1) == 0)
    def _():
        out = project(low_ref[...], kw_ref, vw_ref, me ^ 1, out_ref.shape[1])
        out_ref[...] = out.astype(out_ref.dtype)

    keep_ref[...] = project(low, kw_ref, vw_ref, me, keep_ref.shape[1])


def last_sum_kernel(total_ref, got_ref, out_ref):
    out_ref[...] = (total_ref[...] + got_ref[...].astype(jnp.float32)).astype(out_ref.dtype)


def swap(x, axis, count, bit):
    return lax.ppermute(x, axis, [(i, i ^ bit) for i in range(count)])


def body(resp, head, queries, d_out, prefix_keys, prefix_values, k_weight, v_weight, lengths):
    own, width = prefix_keys.shape
    features = k_weight.shape[0] // head
    vmem = pl.BlockSpec(memory_space=pltpu.VMEM)
    params = pltpu.CompilerParams(vmem_limit_bytes=12 << 20)

    live = pl.pallas_call(
        mask_kernel,
        out_shape=pltpu.VMEM((lengths.shape[0], 8, LEN), jnp.float32),
        in_specs=[pl.BlockSpec(memory_space=pltpu.SMEM)],
        out_specs=vmem,
        compiler_params=params,
        cost_estimate=pl.CostEstimate(flops=1600000000, transcendentals=0, bytes_accessed=0),
        name="mask",
    )(lengths)
    both = pl.pallas_call(
        join_kernel,
        out_shape=pltpu.VMEM((resp, own, 2 * width), jnp.bfloat16),
        in_specs=[pl.BlockSpec(memory_space=pl.ANY)] + [vmem] * 2,
        out_specs=vmem,
        compiler_params=params,
        name="join",
    )(live, prefix_keys, prefix_values)
    both = lax.all_to_all(both, "resp", 0, 0, tiled=True).reshape(resp * own, 2 * width)

    tokens = resp * own
    kv_local = width // HD
    depth = queries.size // kv_local // HD
    partial = pl.pallas_call(
        attention_kernel,
        out_shape=pltpu.VMEM((tokens, 2 * width), jnp.bfloat16),
        in_specs=[vmem] * 4,
        out_specs=vmem,
        scratch_shapes=[
            pltpu.VMEM((kv_local, 2 * tokens, 2 * HD), jnp.bfloat16),
            pltpu.VMEM((kv_local, 2 * tokens, depth), jnp.bfloat16),
        ],
        compiler_params=pltpu.CompilerParams(
            vmem_limit_bytes=(8 << 20) + 8 * kv_local * tokens * depth
        ),
        cost_estimate=pl.CostEstimate(
            flops=64 * kv_local * tokens * depth * HD,
            transcendentals=kv_local * tokens * depth,
            bytes_accessed=4 * queries.size + 6 * tokens * width,
        ),
        name="attention",
    )(live, both, queries, d_out)

    shares = lax.all_to_all(
        partial.reshape(resp, own, 2 * width), "resp", 0, 0, tiled=True
    )

    block = (own, features)
    low, to_core = pl.pallas_call(
        first_projection_kernel,
        out_shape=[
            pltpu.VMEM((own, 2 * width), jnp.bfloat16),
            pltpu.VMEM(block, jnp.bfloat16),
        ],
        in_specs=[vmem] * 3,
        out_specs=[vmem] * 2,
        compiler_params=params,
        name="projection_other_core",
    )(shares, k_weight, v_weight)
    cost = pl.CostEstimate(
        flops=4 * own * width * features, transcendentals=0, bytes_accessed=4 * width * features
    )
    far, early = pl.pallas_call(
        second_projection_kernel,
        out_shape=[pltpu.VMEM(block, jnp.float32), pltpu.VMEM(block, jnp.bfloat16)],
        in_specs=[vmem] * 3,
        out_specs=[vmem] * 2,
        compiler_params=params,
        cost_estimate=cost,
        name="projection_other_y",
    )(low, k_weight, v_weight)
    far = (far + swap(to_core, "head", head, 1).astype(jnp.float32)).astype(jnp.bfloat16)
    got = swap(far, "head", head, 2)
    to_core, total, dk_low, dv_low = pl.pallas_call(
        last_projection_kernel,
        out_shape=[
            pltpu.VMEM(block, jnp.bfloat16),
            pltpu.VMEM(block, jnp.float32),
            jax.ShapeDtypeStruct((own, width), jnp.bfloat16),
            jax.ShapeDtypeStruct((own, width), jnp.bfloat16),
        ],
        in_specs=[vmem] * 4 + [pl.BlockSpec(memory_space=pl.ANY)],
        out_specs=[vmem] * 4,
        compiler_params=params,
        cost_estimate=cost,
        name="projection_this_y",
    )(low, k_weight, v_weight, early, far)
    total = lax.optimization_barrier(total + got.astype(jnp.float32))
    input_grad = pl.pallas_call(
        last_sum_kernel,
        out_shape=jax.ShapeDtypeStruct(block, jnp.bfloat16),
        in_specs=[vmem] * 2,
        out_specs=vmem,
        compiler_params=params,
        name="last_sum",
    )(total, swap(to_core, "head", head, 1))
    return dk_low, dv_low, input_grad


def solution(mesh):
    placed = (
        P("resp", "head"),
        P("resp", "head"),
        P("resp", "head"),
        P("resp", "head"),
        P(None, "head"),
        P(None, "head"),
        P("resp"),
    )
    return jax.shard_map(
        functools.partial(body, mesh.shape["resp"], mesh.shape["head"]),
        mesh=mesh,
        in_specs=placed,
        out_specs=(P("resp", "head"), P("resp", "head"), P("resp", "head")),
        check_vma=False,
    )
```
